256 devices in a mesh: face: 8 (over y_hi, x), tile: 32 (over y_lo, z, core).
Axes of the slice: x: 4, y: 4 (y_hi: 2, y_lo: 2; y = y_hi * 2 + y_lo), z: 8, core: 2. Of those that a mesh axis runs over, the one named last changes fastest.
Arguments:
- inputs: bfloat16 [8, 256, 256, 128], P('face', 'tile'), may hold values from -6 to 6
- kernel: float32 [7, 7, 128], replicated, may hold values from -0.875 to 0.875
- conv_bias: float32 [128], replicated, may hold values from -3 to 3
- norm_gain: float32 [128], replicated, may hold values from 0.5 to 1.5
- norm_bias: float32 [128], replicated, may hold values from -3 to 3
- expand_weight: bfloat16 [128, 512], replicated, may hold values from -0.5 to 0.5
- expand_bias: float32 [512], replicated, may hold values from -3 to 3
- reduce_weight: bfloat16 [512, 128], replicated, may hold values from -0.25 to 0.25
- reduce_bias: float32 [128], replicated, may hold values from -3 to 3
- layer_scale: float32 [128], replicated, may hold values from 0.5 to 1.5
- neighbours: int32 [8, 4, 3], replicated, may hold values from 0 to 7, as said below
- cotangent: bfloat16 [8, 256, 256, 128], P('face', 'tile'), may hold values from -6 to 6
Outputs:
- output: bfloat16 [8, 256, 256, 128], P('face', 'tile')
- kernel_grad: float32 [7, 7, 128], replicated
- conv_bias_grad: float32 [128], replicated
- gain_grad: float32 [128], replicated
- norm_bias_grad: float32 [128], replicated
- expand_grad: float32 [128, 512], replicated
- expand_bias_grad: float32 [512], replicated
- reduce_grad: float32 [512, 128], replicated
- reduce_bias_grad: float32 [128], replicated
- scale_grad: float32 [128], replicated
The draws below stay inside these ranges and needn't reach their ends.
Inputs may be any that keep to these rules, and one draw needn't show every extreme that they name: neighbours[f, s] = (partner face, partner side, reversal flag 0 or 1); the partner face is never f itself; sides numbered 0 north, 1 east, 2 south, 3 west; side 0 is always glued to side 2 and side 1 to side 3; the gluing is reciprocal: if side s of f takes side s2 of g, then side s2 of g takes side s of f with the same flag.
All inputs are finite; a program needn't handle non-finite values.
Results may differ from the reference program's by a relative error of at most 0.0075.
Values may be sent and summed in bfloat16 or wider, within the bound.
A program may use at most 64 MiB of HBM per device.

```python
import math
import jax
import jax.numpy as jnp
from jax import lax

C = 128
HID = 512
KS = 7
NSIDE = 256
FACES = 8


def glue_cycle(table, order, side_a, side_b, flips):
    count = order.shape[0]
    after = jnp.roll(order, -1)
    ones = jnp.ones((count,), jnp.int32)
    table = table.at[order, side_a].set(jnp.stack([after, side_b * ones, flips], -1))
    table = table.at[after, side_b].set(jnp.stack([order, side_a * ones, flips], -1))
    return table


def draw_neighbours(key, part):
    key = jax.random.fold_in(key, 7)
    keys = jax.random.split(key, 5)
    first_order = jax.random.permutation(keys[0], FACES).astype(jnp.int32)
    second_order = jax.random.permutation(keys[1], FACES).astype(jnp.int32)
    pairings = jnp.array([[0, 2, 1, 3], [2, 0, 3, 1], [0, 2, 3, 1], [2, 0, 1, 3]], jnp.int32)
    pairing = pairings[jax.random.randint(keys[2], (), 0, 4, dtype=jnp.int32)]
    first_flips = jax.random.randint(keys[3], (FACES,), 0, 2, dtype=jnp.int32)
    second_flips = jax.random.randint(keys[4], (FACES,), 0, 2, dtype=jnp.int32).at[0].set(1)
    table = jnp.zeros((FACES, 4, 3), jnp.int32)
    table = glue_cycle(table, first_order, pairing[0], pairing[1], first_flips)
    table = glue_cycle(table, second_order, pairing[2], pairing[3], second_flips)
    return table.astype(jnp.int32)


def block_scale(own_key, shape, cuts, low, largest):
    gain = 1.0
    for position, parts in cuts:
        draws = jax.random.uniform(jax.random.fold_in(jax.random.fold_in(own_key, 6), position), (parts,), jnp.float32, low / len(cuts), largest / len(cuts))
        gain = gain * jnp.repeat(jnp.exp(draws), shape[position] // parts).reshape((-1,) + (1,) * (len(shape) - 1 - position))
    return gain


def gaussian(key, dims, scale, limit, cuts=(), kind=jnp.bfloat16):
    loudness = block_scale(key, dims, cuts, -0.22, 0.18) if cuts else 1.0
    values = jax.random.normal(key, dims, jnp.float32) * scale * loudness
    return jnp.minimum(jnp.maximum(values, -limit), limit).astype(kind)


def setup_inputs(seed: int = 0) -> dict:
    key_list = jax.random.split(jax.random.key(seed), 13)
    inputs = gaussian(key_list[0], (FACES, NSIDE, NSIDE, C), 1.0, 6.0, ((0, 8), (1, 32)))
    kernel = gaussian(key_list[1], (KS, KS, C), (KS * KS) ** -0.5, 0.875, (), jnp.float32)
    conv_bias = gaussian(key_list[2], (C,), 0.5, 3.0, (), jnp.float32)
    norm_gain = jnp.clip(jax.random.uniform(key_list[3], (C,), jnp.float32, 0.5, 1.5), 0.5, 1.5)
    norm_bias = gaussian(key_list[4], (C,), 0.5, 3.0, (), jnp.float32)
    expand_weight = gaussian(key_list[5], (C, HID), C ** -0.5, 0.5)
    expand_bias = gaussian(key_list[6], (HID,), 0.5, 3.0, (), jnp.float32)
    reduce_weight = gaussian(key_list[7], (HID, C), HID ** -0.5, 0.25)
    reduce_bias = gaussian(key_list[8], (C,), 0.5, 3.0, (), jnp.float32)
    layer_scale = jnp.clip(jax.random.uniform(key_list[9], (C,), jnp.float32, 0.5, 1.5), 0.5, 1.5)
    neighbours = draw_neighbours(jax.random.fold_in(key_list[12], 71), 0)
    cotangent = gaussian(key_list[11], (FACES, NSIDE, NSIDE, C), 1.0, 6.0, ((0, 8), (1, 32)))
    return {"inputs": inputs, "kernel": kernel, "conv_bias": conv_bias, "norm_gain": norm_gain, "norm_bias": norm_bias, "expand_weight": expand_weight, "expand_bias": expand_bias, "reduce_weight": reduce_weight, "reduce_bias": reduce_bias, "layer_scale": layer_scale, "neighbours": neighbours, "cotangent": cotangent}


EPS = 1e-06

def side_bands(face):
    north = face[0:3]
    east = jnp.swapaxes(face[:, ::-1][:, 0:3], 0, 1)
    south = face[::-1][0:3]
    west = jnp.swapaxes(face[:, 0:3], 0, 1)
    return jnp.stack([north, east, south, west])

def orient_halos(bands_all, neighbours):

    def single(entry):
        band = bands_all[entry[0], entry[1]]
        return jnp.where(entry[2] == 1, band[:, ::-1], band)
    return jax.vmap(jax.vmap(single))(neighbours)

def pad_face(face, halos):
    north, east, south, west = (halos[0], halos[1], halos[2], halos[3])
    middle = jnp.concatenate([north[::-1], face, south], 0)
    corner = jnp.zeros((3, 3, face.shape[2]), face.dtype)
    west_cols = jnp.concatenate([corner, jnp.swapaxes(west[::-1], 0, 1), corner], 0)
    east_cols = jnp.concatenate([corner, jnp.swapaxes(east, 0, 1), corner], 0)
    return jnp.concatenate([west_cols, middle, east_cols], 1)

def contract_rows(left, right):
    return lax.dot_general(left, right, (((0,), (0,)), ((), ())), preferred_element_type=jnp.float32)

def contract_cols(left, right):
    return lax.dot_general(left, right, (((1,), (1,)), ((), ())), preferred_element_type=jnp.float32)

def block_pass(padded, residual, cotangent, kernel, conv_bias, norm_gain, norm_bias, expand_weight, expand_bias, reduce_weight, reduce_bias, layer_scale):
    rows, width, chans = residual.shape
    side = kernel.shape[0]
    conv = jnp.zeros((rows, width, chans), jnp.float32) + conv_bias
    for first in range(side):
        for second in range(side):
            conv = conv + kernel[first, second] * padded[first:first + rows, second:second + width].astype(jnp.float32)
    flat = conv.reshape(-1, chans)
    mean = lax.optimization_barrier(jnp.mean(flat, -1, keepdims=True))
    centred = flat - mean
    variance = lax.optimization_barrier(jnp.mean(centred * centred, -1, keepdims=True))
    inverse = lax.rsqrt(variance + EPS)
    normed = centred * inverse
    scaled = (normed * norm_gain + norm_bias).astype(jnp.bfloat16)
    hidden = jnp.dot(scaled, expand_weight, preferred_element_type=jnp.float32) + expand_bias
    active, gelu_back = jax.vjp(jax.nn.gelu, hidden)
    active_low = active.astype(jnp.bfloat16)
    branch = jnp.dot(active_low, reduce_weight, preferred_element_type=jnp.float32) + reduce_bias
    output = (residual.reshape(-1, chans).astype(jnp.float32) + layer_scale * branch).astype(jnp.bfloat16)
    cot = cotangent.reshape(-1, chans).astype(jnp.float32)
    scale_grad = lax.optimization_barrier(jnp.sum(cot * branch, 0))
    branch_cot = (cot * layer_scale).astype(jnp.bfloat16)
    reduce_grad = contract_rows(active_low, branch_cot)
    reduce_bias_grad = lax.optimization_barrier(jnp.sum(branch_cot.astype(jnp.float32), 0))
    active_cot = contract_cols(branch_cot, reduce_weight)
    hidden_cot = gelu_back(active_cot)[0].astype(jnp.bfloat16)
    expand_grad = contract_rows(scaled, hidden_cot)
    expand_bias_grad = lax.optimization_barrier(jnp.sum(hidden_cot.astype(jnp.float32), 0))
    scaled_cot = contract_cols(hidden_cot, expand_weight)
    gain_grad = lax.optimization_barrier(jnp.sum(scaled_cot * normed, 0))
    norm_bias_grad = lax.optimization_barrier(jnp.sum(scaled_cot, 0))
    normed_cot = scaled_cot * norm_gain
    conv_cot = inverse * (normed_cot - lax.optimization_barrier(jnp.mean(normed_cot, -1, keepdims=True)) - normed * lax.optimization_barrier(jnp.mean(normed_cot * normed, -1, keepdims=True)))
    conv_bias_grad = lax.optimization_barrier(jnp.sum(conv_cot, 0))
    conv_cot = conv_cot.reshape(rows, width, chans)
    kernel_grad = jnp.stack([jnp.stack([lax.optimization_barrier(jnp.sum(padded[first:first + rows, second:second + width].astype(jnp.float32) * conv_cot, (0, 1))) for second in range(side)]) for first in range(side)])
    grads = (kernel_grad, conv_bias_grad, gain_grad, norm_bias_grad, expand_grad, expand_bias_grad, reduce_grad, reduce_bias_grad, scale_grad)
    return (output.reshape(rows, width, chans), grads)

def reference(inputs, kernel, conv_bias, norm_gain, norm_bias, expand_weight, expand_bias, reduce_weight, reduce_bias, layer_scale, neighbours, cotangent):
    bands_all = jax.vmap(side_bands)(inputs)
    halos = orient_halos(bands_all, neighbours)

    def per_face(item):
        face, halo, cot = item
        padded = pad_face(face, halo)
        return block_pass(padded, face, cot, kernel, conv_bias, norm_gain, norm_bias, expand_weight, expand_bias, reduce_weight, reduce_bias, layer_scale)
    output, grads = lax.map(per_face, (inputs, halos, cotangent))
    factor = 1.0 / math.sqrt(inputs.shape[0] * inputs.shape[1] * inputs.shape[2])
    summed = [lax.optimization_barrier(jnp.sum(item, 0)) * factor for item in grads]
    return (output, summed[0], summed[1], summed[2], summed[3], summed[4], summed[5], summed[6], summed[7], summed[8])
```

```python
import functools
import math

import jax
import jax.numpy as jnp
from jax import lax
from jax.experimental import pallas as pl
from jax.experimental.pallas import tpu as pltpu
from jax.sharding import PartitionSpec as P

EPS = 1e-06
MESH = pl.DeviceIdType.MESH
BF = jnp.bfloat16
F32 = jnp.float32
ROOT = math.sqrt(2.0 / math.pi)
CUBE = 0.044715
FACES = 8
TILES = 32
VMEM = pl.BlockSpec(memory_space=pltpu.VMEM)
SMEM = pl.BlockSpec(memory_space=pltpu.SMEM)
ANY = pl.BlockSpec(memory_space=pl.ANY)


def place():
    return lax.axis_index("face"), lax.axis_index("tile")


def remote(src, dst, send, recv, face, tile):
    return pltpu.make_async_remote_copy(
        src_ref=src, dst_ref=dst, send_sem=send, recv_sem=recv,
        device_id=(face, tile), device_id_type=MESH,
    )


def halo_kernel(
    nbr, x, top, bot, hbuf, side,
    pieces, chosen, nsbuf, nsend,
    row_send, row_recv, piece_send, piece_recv, band_send, band_recv,
    side_send, side_recv, fwd_send, fwd_recv, local_sem,
):
    f, t = place()
    last = TILES - 1
    mirror = last - t
    is_first = t == 0
    is_last = t == last

    barrier = pltpu.get_barrier_semaphore()

    def hello(face, tile):
        pl.semaphore_signal(barrier, inc=1, device_id=(face, tile), device_id_type=MESH)

    others = [lax.rem(f + k, FACES) for k in range(1, FACES)]
    for g in others:
        hello(g, t)
    hello(f, mirror)
    has_up = t > 0
    has_down = t < last
    mir_up = jnp.logical_and(mirror < last, mirror + 1 != t)
    mir_down = jnp.logical_and(mirror > 0, mirror - 1 != t)

    @pl.when(has_up)
    def _():
        hello(f, t - 1)

    @pl.when(has_down)
    def _():
        hello(f, t + 1)

    @pl.when(mir_up)
    def _():
        hello(f, mirror + 1)

    @pl.when(mir_down)
    def _():
        hello(f, mirror - 1)

    edge = jnp.logical_or(is_first, is_last)

    @pl.when(edge)
    def _():
        for g in range(FACES):
            hello(g, mirror)

    for d in range(3):
        west = x[:, d : d + 1, :].astype(F32).reshape(8, 128)
        east = x[:, 255 - d : 256 - d, :].astype(F32).reshape(8, 128)
        pieces[f, d] = jnp.concatenate([west, east], 0).astype(BF)

    one = lambda cond: cond.astype(jnp.int32)
    count = 8 + one(has_up) + one(has_down) + one(mir_up) + one(mir_down) + 8 * one(edge)
    pl.semaphore_wait(barrier, count)

    def band_copy(rows, k, g):
        return remote(
            x.at[pl.ds(rows, 3), pl.ds(g * 32, 32), :], nsbuf.at[f],
            band_send.at[k], band_recv.at[f], g, t,
        )

    def piece_copy(k, g):
        return remote(pieces.at[f], pieces.at[f], piece_send.at[k], piece_recv.at[f], g, t)

    def up_copy():
        return remote(x.at[pl.ds(0, 3)], bot, row_send.at[0], row_recv.at[0], f, t - 1)

    def down_copy():
        return remote(x.at[pl.ds(5, 3)], top, row_send.at[1], row_recv.at[1], f, t + 1)

    for rows, cond in ((0, is_first), (5, is_last)):

        @pl.when(cond)
        def _(rows=rows):
            for k, g in enumerate(others):
                band_copy(rows, k, g).start()
            nsbuf[f] = x[rows : rows + 3, pl.ds(pl.multiple_of(f * 32, 32), 32), :]

    for k, g in enumerate(others):
        piece_copy(k, g).start()

    @pl.when(has_up)
    def _():
        up_copy().start()

    @pl.when(has_down)
    def _():
        down_copy().start()

    def forward(g):
        return remote(nsend.at[g], hbuf.at[f], fwd_send.at[g], fwd_recv.at[f], g, mirror)

    for side_id, rows, cond in ((0, 5, is_last), (2, 0, is_first)):

        @pl.when(cond)
        def _(side_id=side_id, rows=rows):
            for k, g in enumerate(others):
                remote(
                    x.at[pl.ds(rows, 3), pl.ds(g * 32, 32), :], nsbuf.at[g],
                    band_send.at[k], band_recv.at[g], g, t,
                ).wait_recv()
            for g in range(FACES):
                nsend[g] = nsbuf[nbr[g, side_id, 0]]
                forward(g).start()

    for k, g in enumerate(others):
        remote(pieces.at[f], pieces.at[g], piece_send.at[k], piece_recv.at[g], g, t).wait_recv()
    from_west = pieces[nbr[f, 3, 0]]
    from_east = pieces[nbr[f, 1, 0]]
    chosen[...] = jnp.concatenate(
        [from_west.astype(F32)[:, 8:16], from_east.astype(F32)[:, 0:8]], 1
    ).astype(BF)

    def side_copy(slot, tile):
        return remote(chosen, side.at[slot], side_send.at[slot], side_recv.at[slot], f, tile)

    own = pltpu.make_async_copy(chosen, side.at[1], local_sem.at[0])
    own.start()
    side_copy(4, mirror).start()

    @pl.when(has_down)
    def _():
        side_copy(0, t + 1).start()

    @pl.when(has_up)
    def _():
        side_copy(2, t - 1).start()

    @pl.when(mir_up)
    def _():
        side_copy(3, mirror + 1).start()

    @pl.when(mir_down)
    def _():
        side_copy(5, mirror - 1).start()

    @pl.when(mirror + 1 == t)
    def _():
        same = pltpu.make_async_copy(chosen, side.at[3], local_sem.at[1])
        same.start()
        same.wait()

    @pl.when(mirror - 1 == t)
    def _():
        same = pltpu.make_async_copy(chosen, side.at[5], local_sem.at[1])
        same.start()
        same.wait()

    own.wait()

    side_copy(4, mirror).wait_recv()

    @pl.when(has_up)
    def _():
        side_copy(0, t - 1).wait_recv()
        down_copy().wait_recv()

    @pl.when(has_down)
    def _():
        side_copy(2, t + 1).wait_recv()
        up_copy().wait_recv()

    @pl.when(mir_up)
    def _():
        side_copy(3, mirror + 1).wait_recv()

    @pl.when(mir_down)
    def _():
        side_copy(5, mirror - 1).wait_recv()

    @pl.when(edge)
    def _():
        for g in range(FACES):
            remote(
                nsend.at[g], hbuf.at[g], fwd_send.at[g], fwd_recv.at[g], g, mirror
            ).wait_recv()

    for k, g in enumerate(others):
        piece_copy(k, g).wait_send()
    side_copy(4, mirror).wait_send()

    @pl.when(has_up)
    def _():
        side_copy(2, t - 1).wait_send()
        up_copy().wait_send()

    @pl.when(has_down)
    def _():
        side_copy(0, t + 1).wait_send()
        down_copy().wait_send()

    @pl.when(mir_up)
    def _():
        side_copy(3, mirror + 1).wait_send()

    @pl.when(mir_down)
    def _():
        side_copy(5, mirror - 1).wait_send()

    @pl.when(edge)
    def _():
        for k, g in enumerate(others):
            band_copy(0, k, g).wait_send()
        for g in range(FACES):
            forward(g).wait_send()


def exchange_halos(neighbours, x):
    dma = pltpu.SemaphoreType.DMA
    return pl.pallas_call(
        halo_kernel,
        out_shape=(
            jax.ShapeDtypeStruct((3, 256, 128), BF),
            jax.ShapeDtypeStruct((3, 256, 128), BF),
            jax.ShapeDtypeStruct((8, 3, 32, 128), BF),
            jax.ShapeDtypeStruct((6, 3, 16, 128), BF),
        ),
        in_specs=[SMEM, VMEM],
        out_specs=(ANY, ANY, ANY, ANY),
        scratch_shapes=[
            pltpu.VMEM((8, 3, 16, 128), BF),
            pltpu.VMEM((3, 16, 128), BF),
            pltpu.VMEM((8, 3, 32, 128), BF),
            pltpu.VMEM((8, 3, 32, 128), BF),
            dma((2,)), dma((2,)), dma((8,)), dma((8,)), dma((8,)), dma((8,)),
            dma((6,)), dma((6,)), dma((8,)), dma((8,)), dma((2,)),
        ],
        compiler_params=pltpu.CompilerParams(
            collective_id=0, has_side_effects=True, vmem_limit_bytes=16 * 1024 * 1024
        ),
        name="halo",
    )(neighbours, x)


def nt(left, right):
    return lax.dot_general(left, right, (((1,), (1,)), ((), ())), preferred_element_type=F32)


def nn(left, right):
    return lax.dot_general(left, right, (((1,), (0,)), ((), ())), preferred_element_type=F32)


def one_hot(rows, cols, index):
    r = lax.broadcasted_iota(jnp.int32, (rows, cols), 0)
    c = lax.broadcasted_iota(jnp.int32, (rows, cols), 1)
    return jnp.where(c == index(r), 1.0, 0.0).astype(BF)


def fold(v):
    rows, chans = v.shape
    return jnp.sum(v.reshape(rows // 8, 8, chans), 0)


def block_kernel(
    nbr, x, cot, top, bot, hbuf, side, kern, cb, gain, nb, we, be, wr, br, ls,
    out, big, small,
    pad, conv, taps, acc_e, acc_r, sums,
):
    f, t = place()
    pad[3:11, 8:264, :] = x[...].astype(F32)

    @pl.when(t > 0)
    def _():
        pad[0:3, 8:264, :] = top[...].astype(F32)

    @pl.when(t < TILES - 1)
    def _():
        pad[11:14, 8:264, :] = bot[...].astype(F32)

    def polar(flag, rows):
        turn = one_hot(256, 256, lambda r: 255 - r)
        for d in range(3):
            band = jnp.concatenate([hbuf[k, d] for k in range(8)], 0)
            turned = nn(turn, band)
            pad[rows[d], 8:264, :] = jnp.where(flag == 1, turned, band.astype(F32))

    @pl.when(t == 0)
    def _():
        polar(nbr[f, 0, 2], (0, 1, 2))

    @pl.when(t == TILES - 1)
    def _():
        polar(nbr[f, 2, 2], (11, 12, 13))

    keep_up = t > 0
    keep_down = t < TILES - 1
    turn = one_hot(24, 24, lambda r: r // 8 * 8 + 7 - r % 8)
    for d in range(3):
        slots = [side[s, d].astype(F32) for s in range(6)]
        for s in (0, 3):
            slots[s] = jnp.where(keep_up, slots[s], 0.0)
        for s in (2, 5):
            slots[s] = jnp.where(keep_down, slots[s], 0.0)
        for first, side_id, col in ((0, 3, 7 - d), (8, 1, 264 + d)):
            straight = jnp.concatenate([slots[s][first : first + 8] for s in (0, 1, 2)], 0)
            turned = jnp.concatenate([slots[s][first : first + 8] for s in (3, 4, 5)], 0)
            turned = nn(turn, turned.astype(BF))
            halo = jnp.where(nbr[f, side_id, 2] == 1, turned, straight)
            pad[0:14, col : col + 1, :] = halo[5:19].reshape(14, 1, 128)

    for a in range(7):
        for b in range(7):
            taps[a * 7 + b] = jnp.broadcast_to(kern[a, b : b + 1, :], (8, 128))

    bias = jnp.broadcast_to(cb[...].reshape(1, 128), (8, 128))

    @pl.loop(0, 32)
    def _(jb):
        col = pl.multiple_of(jb * 8, 8)
        acc = [bias] * 8
        for b in range(7):
            tap = [taps[a * 7 + b] for a in range(7)]
            for row in range(14):
                v = pad[row, pl.ds(col + 5 + b, 8), :]
                for a in range(7):
                    if 0 <= row - a < 8:
                        acc[row - a] = acc[row - a] + tap[a] * v
        for r in range(8):
            conv[r, pl.ds(col, 8), :] = acc[r]

    acc_e[...] = jnp.zeros_like(acc_e)
    acc_r[...] = jnp.zeros_like(acc_r)
    sums[...] = jnp.zeros_like(sums)
    mean_of = jnp.full((128, 128), 1.0 / 128, BF)
    vec = lambda ref: ref[...].reshape(1, -1)
    ones = jnp.ones((16, 256), BF)

    @pl.loop(0, 8)
    def _(r):
        c = conv[r]
        centred = c - nn(c.astype(BF), mean_of)
        variance = nn((centred * centred).astype(BF), mean_of)
        inverse = lax.rsqrt(variance + EPS)
        normed = centred * inverse
        scaled = (normed * vec(gain) + vec(nb)).astype(BF)
        g = cot[r].astype(F32)
        branch_cot = (g * vec(ls)).astype(BF)
        hidden = nn(scaled, we[...]) + vec(be)
        active_cot = nt(branch_cot, wr[...])
        square = hidden * hidden
        s = 0.5 + 0.5 * jnp.tanh(hidden * (ROOT + (ROOT * CUBE) * square))
        active = hidden * s
        active_low = active.astype(BF)
        slope = s + active * (1.0 - s) * (2.0 * ROOT + (6.0 * ROOT * CUBE) * square)
        hidden_cot = (active_cot * slope).astype(BF)
        branch = nn(active_low, wr[...]) + vec(br)
        out[r] = (x[r].astype(F32) + vec(ls) * branch).astype(BF)
        left = jnp.concatenate([scaled.T, ones], 0)
        acc_e[...] += nn(left, hidden_cot)
        acc_r[...] += nn(branch_cot.T, active_low)
        scaled_cot = nt(hidden_cot, we[...])
        normed_cot = scaled_cot * vec(gain)
        m1 = nn(normed_cot.astype(BF), mean_of)
        m2 = nn((normed_cot * normed).astype(BF), mean_of)
        conv_cot = inverse * (normed_cot - m1 - normed * m2)
        sums[0] += fold(conv_cot)
        sums[1] += fold(scaled_cot * normed)
        sums[2] += fold(scaled_cot)
        sums[3] += fold(branch_cot.astype(F32))
        sums[4] += fold(g * branch)
        conv[r] = conv_cot

    for q in range(4):
        big[q * 128 : q * 128 + 128, :] = acc_e[0:128, q * 128 : q * 128 + 128].astype(BF)
        big[512 + q * 128 : 640 + q * 128, :] = acc_r[:, q * 128 : q * 128 + 128].T.astype(BF)

    small[...] = jnp.zeros_like(small)
    for b in range(7):

        def step(jb, acc):
            col = pl.multiple_of(jb * 8, 8)
            acc = list(acc)
            cots = [conv[r, pl.ds(col, 8), :] for r in range(8)]
            for row in range(14):
                v = pad[row, pl.ds(col + 5 + b, 8), :]
                for a in range(7):
                    if 0 <= row - a < 8:
                        acc[a] = acc[a] + cots[row - a] * v
            return tuple(acc)

        acc = lax.fori_loop(0, 32, step, (jnp.zeros((8, 128), F32),) * 7)
        for a in range(7):
            small[a * 7 + b : a * 7 + b + 1, :] = jnp.sum(acc[a], 0, keepdims=True)
    for i in range(5):
        small[49 + i : 50 + i, :] = jnp.sum(sums[i], 0, keepdims=True)
    for q in range(4):
        small[54 + q : 55 + q, :] = acc_e[128:129, q * 128 : q * 128 + 128]


def run_block(neighbours, x, cot, halos, params):
    return pl.pallas_call(
        block_kernel,
        out_shape=(
            jax.ShapeDtypeStruct((8, 256, 128), BF),
            jax.ShapeDtypeStruct((1024, 128), BF),
            jax.ShapeDtypeStruct((64, 128), F32),
        ),
        in_specs=[SMEM] + [VMEM] * 15,
        out_specs=(VMEM, VMEM, VMEM),
        scratch_shapes=[
            pltpu.VMEM((14, 272, 128), F32),
            pltpu.VMEM((8, 256, 128), F32),
            pltpu.VMEM((49, 8, 128), F32),
            pltpu.VMEM((144, 512), F32),
            pltpu.VMEM((128, 512), F32),
            pltpu.VMEM((5, 8, 128), F32),
        ],
        compiler_params=pltpu.CompilerParams(vmem_limit_bytes=48 * 1024 * 1024),
        name="block",
    )(neighbours, x, cot, *halos, *params)


def sum_kernel(
    factor, big, small, gath, sgath,
    slots1, sslots1, send2, slots2, parts, fin, sfin,
    s1, r1, ss1, sr1, s2, r2, s3, r3, s4, r4, ss4, sr4, local_sem,
):
    f, t = place()
    hi = t // 16
    s = t % 16
    z = s // 2
    a = hi * 8 + f
    plane = [lax.rem(a + k, 16) for k in range(1, 16)]
    line = [lax.rem(s + k, 16) for k in range(1, 16)]
    stack = [lax.rem(z + k, 8) for k in range(1, 8)]
    faces = [lax.rem(f + k, 8) for k in range(1, 8)]

    def plane_id(p):
        return lax.rem(p, 8), p // 8 * 16 + s

    barrier = pltpu.get_barrier_semaphore()
    for p in plane:
        pl.semaphore_signal(barrier, inc=1, device_id=plane_id(p), device_id_type=MESH)
    for p in line:
        pl.semaphore_signal(barrier, inc=1, device_id=(f, hi * 16 + p), device_id_type=MESH)
    pl.semaphore_wait(barrier, 30)

    def big1(k, p, slot):
        return remote(
            big.at[pl.ds(pl.multiple_of(p * 64, 64), 64)], slots1.at[slot], s1.at[k], r1.at[slot],
            *plane_id(p)
        )

    def small1(k, p, slot):
        rows = pl.ds(pl.multiple_of(lax.rem(p, 8) * 8, 8), 8)
        return remote(small.at[rows], sslots1.at[slot], ss1.at[k], sr1.at[slot], *plane_id(p))

    for k, p in enumerate(plane):
        big1(k, p, a).start()
        small1(k, p, a).start()
    slots1[a] = big[pl.ds(pl.multiple_of(a * 64, 64), 64), :]
    sslots1[a] = small[pl.ds(pl.multiple_of(f * 8, 8), 8), :]
    for k, p in enumerate(plane):
        small1(k, p, p).wait_recv()
    few = sslots1[0]
    for p in range(1, 16):
        few = few + sslots1[p]
    for k, p in enumerate(plane):
        big1(k, p, p).wait_recv()
    total = slots1[0].astype(F32)
    for p in range(1, 16):
        total = total + slots1[p].astype(F32)
    for q in range(8):
        send2[q, 0:8] = total[q * 8 : q * 8 + 8]
        send2[q, 8:16] = few

    def second(k, p, slot):
        return remote(
            send2.at[p // 2], slots2.at[slot], s2.at[k], r2.at[slot], f, hi * 16 + p
        )

    for k, p in enumerate(line):
        second(k, p, s).start()
    slots2[s] = send2[z]
    for k, p in enumerate(line):
        second(k, p, p).wait_recv()
    both = slots2[0]
    for p in range(1, 16):
        both = both + slots2[p]
    both = both * factor
    parts[z] = both[0:8]
    sfin[f] = both[8:16]

    def third(k, q, slot):
        return remote(
            parts.at[z], parts.at[slot], s3.at[k], r3.at[slot], f, hi * 16 + q * 2 + s % 2
        )

    for k, q in enumerate(stack):
        third(k, q, z).start()

    def small4(k, g, slot):
        return remote(sfin.at[f], sfin.at[slot], ss4.at[k], sr4.at[slot], g, t)

    for k, g in enumerate(faces):
        small4(k, g, f).start()
    for k, q in enumerate(stack):
        third(k, q, q).wait_recv()
    fin[a] = parts[...].reshape(64, 128).astype(BF)

    def big4(k, p, slot):
        return remote(fin.at[a], fin.at[slot], s4.at[k], r4.at[slot], *plane_id(p))

    for k, p in enumerate(plane):
        big4(k, p, a).start()
    for k, g in enumerate(faces):
        small4(k, g, g).wait_recv()
    sgath[...] = sfin[...]
    for k, p in enumerate(plane):
        big4(k, p, p).wait_recv()
    gath[...] = fin[...]

    for k, p in enumerate(plane):
        big1(k, p, a).wait_send()
        small1(k, p, a).wait_send()
        big4(k, p, a).wait_send()
    for k, p in enumerate(line):
        second(k, p, s).wait_send()
    for k, q in enumerate(stack):
        third(k, q, z).wait_send()
    for k, g in enumerate(faces):
        small4(k, g, f).wait_send()


def sum_all(big, small, factor):
    dma = pltpu.SemaphoreType.DMA
    return pl.pallas_call(
        functools.partial(sum_kernel, factor),
        out_shape=(
            jax.ShapeDtypeStruct((16, 64, 128), BF),
            jax.ShapeDtypeStruct((8, 8, 128), F32),
        ),
        in_specs=[VMEM, VMEM],
        out_specs=(VMEM, VMEM),
        scratch_shapes=[
            pltpu.VMEM((16, 64, 128), BF),
            pltpu.VMEM((16, 8, 128), F32),
            pltpu.VMEM((8, 16, 128), F32),
            pltpu.VMEM((16, 16, 128), F32),
            pltpu.VMEM((8, 8, 128), F32),
            pltpu.VMEM((16, 64, 128), BF),
            pltpu.VMEM((8, 8, 128), F32),
        ]
        + [dma((16,))] * 12
        + [dma((1,))],
        compiler_params=pltpu.CompilerParams(
            collective_id=1, has_side_effects=True, vmem_limit_bytes=16 * 1024 * 1024
        ),
        name="sum",
    )(big, small)


def unpack_kernel(
    gath, sgath, kernel_grad, cb_grad, gain_grad, nb_grad, we_grad, be_grad, wr_grad, br_grad, ls_grad
):
    rows = gath.reshape(1024, 128)
    few = sgath[...].reshape(64, 128)
    for q in range(4):
        we_grad[:, q * 128 : q * 128 + 128] = rows[q * 128 : q * 128 + 128, :].astype(F32)
        be_grad[q * 128 : q * 128 + 128] = few[54 + q]
    wr_grad[...] = rows[512:1024, :].astype(F32)
    for a in range(7):
        kernel_grad[a] = few[a * 7 : a * 7 + 7]
    for i, ref in enumerate((cb_grad, gain_grad, nb_grad, br_grad, ls_grad)):
        ref[...] = few[49 + i]


def unpack(gath, sgath):
    one = lambda *shape: jax.ShapeDtypeStruct(shape, F32)
    return pl.pallas_call(
        unpack_kernel,
        out_shape=(
            one(7, 7, 128), one(128), one(128), one(128), one(128, 512), one(512),
            one(512, 128), one(128), one(128),
        ),
        in_specs=[VMEM, VMEM],
        out_specs=(VMEM,) * 9,
        name="unpack",
    )(gath, sgath)


def body(
    inputs, kernel, conv_bias, norm_gain, norm_bias, expand_weight, expand_bias,
    reduce_weight, reduce_bias, layer_scale, neighbours, cotangent,
):
    x = inputs[0]
    halos = exchange_halos(neighbours, x)
    params = (
        kernel, conv_bias, norm_gain, norm_bias, expand_weight, expand_bias,
        reduce_weight, reduce_bias, layer_scale,
    )
    out, big, small = run_block(neighbours, x, cotangent[0], halos, params)
    factor = 1.0 / math.sqrt(FACES * 256 * 256)
    gath, sgath = sum_all(big, small, factor)
    return (out[None], *unpack(gath, sgath))


def solution(mesh):
    split = P("face", "tile", None, None)
    return jax.shard_map(
        body,
        mesh=mesh,
        in_specs=(split,) + (P(),) * 10 + (split,),
        out_specs=(split,) + (P(),) * 9,
        check_vma=False,
    )
```

```python
import functools
import math

import jax
import jax.numpy as jnp
from jax import lax
from jax.experimental import pallas as pl
from jax.experimental.pallas import tpu as pltpu
from jax.sharding import PartitionSpec as P

EPS = 1e-06
MESH = pl.DeviceIdType.MESH
BF = jnp.bfloat16
F32 = jnp.float32
ROOT = math.sqrt(2.0 / math.pi)
CUBE = 0.044715
FACES = 8
TILES = 32
VMEM = pl.BlockSpec(memory_space=pltpu.VMEM)
SMEM = pl.BlockSpec(memory_space=pltpu.SMEM)
ANY = pl.BlockSpec(memory_space=pl.ANY)


def place():
    return lax.axis_index("face"), lax.axis_index("tile")


def remote(src, dst, send, recv, face, tile):
    return pltpu.make_async_remote_copy(
        src_ref=src, dst_ref=dst, send_sem=send, recv_sem=recv,
        device_id=(face, tile), device_id_type=MESH,
    )


def nt(left, right):
    return lax.dot_general(left, right, (((1,), (1,)), ((), ())), preferred_element_type=F32)


def nn(left, right):
    return lax.dot_general(left, right, (((1,), (0,)), ((), ())), preferred_element_type=F32)


def one_hot(rows, cols, index):
    r = lax.broadcasted_iota(jnp.int32, (rows, cols), 0)
    c = lax.broadcasted_iota(jnp.int32, (rows, cols), 1)
    return jnp.where(c == index(r), 1.0, 0.0).astype(BF)


def fold(v):
    rows, chans = v.shape
    return jnp.sum(v.reshape(rows // 8, 8, chans), 0)


def main_kernel(
    factor,
    nbr, x_hbm, cot_hbm, kern_hbm, cb_hbm, gain_hbm, nb_hbm, we_hbm, be_hbm, wr_hbm, br_hbm, ls_hbm,
    out_hbm, gath, sgath,
    x, cot, kern, cb, gain, nb, we, be, wr, br, ls, out,
    top, bot, hbuf, side, pieces, chosen, nsbuf, nsend,
    pad, conv, taps, act, acc_e, acc_r, sums,
    bigf, half, bigb, slots1, slotsz, small, sslots1, sslots2, few_ref,
    load_sem, out_sem, row_send, row_recv, piece_send, piece_recv, band_send, band_recv,
    side_send, side_recv, fwd_send, fwd_recv, local_sem,
    core_sem, s1, r1, sz, rz, s4, r4, ss1, sr1, ss2, sr2, ss4, sr4,
):
    f, t = place()
    last = TILES - 1
    mirror = last - t
    is_first = t == 0
    is_last = t == last
    has_up = t > 0
    has_down = t < last
    mir_up = jnp.logical_and(mirror < last, mirror + 1 != t)
    mir_down = jnp.logical_and(mirror > 0, mirror - 1 != t)
    edge = jnp.logical_or(is_first, is_last)
    hi = t // 16
    s = t % 16
    z = s // 2
    core = s % 2
    twin = t + 1 - 2 * core
    a = hi * 8 + f
    others = [lax.rem(f + k, FACES) for k in range(1, FACES)]
    plane = [lax.rem(a + k, 16) for k in range(1, 16)]
    line = [lax.rem(s + k, 16) for k in range(1, 16)]
    stack = [lax.rem(z + k, 8) for k in range(1, 8)]

    def plane_id(p):
        return lax.rem(p, 8), p // 8 * 16 + s

    loads = [
        pltpu.make_async_copy(src, dst, load_sem.at[i])
        for i, (src, dst) in enumerate(
            (
                (x_hbm, x), (kern_hbm, kern), (cb_hbm, cb), (cot_hbm, cot), (we_hbm, we), (wr_hbm, wr),
                (gain_hbm, gain), (nb_hbm, nb), (be_hbm, be), (br_hbm, br), (ls_hbm, ls),
            )
        )
    ]
    for load in loads:
        load.start()

    barrier = pltpu.get_barrier_semaphore()

    def hello(face, tile):
        pl.semaphore_signal(barrier, inc=1, device_id=(face, tile), device_id_type=MESH)

    for p in plane:
        hello(*plane_id(p))
    for p in line:
        hello(f, hi * 16 + p)
    hello(f, mirror)

    @pl.when(has_up)
    def _():
        hello(f, t - 1)

    @pl.when(has_down)
    def _():
        hello(f, t + 1)

    @pl.when(mir_up)
    def _():
        hello(f, mirror + 1)

    @pl.when(mir_down)
    def _():
        hello(f, mirror - 1)

    @pl.when(edge)
    def _():
        for g in range(FACES):
            hello(g, mirror)

    loads[0].wait()
    for d in range(3):
        west = x[:, d : d + 1, :].astype(F32).reshape(8, 128)
        east = x[:, 255 - d : 256 - d, :].astype(F32).reshape(8, 128)
        pieces[f, d] = jnp.concatenate([west, east], 0).astype(BF)
    pad[3:11, 8:264, :] = x[...].astype(F32)
    for load in loads[1:3]:
        load.wait()
    for i in range(7):
        for j in range(7):
            taps[i * 7 + j] = jnp.broadcast_to(kern[i, j : j + 1, :], (8, 128))
    bias = jnp.broadcast_to(cb[...].reshape(1, 128), (8, 128))

    def convolve(col, acc, out_rows, in_rows):
        acc = dict(zip(out_rows, acc))
        for j in range(7):
            for row in in_rows:
                hit = [r for r in out_rows if 0 <= row - r < 7]
                if hit:
                    v = pad[row, pl.ds(col + 5 + j, 8), :]
                    for r in hit:
                        acc[r] = acc[r] + taps[(row - r) * 7 + j] * v
        return [acc[r] for r in out_rows]

    @pl.loop(2, 30)
    def _(jb):
        col = pl.multiple_of(jb * 8, 8)
        for r, v in enumerate(convolve(col, [bias] * 8, range(8), range(3, 11))):
            conv[r, pl.ds(col, 8), :] = v

    one = lambda cond: cond.astype(jnp.int32)
    count = 31 + one(has_up) + one(has_down) + one(mir_up) + one(mir_down) + 8 * one(edge)
    pl.semaphore_wait(barrier, count)

    def band_copy(rows, k, g):
        return remote(
            x.at[pl.ds(rows, 3), pl.ds(pl.multiple_of(g * 32, 32), 32), :], nsbuf.at[f],
            band_send.at[k], band_recv.at[f], g, t,
        )

    def piece_copy(k, g):
        return remote(pieces.at[f], pieces.at[f], piece_send.at[k], piece_recv.at[f], g, t)

    def up_copy():
        return remote(x.at[pl.ds(0, 3)], bot, row_send.at[0], row_recv.at[0], f, t - 1)

    def down_copy():
        return remote(x.at[pl.ds(5, 3)], top, row_send.at[1], row_recv.at[1], f, t + 1)

    for rows, cond in ((0, is_first), (5, is_last)):

        @pl.when(cond)
        def _(rows=rows):
            for k, g in enumerate(others):
                band_copy(rows, k, g).start()
            nsbuf[f] = x[rows : rows + 3, pl.ds(pl.multiple_of(f * 32, 32), 32), :]

    for k, g in enumerate(others):
        piece_copy(k, g).start()

    @pl.when(has_up)
    def _():
        up_copy().start()

    @pl.when(has_down)
    def _():
        down_copy().start()

    for load in loads[3:]:
        load.wait()

    def forward(g):
        return remote(nsend.at[g], hbuf.at[f], fwd_send.at[g], fwd_recv.at[f], g, mirror)

    def side_copy(slot, tile):
        return remote(chosen, side.at[slot], side_send.at[slot], side_recv.at[slot], f, tile)

    def phase_two():
        for side_id, rows, cond in ((0, 5, is_last), (2, 0, is_first)):

            @pl.when(cond)
            def _(side_id=side_id, rows=rows):
                for k, g in enumerate(others):
                    remote(
                        x.at[pl.ds(rows, 3), pl.ds(pl.multiple_of(g * 32, 32), 32), :], nsbuf.at[g],
                        band_send.at[k], band_recv.at[g], g, t,
                    ).wait_recv()
                for g in range(FACES):
                    nsend[g] = nsbuf[nbr[g, side_id, 0]]
                    forward(g).start()

        for k, g in enumerate(others):
            remote(pieces.at[f], pieces.at[g], piece_send.at[k], piece_recv.at[g], g, t).wait_recv()
        from_west = pieces[nbr[f, 3, 0]]
        from_east = pieces[nbr[f, 1, 0]]
        chosen[...] = jnp.concatenate(
            [from_west.astype(F32)[:, 8:16], from_east.astype(F32)[:, 0:8]], 1
        ).astype(BF)
        side_copy(4, mirror).start()

        @pl.when(has_down)
        def _():
            side_copy(0, t + 1).start()

        @pl.when(has_up)
        def _():
            side_copy(2, t - 1).start()

        @pl.when(mir_up)
        def _():
            side_copy(3, mirror + 1).start()

        @pl.when(mir_down)
        def _():
            side_copy(5, mirror - 1).start()

        side[1] = chosen[...]

        @pl.when(mirror + 1 == t)
        def _():
            side[3] = chosen[...]

        @pl.when(mirror - 1 == t)
        def _():
            side[5] = chosen[...]

    def polar(flag, rows):
        for g in range(FACES):
            remote(
                nsend.at[g], hbuf.at[g], fwd_send.at[g], fwd_recv.at[g], g, mirror
            ).wait_recv()
        turn = one_hot(256, 256, lambda r: 255 - r)
        for d in range(3):
            band = jnp.concatenate([hbuf[k, d] for k in range(8)], 0)
            turned = nn(turn, band)
            pad[rows[d], 8:264, :] = jnp.where(flag == 1, turned, band.astype(F32))

    def finish(out_rows, in_rows):
        @pl.loop(2, 30)
        def _(jb):
            col = pl.multiple_of(jb * 8, 8)
            acc = [conv[r, pl.ds(col, 8), :] for r in out_rows]
            for r, v in zip(out_rows, convolve(col, acc, out_rows, in_rows)):
                conv[r, pl.ds(col, 8), :] = v

    def finish_top():
        @pl.when(has_up)
        def _():
            down_copy().wait_recv()
            pad[0:3, 8:264, :] = top[...].astype(F32)

        @pl.when(is_first)
        def _():
            polar(nbr[f, 0, 2], (0, 1, 2))

        finish(range(0, 3), range(0, 3))

    def finish_bottom():
        @pl.when(has_down)
        def _():
            up_copy().wait_recv()
            pad[11:14, 8:264, :] = bot[...].astype(F32)

        @pl.when(is_last)
        def _():
            polar(nbr[f, 2, 2], (11, 12, 13))

        finish(range(5, 8), range(11, 14))

    acc_e[...] = jnp.zeros_like(acc_e)
    acc_r[...] = jnp.zeros_like(acc_r)
    sums[...] = jnp.zeros_like(sums)
    mean_of = jnp.full((128, 128), 1.0 / 128, BF)
    vec = lambda ref: ref[...].reshape(1, -1)

    def mlp(c, cotangent, rows):
        count = c.shape[0]
        centred = c - nn(c.astype(BF), mean_of)
        variance = nn((centred * centred).astype(BF), mean_of)
        inverse = lax.rsqrt(variance + EPS)
        normed = centred * inverse
        scaled = (normed * vec(gain) + vec(nb)).astype(BF)
        branch_cot = (cotangent.astype(F32) * vec(ls)).astype(BF)
        hidden = nn(scaled, we[...]) + vec(be)
        active_cot = nt(branch_cot, wr[...])
        square = hidden * hidden
        gate = 0.5 + 0.5 * jnp.tanh(hidden * (ROOT + (ROOT * CUBE) * square))
        active = hidden * gate
        active_low = active.astype(BF)
        slope = gate + active * (1.0 - gate) * (2.0 * ROOT + (6.0 * ROOT * CUBE) * square)
        hidden_cot = (active_cot * slope).astype(BF)
        act[rows, :] = active_low
        left = jnp.concatenate([scaled.T, jnp.ones((16, count), BF)], 0)
        acc_e[...] += nn(left, hidden_cot)
        acc_r[...] += nn(branch_cot.T, active_low)
        scaled_cot = nt(hidden_cot, we[...])
        normed_cot = scaled_cot * vec(gain)
        m1 = nn(normed_cot.astype(BF), mean_of)
        m2 = nn((normed_cot * normed).astype(BF), mean_of)
        conv_cot = inverse * (normed_cot - m1 - normed * m2)
        sums[0] += fold(conv_cot)
        sums[1] += fold(scaled_cot * normed)
        sums[2] += fold(scaled_cot)
        sums[3] += fold(branch_cot.astype(F32))
        return conv_cot

    low_first = t < 16

    def row_of(i):
        return jnp.where(low_first, 4 - 4 * i, 4 * i)

    @pl.loop(0, 2)
    def _(i):
        r0 = row_of(i)

        @pl.when(r0 == 0)
        def _():
            finish_top()

        @pl.when(r0 == 4)
        def _():
            finish_bottom()

        @pl.when(i == 0)
        def _():
            phase_two()

        four = pl.ds(r0, 4)
        got = mlp(
            conv[four, 16:240, :].reshape(896, 128),
            cot[four, 16:240, :].reshape(896, 128),
            pl.ds(pl.multiple_of(i * 896, 128), 896),
        )
        conv[four, 16:240, :] = got.reshape(4, 224, 128)

    side_copy(4, mirror).wait_recv()

    @pl.when(has_up)
    def _():
        side_copy(0, t - 1).wait_recv()

    @pl.when(has_down)
    def _():
        side_copy(2, t + 1).wait_recv()

    @pl.when(mir_up)
    def _():
        side_copy(3, mirror + 1).wait_recv()

    @pl.when(mir_down)
    def _():
        side_copy(5, mirror - 1).wait_recv()

    @pl.when(is_first)
    def _():
        side[0] = jnp.zeros((3, 16, 128), BF)
        side[3] = jnp.zeros((3, 16, 128), BF)

    @pl.when(is_last)
    def _():
        side[2] = jnp.zeros((3, 16, 128), BF)
        side[5] = jnp.zeros((3, 16, 128), BF)

    turn = one_hot(24, 24, lambda r: r // 8 * 8 + 7 - r % 8)
    for d in range(3):
        slots = [side[i, d].astype(F32) for i in range(6)]
        for first, side_id, col in ((0, 3, 7 - d), (8, 1, 264 + d)):
            straight = jnp.concatenate([slots[i][first : first + 8] for i in (0, 1, 2)], 0)
            turned = jnp.concatenate([slots[i][first : first + 8] for i in (3, 4, 5)], 0)
            turned = nn(turn, turned.astype(BF))
            halo = jnp.where(nbr[f, side_id, 2] == 1, turned, straight)
            pad[0:14, col : col + 1, :] = halo[5:19].reshape(14, 1, 128)

    @pl.loop(0, 4)
    def _(i):
        col = pl.multiple_of((i + i // 2 * 28) * 8, 8)
        for r, v in enumerate(convolve(col, [bias] * 8, range(8), range(14))):
            conv[r, pl.ds(col, 8), :] = v

    got = mlp(
        jnp.concatenate([conv[:, 0:16, :], conv[:, 240:256, :]], 1).reshape(256, 128),
        jnp.concatenate([cot[:, 0:16, :], cot[:, 240:256, :]], 1).reshape(256, 128),
        pl.ds(1792, 256),
    ).reshape(8, 32, 128)
    conv[:, 0:16, :] = got[:, 0:16]
    conv[:, 240:256, :] = got[:, 16:32]

    scale = jnp.zeros((8, 128), F32)
    for q in range(4):
        cols = slice(q * 128, q * 128 + 128)
        bigf[q * 128 : q * 128 + 128, :] = acc_e[0:128, cols]
        turned = acc_r[:, cols].T
        bigf[512 + q * 128 : 640 + q * 128, :] = turned
        scale = scale + fold(turned * wr[cols, :].astype(F32))

    def halve(part):
        return remote(
            bigf.at[pl.ds(pl.multiple_of(part * 512, 512), 512)], half, core_sem.at[0], core_sem.at[1],
            f, twin,
        )

    halve(1 - core).start()

    small[...] = jnp.zeros_like(small)
    totals = [jnp.sum(sums[i], 0, keepdims=True) for i in range(4)]
    totals.append((jnp.sum(scale, 0, keepdims=True) + vec(br) * totals[3]) / vec(ls))
    for i in range(5):
        small[49 + i : 50 + i, :] = totals[i]
    for q in range(4):
        small[54 + q : 55 + q, :] = acc_e[128:129, q * 128 : q * 128 + 128]

    def kernel_grad(first, stop):
        @pl.loop(first, stop)
        def _(j):
            def step(jb, acc):
                col = pl.multiple_of(jb * 8, 8)
                acc = list(acc)
                cots = [conv[r, pl.ds(col, 8), :] for r in range(8)]
                for row in range(14):
                    v = pad[row, pl.ds(col + 5 + j, 8), :]
                    for i in range(7):
                        if 0 <= row - i < 8:
                            acc[i] = acc[i] + cots[row - i] * v
                return tuple(acc)

            acc = lax.fori_loop(0, 32, step, (jnp.zeros((8, 128), F32),) * 7)
            for i in range(7):
                small[pl.ds(i * 7 + j, 1), :] = jnp.sum(acc[i], 0, keepdims=True)

    kernel_grad(0, 2)
    halve(core).wait_recv()
    mine = bigf[pl.ds(pl.multiple_of(core * 512, 512), 512), :] + half[...]
    bigb[...] = mine.astype(BF).reshape(16, 32, 128)

    def big1(k, p, slot):
        return remote(bigb.at[p], slots1.at[slot], s1.at[k], r1.at[slot], *plane_id(p))

    for k, p in enumerate(plane):
        big1(k, p, a).start()
    slots1[a] = bigb[a]
    kernel_grad(2, 7)

    def small1(k, p, slot):
        rows = pl.ds(pl.multiple_of(lax.rem(p, 8) * 8, 8), 8)
        return remote(small.at[rows], sslots1.at[slot], ss1.at[k], sr1.at[slot], *plane_id(p))

    for k, p in enumerate(plane):
        small1(k, p, a).start()
    sslots1[a] = small[pl.ds(pl.multiple_of(f * 8, 8), 8), :]

    for k, p in enumerate(plane):
        big1(k, p, p).wait_recv()
    total = slots1[0].astype(F32)
    for p in range(1, 16):
        total = total + slots1[p].astype(F32)
    slotsz[z] = total.astype(BF)

    def bigz(k, q, slot):
        return remote(
            slotsz.at[z], slotsz.at[slot], sz.at[k], rz.at[slot], f, hi * 16 + q * 2 + core
        )

    for k, q in enumerate(stack):
        bigz(k, q, z).start()

    def output(rows, residual):
        branch = nn(act[rows, :], wr[...]) + vec(br)
        return (residual.astype(F32) + vec(ls) * branch).astype(BF)

    @pl.loop(0, 2)
    def _(i):
        four = pl.ds(row_of(i), 4)
        rows = pl.ds(pl.multiple_of(i * 896, 128), 896)
        out[four, 16:240, :] = output(rows, x[four, 16:240, :].reshape(896, 128)).reshape(4, 224, 128)

    sides = output(
        pl.ds(1792, 256),
        jnp.concatenate([x[:, 0:16, :], x[:, 240:256, :]], 1).reshape(256, 128),
    ).reshape(8, 32, 128)
    out[:, 0:16, :] = sides[:, 0:16]
    out[:, 240:256, :] = sides[:, 16:32]
    store = pltpu.make_async_copy(out, out_hbm, out_sem.at[0])
    store.start()

    for k, p in enumerate(plane):
        small1(k, p, p).wait_recv()
    few = sslots1[0]
    for p in range(1, 16):
        few = few + sslots1[p]
    few_ref[...] = few

    def small2(k, p, slot):
        return remote(few_ref, sslots2.at[slot], ss2.at[k], sr2.at[slot], f, hi * 16 + p)

    for k, p in enumerate(line):
        small2(k, p, s).start()
    sslots2[s] = few

    for k, q in enumerate(stack):
        bigz(k, q, q).wait_recv()
    total = slotsz[0].astype(F32)
    for q in range(1, 8):
        total = total + slotsz[q].astype(F32)
    gath[core, a] = (total * factor).astype(BF)

    def big4(k, p, slot):
        return remote(gath.at[core, a], gath.at[core, slot], s4.at[k], r4.at[slot], *plane_id(p))

    for k, p in enumerate(plane):
        big4(k, p, a).start()

    for k, p in enumerate(line):
        small2(k, p, p).wait_recv()
    few = sslots2[0]
    for p in range(1, 16):
        few = few + sslots2[p]
    sgath[f] = few * factor

    def small4(k, g, slot):
        return remote(sgath.at[f], sgath.at[slot], ss4.at[k], sr4.at[slot], g, t)

    for k, g in enumerate(others):
        small4(k, g, f).start()

    for k, p in enumerate(plane):
        big4(k, p, p).wait_recv()

    def share(part):
        return remote(gath.at[part], gath.at[part], core_sem.at[2], core_sem.at[3], f, twin)

    share(core).start()
    for k, g in enumerate(others):
        small4(k, g, g).wait_recv()
    share(1 - core).wait_recv()

    store.wait()
    for k, g in enumerate(others):
        piece_copy(k, g).wait_send()
        small4(k, g, f).wait_send()
    side_copy(4, mirror).wait_send()

    @pl.when(has_up)
    def _():
        side_copy(2, t - 1).wait_send()
        up_copy().wait_send()

    @pl.when(has_down)
    def _():
        side_copy(0, t + 1).wait_send()
        down_copy().wait_send()

    @pl.when(mir_up)
    def _():
        side_copy(3, mirror + 1).wait_send()

    @pl.when(mir_down)
    def _():
        side_copy(5, mirror - 1).wait_send()

    @pl.when(edge)
    def _():
        for k, g in enumerate(others):
            band_copy(0, k, g).wait_send()
        for g in range(FACES):
            forward(g).wait_send()

    halve(1 - core).wait_send()
    share(core).wait_send()
    for k, p in enumerate(plane):
        big1(k, p, a).wait_send()
        small1(k, p, a).wait_send()
        big4(k, p, a).wait_send()
    for k, p in enumerate(line):
        small2(k, p, s).wait_send()
    for k, q in enumerate(stack):
        bigz(k, q, z).wait_send()


def run_main(factor, neighbours, *operands):
    dma = pltpu.SemaphoreType.DMA
    shape = lambda *dims: jax.ShapeDtypeStruct(dims, BF)
    return pl.pallas_call(
        functools.partial(main_kernel, factor),
        out_shape=(
            shape(8, 256, 128),
            shape(2, 16, 32, 128),
            jax.ShapeDtypeStruct((8, 8, 128), F32),
        ),
        in_specs=[SMEM] + [ANY] * 11,
        out_specs=(ANY, VMEM, VMEM),
        scratch_shapes=[pltpu.VMEM(item.shape, item.dtype) for item in operands]
        + [
            pltpu.VMEM((8, 256, 128), BF),
            pltpu.VMEM((3, 256, 128), BF),
            pltpu.VMEM((3, 256, 128), BF),
            pltpu.VMEM((8, 3, 32, 128), BF),
            pltpu.VMEM((6, 3, 16, 128), BF),
            pltpu.VMEM((8, 3, 16, 128), BF),
            pltpu.VMEM((3, 16, 128), BF),
            pltpu.VMEM((8, 3, 32, 128), BF),
            pltpu.VMEM((8, 3, 32, 128), BF),
            pltpu.VMEM((14, 272, 128), F32),
            pltpu.VMEM((8, 256, 128), F32),
            pltpu.VMEM((49, 8, 128), F32),
            pltpu.VMEM((2048, 512), BF),
            pltpu.VMEM((144, 512), F32),
            pltpu.VMEM((128, 512), F32),
            pltpu.VMEM((4, 8, 128), F32),
            pltpu.VMEM((1024, 128), F32),
            pltpu.VMEM((512, 128), F32),
            pltpu.VMEM((16, 32, 128), BF),
            pltpu.VMEM((16, 32, 128), BF),
            pltpu.VMEM((8, 32, 128), BF),
            pltpu.VMEM((64, 128), F32),
            pltpu.VMEM((16, 8, 128), F32),
            pltpu.VMEM((16, 8, 128), F32),
            pltpu.VMEM((8, 128), F32),
            dma((11,)), dma((1,)), dma((2,)), dma((2,)), dma((8,)), dma((8,)), dma((8,)), dma((8,)),
            dma((6,)), dma((6,)), dma((8,)), dma((8,)), dma((2,)),
            dma((4,)),
        ]
        + [dma((16,))] * 12,
        compiler_params=pltpu.CompilerParams(
            collective_id=0, has_side_effects=True, vmem_limit_bytes=56 * 1024 * 1024
        ),
        name="main",
    )(neighbours, *operands)


def unpack_kernel(
    raw, gath, sgath,
    out, kernel_grad, cb_grad, gain_grad, nb_grad, we_grad, be_grad, wr_grad, br_grad, ls_grad,
    sem,
):
    copy = pltpu.make_async_copy(raw, out, sem.at[0])
    copy.start()
    rows = gath.reshape(1024, 128)
    few = sgath[...].reshape(64, 128)
    for q in range(4):
        we_grad[:, q * 128 : q * 128 + 128] = rows[q * 128 : q * 128 + 128, :].astype(F32)
        be_grad[q * 128 : q * 128 + 128] = few[54 + q]
    wr_grad[...] = rows[512:1024, :].astype(F32)
    for i in range(7):
        kernel_grad[i] = few[i * 7 : i * 7 + 7]
    for i, ref in enumerate((cb_grad, gain_grad, nb_grad, br_grad, ls_grad)):
        ref[...] = few[49 + i]
    copy.wait()


def unpack(raw, gath, sgath):
    one = lambda *shape: jax.ShapeDtypeStruct(shape, F32)
    return pl.pallas_call(
        unpack_kernel,
        out_shape=(
            jax.ShapeDtypeStruct(raw.shape, raw.dtype),
            one(7, 7, 128), one(128), one(128), one(128), one(128, 512), one(512),
            one(512, 128), one(128), one(128),
        ),
        in_specs=[ANY, VMEM, VMEM],
        out_specs=(ANY,) + (VMEM,) * 9,
        scratch_shapes=[pltpu.SemaphoreType.DMA((1,))],
        name="unpack",
    )(raw, gath, sgath)


def body(
    inputs, kernel, conv_bias, norm_gain, norm_bias, expand_weight, expand_bias,
    reduce_weight, reduce_bias, layer_scale, neighbours, cotangent,
):
    factor = 1.0 / math.sqrt(FACES * 256 * 256)
    raw, gath, sgath = run_main(
        factor, neighbours, inputs[0], cotangent[0], kernel, conv_bias, norm_gain, norm_bias,
        expand_weight, expand_bias, reduce_weight, reduce_bias, layer_scale,
    )
    out, *grads = unpack(raw, gath, sgath)
    return (out[None], *grads)


def solution(mesh):
    split = P("face", "tile", None, None)
    return jax.shard_map(
        body,
        mesh=mesh,
        in_specs=(split,) + (P(),) * 10 + (split,),
        out_specs=(split,) + (P(),) * 9,
        check_vma=False,
    )
```

```python
import functools
import math

import jax
import jax.numpy as jnp
from jax import lax
from jax.experimental import pallas as pl
from jax.experimental.pallas import tpu as pltpu
from jax.sharding import PartitionSpec as P

EPS = 1e-06
MESH = pl.DeviceIdType.MESH
BF = jnp.bfloat16
F32 = jnp.float32
ROOT = math.sqrt(2.0 / math.pi)
CUBE = 0.044715
FACES = 8
TILES = 32
VMEM = pl.BlockSpec(memory_space=pltpu.VMEM)
SMEM = pl.BlockSpec(memory_space=pltpu.SMEM)
ANY = pl.BlockSpec(memory_space=pl.ANY)


def place():
    return lax.axis_index("face"), lax.axis_index("tile")


def remote(src, dst, send, recv, face, tile):
    return pltpu.make_async_remote_copy(
        src_ref=src, dst_ref=dst, send_sem=send, recv_sem=recv,
        device_id=(face, tile), device_id_type=MESH,
    )


def nt(left, right):
    return lax.dot_general(left, right, (((1,), (1,)), ((), ())), preferred_element_type=F32)


def nn(left, right):
    return lax.dot_general(left, right, (((1,), (0,)), ((), ())), preferred_element_type=F32)


def one_hot(rows, cols, index):
    r = lax.broadcasted_iota(jnp.int32, (rows, cols), 0)
    c = lax.broadcasted_iota(jnp.int32, (rows, cols), 1)
    return jnp.where(c == index(r), 1.0, 0.0).astype(BF)


def fold(v):
    rows, chans = v.shape
    return jnp.sum(v.reshape(rows // 8, 8, chans), 0)


def main_kernel(
    factor,
    nbr_hbm, x_hbm, cot_hbm, kern_hbm, cb_hbm, gain_hbm, nb_hbm, we_hbm, be_hbm, wr_hbm, br_hbm, ls_hbm,
    out_hbm, gath, sgath,
    nbr, x, cot, kern, cb, gain, nb, we, be, wr, br, ls, out,
    top, bot, hbuf, side, pieces, chosen, nsbuf, nsend,
    pad, conv, taps, act, acc_e, acc_r, sums,
    bigf, half, bigb, slots1, slotsz, small, sslots1, sslots2, few_ref,
    load_sem, out_sem, row_send, row_recv, piece_send, piece_recv, band_send, band_recv,
    side_send, side_recv, fwd_send, fwd_recv, local_sem,
    core_sem, s1, r1, sz, rz, s4, r4, ss1, sr1, ss2, sr2, ss4, sr4,
):
    f, t = place()
    last = TILES - 1
    mirror = last - t
    is_first = t == 0
    is_last = t == last
    has_up = t > 0
    has_down = t < last
    mir_up = jnp.logical_and(mirror < last, mirror + 1 != t)
    mir_down = jnp.logical_and(mirror > 0, mirror - 1 != t)
    edge = jnp.logical_or(is_first, is_last)
    hi = t // 16
    s = t % 16
    z = s // 2
    core = s % 2
    twin = t + 1 - 2 * core
    a = hi * 8 + f
    others = [lax.rem(f + k, FACES) for k in range(1, FACES)]
    plane = [lax.rem(a + k, 16) for k in range(1, 16)]
    line = [lax.rem(s + k, 16) for k in range(1, 16)]
    stack = [lax.rem(z + k, 8) for k in range(1, 8)]

    def plane_id(p):
        return lax.rem(p, 8), p // 8 * 16 + s

    loads = [
        pltpu.make_async_copy(src, dst, load_sem.at[i])
        for i, (src, dst) in enumerate(
            (
                (x_hbm, x), (kern_hbm, kern), (cb_hbm, cb), (cot_hbm, cot), (we_hbm, we), (wr_hbm, wr),
                (nbr_hbm, nbr), (gain_hbm, gain), (nb_hbm, nb), (be_hbm, be), (br_hbm, br), (ls_hbm, ls),
            )
        )
    ]
    for load in loads:
        load.start()

    barrier = pltpu.get_barrier_semaphore()

    def hello(face, tile):
        pl.semaphore_signal(barrier, inc=1, device_id=(face, tile), device_id_type=MESH)

    for p in plane:
        hello(*plane_id(p))
    for p in line:
        hello(f, hi * 16 + p)
    hello(f, mirror)

    @pl.when(has_up)
    def _():
        hello(f, t - 1)

    @pl.when(has_down)
    def _():
        hello(f, t + 1)

    @pl.when(mir_up)
    def _():
        hello(f, mirror + 1)

    @pl.when(mir_down)
    def _():
        hello(f, mirror - 1)

    @pl.when(edge)
    def _():
        for g in range(FACES):
            hello(g, mirror)

    loads[0].wait()
    for d in range(3):
        west = x[:, d : d + 1, :].astype(F32).reshape(8, 128)
        east = x[:, 255 - d : 256 - d, :].astype(F32).reshape(8, 128)
        pieces[f, d] = jnp.concatenate([west, east], 0).astype(BF)
    pad[3:11, 8:264, :] = x[...].astype(F32)
    for load in loads[1:3]:
        load.wait()
    for i in range(7):
        for j in range(7):
            taps[i * 7 + j] = jnp.broadcast_to(kern[i, j : j + 1, :], (8, 128))
    bias = jnp.broadcast_to(cb[...].reshape(1, 128), (8, 128))

    def convolve(col, acc, out_rows, in_rows):
        acc = dict(zip(out_rows, acc))
        for j in range(7):
            for row in in_rows:
                hit = [r for r in out_rows if 0 <= row - r < 7]
                if hit:
                    v = pad[row, pl.ds(col + 5 + j, 8), :]
                    for r in hit:
                        acc[r] = acc[r] + taps[(row - r) * 7 + j] * v
        return [acc[r] for r in out_rows]

    @pl.loop(2, 30)
    def _(jb):
        col = pl.multiple_of(jb * 8, 8)
        for r, v in enumerate(convolve(col, [bias] * 8, range(8), range(3, 11))):
            conv[r, pl.ds(col, 8), :] = v

    one = lambda cond: cond.astype(jnp.int32)
    count = 31 + one(has_up) + one(has_down) + one(mir_up) + one(mir_down) + 8 * one(edge)
    pl.semaphore_wait(barrier, count)

    def band_copy(rows, k, g):
        return remote(
            x.at[pl.ds(rows, 3), pl.ds(pl.multiple_of(g * 32, 32), 32), :], nsbuf.at[f],
            band_send.at[k], band_recv.at[f], g, t,
        )

    def piece_copy(k, g):
        return remote(pieces.at[f], pieces.at[f], piece_send.at[k], piece_recv.at[f], g, t)

    def up_copy():
        return remote(x.at[pl.ds(0, 3)], bot, row_send.at[0], row_recv.at[0], f, t - 1)

    def down_copy():
        return remote(x.at[pl.ds(5, 3)], top, row_send.at[1], row_recv.at[1], f, t + 1)

    for rows, cond in ((0, is_first), (5, is_last)):

        @pl.when(cond)
        def _(rows=rows):
            for k, g in enumerate(others):
                band_copy(rows, k, g).start()
            nsbuf[f] = x[rows : rows + 3, pl.ds(pl.multiple_of(f * 32, 32), 32), :]

    for k, g in enumerate(others):
        piece_copy(k, g).start()

    @pl.when(has_up)
    def _():
        up_copy().start()

    @pl.when(has_down)
    def _():
        down_copy().start()

    for load in loads[3:]:
        load.wait()

    def forward(g):
        return remote(nsend.at[g], hbuf.at[f], fwd_send.at[g], fwd_recv.at[f], g, mirror)

    def side_copy(slot, tile):
        return remote(chosen, side.at[slot], side_send.at[slot], side_recv.at[slot], f, tile)

    def phase_two():
        for side_id, rows, cond in ((0, 5, is_last), (2, 0, is_first)):

            @pl.when(cond)
            def _(side_id=side_id, rows=rows):
                for k, g in enumerate(others):
                    remote(
                        x.at[pl.ds(rows, 3), pl.ds(pl.multiple_of(g * 32, 32), 32), :], nsbuf.at[g],
                        band_send.at[k], band_recv.at[g], g, t,
                    ).wait_recv()
                for g in range(FACES):
                    nsend[g] = nsbuf[nbr[0, side_id, g]]
                    forward(g).start()

        for k, g in enumerate(others):
            remote(pieces.at[f], pieces.at[g], piece_send.at[k], piece_recv.at[g], g, t).wait_recv()
        from_west = pieces[nbr[0, 3, f]]
        from_east = pieces[nbr[0, 1, f]]
        chosen[...] = jnp.concatenate(
            [from_west.astype(F32)[:, 8:16], from_east.astype(F32)[:, 0:8]], 1
        ).astype(BF)
        side_copy(4, mirror).start()

        @pl.when(has_down)
        def _():
            side_copy(0, t + 1).start()

        @pl.when(has_up)
        def _():
            side_copy(2, t - 1).start()

        @pl.when(mir_up)
        def _():
            side_copy(3, mirror + 1).start()

        @pl.when(mir_down)
        def _():
            side_copy(5, mirror - 1).start()

        side[1] = chosen[...]

        @pl.when(mirror + 1 == t)
        def _():
            side[3] = chosen[...]

        @pl.when(mirror - 1 == t)
        def _():
            side[5] = chosen[...]

    def polar(flag, rows):
        for g in range(FACES):
            remote(
                nsend.at[g], hbuf.at[g], fwd_send.at[g], fwd_recv.at[g], g, mirror
            ).wait_recv()
        turn = one_hot(256, 256, lambda r: 255 - r)
        for d in range(3):
            band = jnp.concatenate([hbuf[k, d] for k in range(8)], 0)
            turned = nn(turn, band)
            pad[rows[d], 8:264, :] = jnp.where(flag == 1, turned, band.astype(F32))

    def finish(out_rows, in_rows):
        @pl.loop(2, 30)
        def _(jb):
            col = pl.multiple_of(jb * 8, 8)
            acc = [conv[r, pl.ds(col, 8), :] for r in out_rows]
            for r, v in zip(out_rows, convolve(col, acc, out_rows, in_rows)):
                conv[r, pl.ds(col, 8), :] = v

    def finish_top():
        @pl.when(has_up)
        def _():
            down_copy().wait_recv()
            pad[0:3, 8:264, :] = top[...].astype(F32)

        @pl.when(is_first)
        def _():
            polar(nbr[2, 0, f], (0, 1, 2))

        finish(range(0, 3), range(0, 3))

    def finish_bottom():
        @pl.when(has_down)
        def _():
            up_copy().wait_recv()
            pad[11:14, 8:264, :] = bot[...].astype(F32)

        @pl.when(is_last)
        def _():
            polar(nbr[2, 2, f], (11, 12, 13))

        finish(range(5, 8), range(11, 14))

    acc_e[...] = jnp.zeros_like(acc_e)
    acc_r[...] = jnp.zeros_like(acc_r)
    sums[...] = jnp.zeros_like(sums)
    mean_of = jnp.full((128, 128), 1.0 / 128, BF)
    vec = lambda ref: ref[...].reshape(1, -1)

    def mlp(c, cotangent, rows):
        count = c.shape[0]
        centred = c - nn(c.astype(BF), mean_of)
        variance = nn((centred * centred).astype(BF), mean_of)
        inverse = lax.rsqrt(variance + EPS)
        normed = centred * inverse
        scaled = (normed * vec(gain) + vec(nb)).astype(BF)
        branch_cot = (cotangent.astype(F32) * vec(ls)).astype(BF)
        hidden = nn(scaled, we[...]) + vec(be)
        active_cot = nt(branch_cot, wr[...])
        square = hidden * hidden
        gate = 0.5 + 0.5 * jnp.tanh(hidden * (ROOT + (ROOT * CUBE) * square))
        active = hidden * gate
        active_low = active.astype(BF)
        slope = gate + active * (1.0 - gate) * (2.0 * ROOT + (6.0 * ROOT * CUBE) * square)
        hidden_cot = (active_cot * slope).astype(BF)
        act[rows, :] = active_low
        left = jnp.concatenate([scaled.T, jnp.ones((16, count), BF)], 0)
        acc_e[...] += nn(left, hidden_cot)
        acc_r[...] += nn(branch_cot.T, active_low)
        scaled_cot = nt(hidden_cot, we[...])
        normed_cot = scaled_cot * vec(gain)
        m1 = nn(normed_cot.astype(BF), mean_of)
        m2 = nn((normed_cot * normed).astype(BF), mean_of)
        conv_cot = inverse * (normed_cot - m1 - normed * m2)
        sums[0] += fold(conv_cot)
        sums[1] += fold(scaled_cot * normed)
        sums[2] += fold(scaled_cot)
        sums[3] += fold(branch_cot.astype(F32))
        return conv_cot

    low_first = t < 16

    def row_of(i):
        return jnp.where(low_first, 4 - 4 * i, 4 * i)

    @pl.loop(0, 2)
    def _(i):
        r0 = row_of(i)

        @pl.when(r0 == 0)
        def _():
            finish_top()

        @pl.when(r0 == 4)
        def _():
            finish_bottom()

        @pl.when(i == 0)
        def _():
            phase_two()

        four = pl.ds(r0, 4)
        got = mlp(
            conv[four, 16:240, :].reshape(896, 128),
            cot[four, 16:240, :].reshape(896, 128),
            pl.ds(pl.multiple_of(i * 896, 128), 896),
        )
        conv[four, 16:240, :] = got.reshape(4, 224, 128)

    side_copy(4, mirror).wait_recv()

    @pl.when(has_up)
    def _():
        side_copy(0, t - 1).wait_recv()

    @pl.when(has_down)
    def _():
        side_copy(2, t + 1).wait_recv()

    @pl.when(mir_up)
    def _():
        side_copy(3, mirror + 1).wait_recv()

    @pl.when(mir_down)
    def _():
        side_copy(5, mirror - 1).wait_recv()

    @pl.when(is_first)
    def _():
        side[0] = jnp.zeros((3, 16, 128), BF)
        side[3] = jnp.zeros((3, 16, 128), BF)

    @pl.when(is_last)
    def _():
        side[2] = jnp.zeros((3, 16, 128), BF)
        side[5] = jnp.zeros((3, 16, 128), BF)

    turn = one_hot(24, 24, lambda r: r // 8 * 8 + 7 - r % 8)
    for d in range(3):
        slots = [side[i, d].astype(F32) for i in range(6)]
        for first, side_id, col in ((0, 3, 7 - d), (8, 1, 264 + d)):
            straight = jnp.concatenate([slots[i][first : first + 8] for i in (0, 1, 2)], 0)
            turned = jnp.concatenate([slots[i][first : first + 8] for i in (3, 4, 5)], 0)
            turned = nn(turn, turned.astype(BF))
            halo = jnp.where(nbr[2, side_id, f] == 1, turned, straight)
            pad[0:14, col : col + 1, :] = halo[5:19].reshape(14, 1, 128)

    @pl.loop(0, 4)
    def _(i):
        col = pl.multiple_of((i + i // 2 * 28) * 8, 8)
        for r, v in enumerate(convolve(col, [bias] * 8, range(8), range(14))):
            conv[r, pl.ds(col, 8), :] = v

    got = mlp(
        jnp.concatenate([conv[:, 0:16, :], conv[:, 240:256, :]], 1).reshape(256, 128),
        jnp.concatenate([cot[:, 0:16, :], cot[:, 240:256, :]], 1).reshape(256, 128),
        pl.ds(1792, 256),
    ).reshape(8, 32, 128)
    conv[:, 0:16, :] = got[:, 0:16]
    conv[:, 240:256, :] = got[:, 16:32]

    scale = jnp.zeros((8, 128), F32)
    for q in range(4):
        cols = slice(q * 128, q * 128 + 128)
        bigf[q * 128 : q * 128 + 128, :] = acc_e[0:128, cols]
        turned = acc_r[:, cols].T
        bigf[512 + q * 128 : 640 + q * 128, :] = turned
        scale = scale + fold(turned * wr[cols, :].astype(F32))

    def halve(part):
        return remote(
            bigf.at[pl.ds(pl.multiple_of(part * 512, 512), 512)], half, core_sem.at[0], core_sem.at[1],
            f, twin,
        )

    halve(1 - core).start()

    small[...] = jnp.zeros_like(small)
    totals = [jnp.sum(sums[i], 0, keepdims=True) for i in range(4)]
    totals.append((jnp.sum(scale, 0, keepdims=True) + vec(br) * totals[3]) / vec(ls))
    for i in range(5):
        small[49 + i : 50 + i, :] = totals[i]
    for q in range(4):
        small[54 + q : 55 + q, :] = acc_e[128:129, q * 128 : q * 128 + 128]

    def kernel_grad(first, stop):
        @pl.loop(first, stop)
        def _(j):
            def step(jb, acc):
                col = pl.multiple_of(jb * 8, 8)
                acc = list(acc)
                cots = [conv[r, pl.ds(col, 8), :] for r in range(8)]
                for row in range(14):
                    v = pad[row, pl.ds(col + 5 + j, 8), :]
                    for i in range(7):
                        if 0 <= row - i < 8:
                            acc[i] = acc[i] + cots[row - i] * v
                return tuple(acc)

            acc = lax.fori_loop(0, 32, step, (jnp.zeros((8, 128), F32),) * 7)
            for i in range(7):
                small[pl.ds(i * 7 + j, 1), :] = jnp.sum(acc[i], 0, keepdims=True)

    kernel_grad(0, 2)
    halve(core).wait_recv()
    mine = bigf[pl.ds(pl.multiple_of(core * 512, 512), 512), :] + half[...]
    bigb[...] = mine.astype(BF).reshape(16, 32, 128)

    def big1(k, p, slot):
        return remote(bigb.at[p], slots1.at[slot], s1.at[k], r1.at[slot], *plane_id(p))

    for k, p in enumerate(plane):
        big1(k, p, a).start()
    slots1[a] = bigb[a]
    kernel_grad(2, 7)

    def small1(k, p, slot):
        rows = pl.ds(pl.multiple_of(lax.rem(p, 8) * 8, 8), 8)
        return remote(small.at[rows], sslots1.at[slot], ss1.at[k], sr1.at[slot], *plane_id(p))

    for k, p in enumerate(plane):
        small1(k, p, a).start()
    sslots1[a] = small[pl.ds(pl.multiple_of(f * 8, 8), 8), :]

    for k, p in enumerate(plane):
        big1(k, p, p).wait_recv()
    total = slots1[0].astype(F32)
    for p in range(1, 16):
        total = total + slots1[p].astype(F32)
    slotsz[z] = total.astype(BF)

    def bigz(k, q, slot):
        return remote(
            slotsz.at[z], slotsz.at[slot], sz.at[k], rz.at[slot], f, hi * 16 + q * 2 + core
        )

    for k, q in enumerate(stack):
        bigz(k, q, z).start()

    def output(rows, residual):
        branch = nn(act[rows, :], wr[...]) + vec(br)
        return (residual.astype(F32) + vec(ls) * branch).astype(BF)

    @pl.loop(0, 2)
    def _(i):
        four = pl.ds(row_of(i), 4)
        rows = pl.ds(pl.multiple_of(i * 896, 128), 896)
        out[four, 16:240, :] = output(rows, x[four, 16:240, :].reshape(896, 128)).reshape(4, 224, 128)

    sides = output(
        pl.ds(1792, 256),
        jnp.concatenate([x[:, 0:16, :], x[:, 240:256, :]], 1).reshape(256, 128),
    ).reshape(8, 32, 128)
    out[:, 0:16, :] = sides[:, 0:16]
    out[:, 240:256, :] = sides[:, 16:32]
    store = pltpu.make_async_copy(out, out_hbm, out_sem.at[0])
    store.start()

    for k, p in enumerate(plane):
        small1(k, p, p).wait_recv()
    few = sslots1[0]
    for p in range(1, 16):
        few = few + sslots1[p]
    few_ref[...] = few

    def small2(k, p, slot):
        return remote(few_ref, sslots2.at[slot], ss2.at[k], sr2.at[slot], f, hi * 16 + p)

    for k, p in enumerate(line):
        small2(k, p, s).start()
    sslots2[s] = few

    for k, q in enumerate(stack):
        bigz(k, q, q).wait_recv()
    total = slotsz[0].astype(F32)
    for q in range(1, 8):
        total = total + slotsz[q].astype(F32)
    gath[core, a] = (total * factor).astype(BF)

    def big4(k, p, slot):
        return remote(gath.at[core, a], gath.at[core, slot], s4.at[k], r4.at[slot], *plane_id(p))

    for k, p in enumerate(plane):
        big4(k, p, a).start()

    for k, p in enumerate(line):
        small2(k, p, p).wait_recv()
    few = sslots2[0]
    for p in range(1, 16):
        few = few + sslots2[p]
    sgath[f] = few * factor

    def small4(k, g, slot):
        return remote(sgath.at[f], sgath.at[slot], ss4.at[k], sr4.at[slot], g, t)

    for k, g in enumerate(others):
        small4(k, g, f).start()

    for k, p in enumerate(plane):
        big4(k, p, p).wait_recv()

    def share(part):
        return remote(gath.at[part], gath.at[part], core_sem.at[2], core_sem.at[3], f, twin)

    share(core).start()
    for k, g in enumerate(others):
        small4(k, g, g).wait_recv()
    share(1 - core).wait_recv()

    store.wait()
    for k, g in enumerate(others):
        piece_copy(k, g).wait_send()
        small4(k, g, f).wait_send()
    side_copy(4, mirror).wait_send()

    @pl.when(has_up)
    def _():
        side_copy(2, t - 1).wait_send()
        up_copy().wait_send()

    @pl.when(has_down)
    def _():
        side_copy(0, t + 1).wait_send()
        down_copy().wait_send()

    @pl.when(mir_up)
    def _():
        side_copy(3, mirror + 1).wait_send()

    @pl.when(mir_down)
    def _():
        side_copy(5, mirror - 1).wait_send()

    @pl.when(edge)
    def _():
        for k, g in enumerate(others):
            band_copy(0, k, g).wait_send()
        for g in range(FACES):
            forward(g).wait_send()

    halve(1 - core).wait_send()
    share(core).wait_send()
    for k, p in enumerate(plane):
        big1(k, p, a).wait_send()
        small1(k, p, a).wait_send()
        big4(k, p, a).wait_send()
    for k, p in enumerate(line):
        small2(k, p, s).wait_send()
    for k, q in enumerate(stack):
        bigz(k, q, z).wait_send()


def run_main(factor, neighbours, *operands):
    dma = pltpu.SemaphoreType.DMA
    shape = lambda *dims: jax.ShapeDtypeStruct(dims, BF)
    return pl.pallas_call(
        functools.partial(main_kernel, factor),
        out_shape=(
            shape(8, 256, 128),
            shape(2, 16, 32, 128),
            jax.ShapeDtypeStruct((8, 8, 128), F32),
        ),
        in_specs=[ANY] * 12,
        out_specs=(ANY, VMEM, VMEM),
        scratch_shapes=[pltpu.SMEM(neighbours.shape, jnp.int32)]
        + [pltpu.VMEM(item.shape, item.dtype) for item in operands]
        + [
            pltpu.VMEM((8, 256, 128), BF),
            pltpu.VMEM((3, 256, 128), BF),
            pltpu.VMEM((3, 256, 128), BF),
            pltpu.VMEM((8, 3, 32, 128), BF),
            pltpu.VMEM((6, 3, 16, 128), BF),
            pltpu.VMEM((8, 3, 16, 128), BF),
            pltpu.VMEM((3, 16, 128), BF),
            pltpu.VMEM((8, 3, 32, 128), BF),
            pltpu.VMEM((8, 3, 32, 128), BF),
            pltpu.VMEM((14, 272, 128), F32),
            pltpu.VMEM((8, 256, 128), F32),
            pltpu.VMEM((49, 8, 128), F32),
            pltpu.VMEM((2048, 512), BF),
            pltpu.VMEM((144, 512), F32),
            pltpu.VMEM((128, 512), F32),
            pltpu.VMEM((4, 8, 128), F32),
            pltpu.VMEM((1024, 128), F32),
            pltpu.VMEM((512, 128), F32),
            pltpu.VMEM((16, 32, 128), BF),
            pltpu.VMEM((16, 32, 128), BF),
            pltpu.VMEM((8, 32, 128), BF),
            pltpu.VMEM((64, 128), F32),
            pltpu.VMEM((16, 8, 128), F32),
            pltpu.VMEM((16, 8, 128), F32),
            pltpu.VMEM((8, 128), F32),
            dma((12,)), dma((1,)), dma((2,)), dma((2,)), dma((8,)), dma((8,)), dma((8,)), dma((8,)),
            dma((6,)), dma((6,)), dma((8,)), dma((8,)), dma((2,)),
            dma((4,)),
        ]
        + [dma((16,))] * 12,
        compiler_params=pltpu.CompilerParams(
            collective_id=0, has_side_effects=True, vmem_limit_bytes=56 * 1024 * 1024
        ),
        name="main",
    )(neighbours, *operands)


def unpack_kernel(
    raw, gath, sgath,
    out, kernel_grad, cb_grad, gain_grad, nb_grad, we_grad, be_grad, wr_grad, br_grad, ls_grad,
    stage, sem,
):
    fetch = pltpu.make_async_copy(raw, stage, sem.at[0])
    store = pltpu.make_async_copy(stage, out, sem.at[1])
    fetch.start()
    rows = gath.reshape(1024, 128)
    few = sgath[...].reshape(64, 128)
    for q in range(4):
        we_grad[:, q * 128 : q * 128 + 128] = rows[q * 128 : q * 128 + 128, :].astype(F32)
        be_grad[q * 128 : q * 128 + 128] = few[54 + q]
    fetch.wait()
    store.start()
    wr_grad[...] = rows[512:1024, :].astype(F32)
    for i in range(7):
        kernel_grad[i] = few[i * 7 : i * 7 + 7]
    for i, ref in enumerate((cb_grad, gain_grad, nb_grad, br_grad, ls_grad)):
        ref[...] = few[49 + i]
    store.wait()


def unpack(raw, gath, sgath):
    one = lambda *shape: jax.ShapeDtypeStruct(shape, F32)
    return pl.pallas_call(
        unpack_kernel,
        out_shape=(
            jax.ShapeDtypeStruct(raw.shape, raw.dtype),
            one(7, 7, 128), one(128), one(128), one(128), one(128, 512), one(512),
            one(512, 128), one(128), one(128),
        ),
        in_specs=[ANY, VMEM, VMEM],
        out_specs=(ANY,) + (VMEM,) * 9,
        scratch_shapes=[pltpu.VMEM(raw.shape, raw.dtype), pltpu.SemaphoreType.DMA((2,))],
        name="unpack",
    )(raw, gath, sgath)


def body(
    inputs, kernel, conv_bias, norm_gain, norm_bias, expand_weight, expand_bias,
    reduce_weight, reduce_bias, layer_scale, neighbours, cotangent,
):
    factor = 1.0 / math.sqrt(FACES * 256 * 256)
    raw, gath, sgath = run_main(
        factor, jnp.transpose(neighbours, (2, 1, 0)), inputs[0], cotangent[0], kernel, conv_bias, norm_gain, norm_bias,
        expand_weight, expand_bias, reduce_weight, reduce_bias, layer_scale,
    )
    out, *grads = unpack(raw, gath, sgath)
    return (out[None], *grads)


def solution(mesh):
    split = P("face", "tile", None, None)
    return jax.shard_map(
        body,
        mesh=mesh,
        in_specs=(split,) + (P(),) * 10 + (split,),
        out_specs=(split,) + (P(),) * 9,
        check_vma=False,
    )
```

```python
import functools
import math

import jax
import jax.numpy as jnp
from jax import lax
from jax.experimental import pallas as pl
from jax.experimental.pallas import tpu as pltpu
from jax.sharding import PartitionSpec as P

EPS = 1e-06
MESH = pl.DeviceIdType.MESH
BF = jnp.bfloat16
F32 = jnp.float32
ROOT = math.sqrt(2.0 / math.pi)
CUBE = 0.044715
FACES = 8
TILES = 32
VMEM = pl.BlockSpec(memory_space=pltpu.VMEM)
SMEM = pl.BlockSpec(memory_space=pltpu.SMEM)
ANY = pl.BlockSpec(memory_space=pl.ANY)


def place():
    return lax.axis_index("face"), lax.axis_index("tile")


def remote(src, dst, send, recv, face, tile):
    return pltpu.make_async_remote_copy(
        src_ref=src, dst_ref=dst, send_sem=send, recv_sem=recv,
        device_id=(face, tile), device_id_type=MESH,
    )


def nt(left, right):
    return lax.dot_general(left, right, (((1,), (1,)), ((), ())), preferred_element_type=F32)


def nn(left, right):
    return lax.dot_general(left, right, (((1,), (0,)), ((), ())), preferred_element_type=F32)


def one_hot(rows, cols, index):
    r = lax.broadcasted_iota(jnp.int32, (rows, cols), 0)
    c = lax.broadcasted_iota(jnp.int32, (rows, cols), 1)
    return jnp.where(c == index(r), 1.0, 0.0).astype(BF)


def fold(v):
    rows, chans = v.shape
    return jnp.sum(v.reshape(rows // 8, 8, chans), 0)


def main_kernel(
    factor,
    nbr_hbm, x_hbm, cot_hbm, kern_hbm, cb_hbm, gain_hbm, nb_hbm, we_hbm, be_hbm, wr_hbm, br_hbm, ls_hbm,
    out_hbm, gath, sgath,
    nbr, x, cot, kern, cb, gain, nb, we, be, wr, br, ls, out,
    top, bot, hbuf, side, pieces, chosen, nsbuf, nsend,
    pad, conv, taps, act, acc_e, acc_r, sums, ksum,
    big, slots1, slotsz, fin, small, sslots1, sslots2, few_ref, sfin,
    load_sem, out_sem, row_send, row_recv, side_send, side_recv, sem,
):
    f, t = place()
    last = TILES - 1
    mirror = last - t
    is_first = t == 0
    is_last = t == last
    has_up = t > 0
    has_down = t < last
    mir_up = jnp.logical_and(mirror < last, mirror + 1 != t)
    mir_down = jnp.logical_and(mirror > 0, mirror - 1 != t)
    edge = jnp.logical_or(is_first, is_last)
    hi = t // 16
    s = t % 16
    z = s // 2
    core = s % 2
    a = hi * 8 + f
    me = a * 2 + core
    others = [lax.rem(f + k, FACES) for k in range(1, FACES)]
    plane = [lax.rem(a + k, 16) for k in range(1, 16)]
    near = [lax.rem(me + k, 32) for k in range(1, 32)]
    line = [lax.rem(s + k, 16) for k in range(1, 16)]
    stack = [lax.rem(z + k, 8) for k in range(1, 8)]

    def plane_id(p):
        return lax.rem(p, 8), p // 8 * 16 + s

    def near_id(q):
        return lax.rem(q // 2, 8), q // 16 * 16 + z * 2 + q % 2

    def drain(ref, which):
        pltpu.make_async_copy(ref, ref, sem.at[which]).wait()

    loads = [
        pltpu.make_async_copy(src, dst, load_sem.at[i])
        for i, (src, dst) in enumerate(
            (
                (x_hbm, x), (kern_hbm, kern), (cb_hbm, cb), (cot_hbm, cot), (we_hbm, we), (wr_hbm, wr),
                (nbr_hbm, nbr), (gain_hbm, gain), (nb_hbm, nb), (be_hbm, be), (br_hbm, br), (ls_hbm, ls),
            )
        )
    ]
    for load in loads:
        load.start()

    barrier = pltpu.get_barrier_semaphore()

    def hello(face, tile):
        pl.semaphore_signal(barrier, inc=1, device_id=(face, tile), device_id_type=MESH)

    for q in near:
        hello(*near_id(q))
    for p in line:
        hello(f, hi * 16 + p)
    hello(f, mirror)

    @pl.when(has_up)
    def _():
        hello(f, t - 1)

    @pl.when(has_down)
    def _():
        hello(f, t + 1)

    @pl.when(mir_up)
    def _():
        hello(f, mirror + 1)

    @pl.when(mir_down)
    def _():
        hello(f, mirror - 1)

    @pl.when(edge)
    def _():
        for g in range(FACES):
            hello(g, mirror)

    loads[0].wait()
    for d in range(3):
        west = x[:, d : d + 1, :].astype(F32).reshape(8, 128)
        east = x[:, 255 - d : 256 - d, :].astype(F32).reshape(8, 128)
        pieces[f, d] = jnp.concatenate([west, east], 0).astype(BF)
    pad[3:11, 8:264, :] = x[...].astype(F32)
    for load in loads[1:3]:
        load.wait()
    for i in range(7):
        for j in range(7):
            taps[i * 7 + j] = jnp.broadcast_to(kern[i, j : j + 1, :], (8, 128))
    bias = jnp.broadcast_to(cb[...].reshape(1, 128), (8, 128))

    def convolve(col, acc, out_rows, in_rows):
        acc = dict(zip(out_rows, acc))
        for j in range(7):
            for row in in_rows:
                hit = [r for r in out_rows if 0 <= row - r < 7]
                if hit:
                    v = pad[row, pl.ds(col + 5 + j, 8), :]
                    for r in hit:
                        acc[r] = acc[r] + taps[(row - r) * 7 + j] * v
        return [acc[r] for r in out_rows]

    @pl.loop(0, 7)
    def _(i):
        for u in range(4):
            col = pl.multiple_of(16 + i * 32 + u * 8, 8)
            for r, v in enumerate(convolve(col, [bias] * 8, range(8), range(3, 11))):
                conv[r, pl.ds(col, 8), :] = v

    one = lambda cond: cond.astype(jnp.int32)
    count = 47 + one(has_up) + one(has_down) + one(mir_up) + one(mir_down) + 8 * one(edge)
    pl.semaphore_wait(barrier, count)

    def band_copy(rows, k, g):
        return remote(
            x.at[pl.ds(rows, 3), pl.ds(pl.multiple_of(g * 32, 32), 32), :], nsbuf.at[f],
            sem.at[0], sem.at[1], g, t,
        )

    def piece_copy(k, g):
        return remote(pieces.at[f], pieces.at[f], sem.at[2], sem.at[3], g, t)

    def up_copy():
        return remote(x.at[pl.ds(0, 3)], bot, row_send.at[0], row_recv.at[0], f, t - 1)

    def down_copy():
        return remote(x.at[pl.ds(5, 3)], top, row_send.at[1], row_recv.at[1], f, t + 1)

    for rows, cond in ((0, is_first), (5, is_last)):

        @pl.when(cond)
        def _(rows=rows):
            for k, g in enumerate(others):
                band_copy(rows, k, g).start()
            nsbuf[f] = x[rows : rows + 3, pl.ds(pl.multiple_of(f * 32, 32), 32), :]

    for k, g in enumerate(others):
        piece_copy(k, g).start()

    @pl.when(has_up)
    def _():
        up_copy().start()

    @pl.when(has_down)
    def _():
        down_copy().start()

    for load in loads[3:]:
        load.wait()

    def forward(g):
        return remote(nsend.at[g], hbuf.at[f], sem.at[4], sem.at[5], g, mirror)

    def side_copy(slot, tile):
        return remote(chosen, side.at[slot], side_send.at[slot], side_recv.at[slot], f, tile)

    def phase_two():
        for side_id, rows, cond in ((0, 5, is_last), (2, 0, is_first)):

            @pl.when(cond)
            def _(side_id=side_id, rows=rows):
                drain(nsbuf.at[pl.ds(0, 7)], 1)
                for g in range(FACES):
                    nsend[g] = nsbuf[nbr[0, side_id, g]]
                    forward(g).start()

        drain(pieces.at[pl.ds(0, 7)], 3)
        from_west = pieces[nbr[0, 3, f]]
        from_east = pieces[nbr[0, 1, f]]
        chosen[...] = jnp.concatenate(
            [from_west.astype(F32)[:, 8:16], from_east.astype(F32)[:, 0:8]], 1
        ).astype(BF)
        side_copy(4, mirror).start()

        @pl.when(has_down)
        def _():
            side_copy(0, t + 1).start()

        @pl.when(has_up)
        def _():
            side_copy(2, t - 1).start()

        @pl.when(mir_up)
        def _():
            side_copy(3, mirror + 1).start()

        @pl.when(mir_down)
        def _():
            side_copy(5, mirror - 1).start()

        side[1] = chosen[...]

        @pl.when(mirror + 1 == t)
        def _():
            side[3] = chosen[...]

        @pl.when(mirror - 1 == t)
        def _():
            side[5] = chosen[...]

    def polar(flag, rows):
        drain(hbuf, 5)
        turn = one_hot(256, 256, lambda r: 255 - r)
        for d in range(3):
            band = jnp.concatenate([hbuf[k, d] for k in range(8)], 0)
            turned = nn(turn, band)
            pad[rows[d], 8:264, :] = jnp.where(flag == 1, turned, band.astype(F32))

    def finish(out_rows, in_rows):
        @pl.loop(0, 7)
        def _(i):
            for u in range(4):
                col = pl.multiple_of(16 + i * 32 + u * 8, 8)
                acc = [conv[r, pl.ds(col, 8), :] for r in out_rows]
                for r, v in zip(out_rows, convolve(col, acc, out_rows, in_rows)):
                    conv[r, pl.ds(col, 8), :] = v

    def finish_top():
        @pl.when(has_up)
        def _():
            down_copy().wait_recv()
            pad[0:3, 8:264, :] = top[...].astype(F32)

        @pl.when(is_first)
        def _():
            polar(nbr[2, 0, f], (0, 1, 2))

        finish(range(0, 3), range(0, 3))

    def finish_bottom():
        @pl.when(has_down)
        def _():
            up_copy().wait_recv()
            pad[11:14, 8:264, :] = bot[...].astype(F32)

        @pl.when(is_last)
        def _():
            polar(nbr[2, 2, f], (11, 12, 13))

        finish(range(5, 8), range(11, 14))

    acc_e[...] = jnp.zeros_like(acc_e)
    acc_r[...] = jnp.zeros_like(acc_r)
    sums[...] = jnp.zeros_like(sums)
    mean_of = jnp.full((128, 128), 1.0 / 128, BF)
    vec = lambda ref: ref[...].reshape(1, -1)

    def mlp(c, cotangent, rows):
        count = c.shape[0]
        centred = c - nn(c.astype(BF), mean_of)
        variance = nn((centred * centred).astype(BF), mean_of)
        inverse = lax.rsqrt(variance + EPS)
        normed = centred * inverse
        scaled = (normed * vec(gain) + vec(nb)).astype(BF)
        branch_cot = (cotangent.astype(F32) * vec(ls)).astype(BF)
        hidden = nn(scaled, we[...]) + vec(be)
        active_cot = nt(branch_cot, wr[...])
        square = hidden * hidden
        gate = 0.5 + 0.5 * jnp.tanh(hidden * (ROOT + (ROOT * CUBE) * square))
        active = hidden * gate
        active_low = active.astype(BF)
        slope = gate + active * (1.0 - gate) * (2.0 * ROOT + (6.0 * ROOT * CUBE) * square)
        hidden_cot = (active_cot * slope).astype(BF)
        act[rows, :] = active_low
        left = jnp.concatenate([scaled.T, jnp.ones((16, count), BF)], 0)
        acc_e[...] += nn(left, hidden_cot)
        acc_r[...] += nn(branch_cot.T, active_low)
        scaled_cot = nt(hidden_cot, we[...])
        normed_cot = scaled_cot * vec(gain)
        m1 = nn(normed_cot.astype(BF), mean_of)
        m2 = nn((normed_cot * normed).astype(BF), mean_of)
        conv_cot = inverse * (normed_cot - m1 - normed * m2)
        sums[0] += fold(conv_cot)
        sums[1] += fold(scaled_cot * normed)
        sums[2] += fold(scaled_cot)
        sums[3] += fold(branch_cot.astype(F32))
        return conv_cot

    def kernel_grad(base, rows, cols):
        steps = len(cols) // 4

        @pl.loop(0, 7)
        def _(j):
            def step(k, acc):
                acc = list(acc)
                for u in range(4):
                    col = cols[u] if steps == 1 else pl.multiple_of(cols[0] + k * 32 + u * 8, 8)
                    cots = [conv[base + r, pl.ds(col, 8), :] for r in range(rows)]
                    for row in range(rows + 6):
                        v = pad[base + row, pl.ds(col + 5 + j, 8), :]
                        for i in range(7):
                            if 0 <= row - i < rows:
                                acc[i] = acc[i] + cots[row - i] * v
                return tuple(acc)

            zero = (jnp.zeros((8, 128), F32),) * 7
            acc = step(0, zero) if steps == 1 else lax.fori_loop(0, steps, step, zero)
            for i in range(7):
                ksum[i * 7 + j] += acc[i]

    inner = range(16, 240, 8)
    low_first = t < 16
    base1 = jnp.where(low_first, 5, 0)
    base2 = 5 - base1
    mid, three1, three2 = pl.ds(3, 2), pl.ds(base1, 3), pl.ds(base2, 3)

    def inside(ref, rows, count):
        return ref[rows, 16:240, :].reshape(count * 224, 128)

    def outside(ref):
        return jnp.concatenate([ref[:, 0:16, :], ref[:, 240:256, :]], 1).reshape(256, 128)

    got = mlp(inside(conv, mid, 2), inside(cot, mid, 2), pl.ds(0, 448))
    conv[mid, 16:240, :] = got.reshape(2, 224, 128)
    ksum[...] = jnp.zeros_like(ksum)
    kernel_grad(3, 2, inner)
    phase_two()

    @pl.when(low_first)
    def _():
        finish_bottom()

    @pl.when(jnp.logical_not(low_first))
    def _():
        finish_top()

    got = mlp(inside(conv, three1, 3), inside(cot, three1, 3), pl.ds(448, 672))
    conv[three1, 16:240, :] = got.reshape(3, 224, 128)
    kernel_grad(base1, 3, inner)

    @pl.when(low_first)
    def _():
        finish_top()

    @pl.when(jnp.logical_not(low_first))
    def _():
        finish_bottom()

    side_copy(4, mirror).wait_recv()

    @pl.when(has_up)
    def _():
        side_copy(0, t - 1).wait_recv()

    @pl.when(has_down)
    def _():
        side_copy(2, t + 1).wait_recv()

    @pl.when(mir_up)
    def _():
        side_copy(3, mirror + 1).wait_recv()

    @pl.when(mir_down)
    def _():
        side_copy(5, mirror - 1).wait_recv()

    @pl.when(is_first)
    def _():
        side[0] = jnp.zeros((3, 16, 128), BF)
        side[3] = jnp.zeros((3, 16, 128), BF)

    @pl.when(is_last)
    def _():
        side[2] = jnp.zeros((3, 16, 128), BF)
        side[5] = jnp.zeros((3, 16, 128), BF)

    turn = one_hot(24, 24, lambda r: r // 8 * 8 + 7 - r % 8)
    for d in range(3):
        slots = [side[i, d].astype(F32) for i in range(6)]
        for first, side_id, col in ((0, 3, 7 - d), (8, 1, 264 + d)):
            straight = jnp.concatenate([slots[i][first : first + 8] for i in (0, 1, 2)], 0)
            turned = jnp.concatenate([slots[i][first : first + 8] for i in (3, 4, 5)], 0)
            turned = nn(turn, turned.astype(BF))
            halo = jnp.where(nbr[2, side_id, f] == 1, turned, straight)
            pad[0:14, col : col + 1, :] = halo[5:19].reshape(14, 1, 128)

    for col in (0, 8, 240, 248):
        for r, v in enumerate(convolve(col, [bias] * 8, range(8), range(14))):
            conv[r, pl.ds(col, 8), :] = v

    got = mlp(
        jnp.concatenate([inside(conv, three2, 3), outside(conv)], 0),
        jnp.concatenate([inside(cot, three2, 3), outside(cot)], 0),
        pl.ds(1120, 928),
    )
    conv[three2, 16:240, :] = got[0:672].reshape(3, 224, 128)
    ends = got[672:928].reshape(8, 32, 128)
    conv[:, 0:16, :] = ends[:, 0:16]
    conv[:, 240:256, :] = ends[:, 16:32]

    scale = jnp.zeros((8, 128), F32)
    for q in range(4):
        cols = slice(q * 128, q * 128 + 128)
        big[q * 4 : q * 4 + 4] = acc_e[0:128, cols].astype(BF).reshape(4, 32, 128)
        turned = acc_r[:, cols].T
        big[16 + q * 4 : 20 + q * 4] = turned.astype(BF).reshape(4, 32, 128)
        scale = scale + fold(turned * wr[cols, :].astype(F32))

    for q in near:
        remote(big.at[q], slots1.at[me], sem.at[6], sem.at[7], *near_id(q)).start()
    slots1[me] = big[me]

    small[...] = jnp.zeros_like(small)
    totals = [jnp.sum(sums[i], 0, keepdims=True) for i in range(4)]
    totals.append((jnp.sum(scale, 0, keepdims=True) + vec(br) * totals[3]) / vec(ls))
    for i in range(5):
        small[49 + i : 50 + i, :] = totals[i]
    for q in range(4):
        small[54 + q : 55 + q, :] = acc_e[128:129, q * 128 : q * 128 + 128]

    kernel_grad(base2, 3, inner)
    kernel_grad(0, 8, (0, 8, 240, 248))
    for i in range(49):
        small[i : i + 1, :] = jnp.sum(ksum[i], 0, keepdims=True)

    for p in plane:
        rows = pl.ds(pl.multiple_of(lax.rem(p, 8) * 8, 8), 8)
        remote(small.at[rows], sslots1.at[a], sem.at[8], sem.at[9], *plane_id(p)).start()
    sslots1[a] = small[pl.ds(pl.multiple_of(f * 8, 8), 8), :]

    def output(rows, residual):
        branch = nn(act[rows, :], wr[...]) + vec(br)
        return (residual.astype(F32) + vec(ls) * branch).astype(BF)

    def output_inside(rows, three, count):
        out[three, 16:240, :] = output(rows, inside(x, three, count)).reshape(count, 224, 128)

    output_inside(pl.ds(0, 448), mid, 2)
    output_inside(pl.ds(448, 672), three1, 3)

    drain(slots1.at[pl.ds(0, 31)], 7)
    total = slots1[0].astype(F32)
    for q in range(1, 32):
        total = total + slots1[q].astype(F32)
    slotsz[z] = total.astype(BF)
    for q in stack:
        remote(
            slotsz.at[z], slotsz.at[z], sem.at[10], sem.at[11], f, hi * 16 + q * 2 + core
        ).start()

    output_inside(pl.ds(1120, 672), three2, 3)
    ends = output(pl.ds(1792, 256), outside(x)).reshape(8, 32, 128)
    out[:, 0:16, :] = ends[:, 0:16]
    out[:, 240:256, :] = ends[:, 16:32]
    store = pltpu.make_async_copy(out, out_hbm, out_sem.at[0])
    store.start()

    drain(sslots1.at[pl.ds(0, 15)], 9)
    few = sslots1[0]
    for p in range(1, 16):
        few = few + sslots1[p]
    few_ref[...] = few
    for p in line:
        remote(few_ref, sslots2.at[s], sem.at[12], sem.at[13], f, hi * 16 + p).start()
    sslots2[s] = few

    drain(slotsz.at[pl.ds(0, 7)], 11)
    total = slotsz[0].astype(F32)
    for q in range(1, 8):
        total = total + slotsz[q].astype(F32)
    fin[...] = (total * factor).astype(BF)
    for q in near:
        remote(fin, gath.at[me], sem.at[14], sem.at[15], *near_id(q)).start()
    own = pltpu.make_async_copy(fin, gath.at[me], out_sem.at[1])
    own.start()

    drain(sslots2.at[pl.ds(0, 15)], 13)
    few = sslots2[0]
    for p in range(1, 16):
        few = few + sslots2[p]
    sfin[...] = few * factor
    for g in others:
        remote(sfin, sgath.at[f], sem.at[16], sem.at[17], g, t).start()
    own_small = pltpu.make_async_copy(sfin, sgath.at[f], out_sem.at[2])
    own_small.start()
    drain(sgath.at[pl.ds(0, 7)], 17)
    drain(gath.at[pl.ds(0, 31)], 15)

    store.wait()
    own.wait()
    own_small.wait()
    side_copy(4, mirror).wait_send()

    @pl.when(has_up)
    def _():
        side_copy(2, t - 1).wait_send()
        up_copy().wait_send()

    @pl.when(has_down)
    def _():
        side_copy(0, t + 1).wait_send()
        down_copy().wait_send()

    @pl.when(mir_up)
    def _():
        side_copy(3, mirror + 1).wait_send()

    @pl.when(mir_down)
    def _():
        side_copy(5, mirror - 1).wait_send()

    @pl.when(edge)
    def _():
        drain(nsbuf.at[pl.ds(0, 7)], 0)
        drain(hbuf, 4)

    drain(pieces.at[pl.ds(0, 7)], 2)
    drain(slots1.at[pl.ds(0, 31)], 6)
    drain(sslots1.at[pl.ds(0, 15)], 8)
    drain(slotsz.at[pl.ds(0, 7)], 10)
    drain(sslots2.at[pl.ds(0, 15)], 12)
    drain(gath.at[pl.ds(0, 31)], 14)
    drain(sgath.at[pl.ds(0, 7)], 16)


def run_main(factor, neighbours, *operands):
    dma = pltpu.SemaphoreType.DMA
    shape = lambda *dims: jax.ShapeDtypeStruct(dims, BF)
    return pl.pallas_call(
        functools.partial(main_kernel, factor),
        out_shape=(
            shape(8, 256, 128),
            shape(32, 32, 128),
            jax.ShapeDtypeStruct((8, 8, 128), F32),
        ),
        in_specs=[ANY] * 12,
        out_specs=(ANY, ANY, ANY),
        scratch_shapes=[pltpu.SMEM(neighbours.shape, jnp.int32)]
        + [pltpu.VMEM(item.shape, item.dtype) for item in operands]
        + [
            pltpu.VMEM((8, 256, 128), BF),
            pltpu.VMEM((3, 256, 128), BF),
            pltpu.VMEM((3, 256, 128), BF),
            pltpu.VMEM((8, 3, 32, 128), BF),
            pltpu.VMEM((6, 3, 16, 128), BF),
            pltpu.VMEM((8, 3, 16, 128), BF),
            pltpu.VMEM((3, 16, 128), BF),
            pltpu.VMEM((8, 3, 32, 128), BF),
            pltpu.VMEM((8, 3, 32, 128), BF),
            pltpu.VMEM((14, 272, 128), F32),
            pltpu.VMEM((8, 256, 128), F32),
            pltpu.VMEM((49, 8, 128), F32),
            pltpu.VMEM((2048, 512), BF),
            pltpu.VMEM((144, 512), F32),
            pltpu.VMEM((128, 512), F32),
            pltpu.VMEM((4, 8, 128), F32),
            pltpu.VMEM((49, 8, 128), F32),
            pltpu.VMEM((32, 32, 128), BF),
            pltpu.VMEM((32, 32, 128), BF),
            pltpu.VMEM((8, 32, 128), BF),
            pltpu.VMEM((32, 128), BF),
            pltpu.VMEM((64, 128), F32),
            pltpu.VMEM((16, 8, 128), F32),
            pltpu.VMEM((16, 8, 128), F32),
            pltpu.VMEM((8, 128), F32),
            pltpu.VMEM((8, 128), F32),
            dma((12,)), dma((3,)), dma((2,)), dma((2,)), dma((6,)), dma((6,)), dma((18,)),
        ],
        compiler_params=pltpu.CompilerParams(
            collective_id=0, has_side_effects=True, vmem_limit_bytes=56 * 1024 * 1024
        ),
        name="main",
    )(neighbours, *operands)


def unpack_kernel(
    raw, gath, sgath,
    out, kernel_grad, cb_grad, gain_grad, nb_grad, we_grad, be_grad, wr_grad, br_grad, ls_grad,
    stage, rows_in, few_in, sem,
):
    fetches = [
        pltpu.make_async_copy(src, dst, sem.at[i])
        for i, (src, dst) in enumerate(((raw, stage), (gath, rows_in), (sgath, few_in)))
    ]
    for fetch in fetches:
        fetch.start()
    store = pltpu.make_async_copy(stage, out, sem.at[3])
    fetches[0].wait()
    store.start()
    fetches[1].wait()
    fetches[2].wait()
    rows = rows_in.reshape(1024, 128)
    few = few_in[...].reshape(64, 128)
    for q in range(4):
        we_grad[:, q * 128 : q * 128 + 128] = rows[q * 128 : q * 128 + 128, :].astype(F32)
        be_grad[q * 128 : q * 128 + 128] = few[54 + q]
    wr_grad[...] = rows[512:1024, :].astype(F32)
    for i in range(7):
        kernel_grad[i] = few[i * 7 : i * 7 + 7]
    for i, ref in enumerate((cb_grad, gain_grad, nb_grad, br_grad, ls_grad)):
        ref[...] = few[49 + i]
    store.wait()


def unpack(raw, gath, sgath):
    one = lambda *shape: jax.ShapeDtypeStruct(shape, F32)
    return pl.pallas_call(
        unpack_kernel,
        out_shape=(
            jax.ShapeDtypeStruct(raw.shape, raw.dtype),
            one(7, 7, 128), one(128), one(128), one(128), one(128, 512), one(512),
            one(512, 128), one(128), one(128),
        ),
        in_specs=[ANY, ANY, ANY],
        out_specs=(ANY,) + (VMEM,) * 9,
        scratch_shapes=[
            pltpu.VMEM(raw.shape, raw.dtype),
            pltpu.VMEM(gath.shape, gath.dtype),
            pltpu.VMEM(sgath.shape, sgath.dtype),
            pltpu.SemaphoreType.DMA((4,)),
        ],
        compiler_params=pltpu.CompilerParams(vmem_limit_bytes=56 * 1024 * 1024),
        name="unpack",
    )(raw, gath, sgath)


def body(
    inputs, kernel, conv_bias, norm_gain, norm_bias, expand_weight, expand_bias,
    reduce_weight, reduce_bias, layer_scale, neighbours, cotangent,
):
    factor = 1.0 / math.sqrt(FACES * 256 * 256)
    raw, gath, sgath = run_main(
        factor, jnp.transpose(neighbours, (2, 1, 0)), inputs[0], cotangent[0], kernel, conv_bias, norm_gain, norm_bias,
        expand_weight, expand_bias, reduce_weight, reduce_bias, layer_scale,
    )
    out, *grads = unpack(raw, gath, sgath)
    return (out[None], *grads)


def solution(mesh):
    split = P("face", "tile", None, None)
    return jax.shard_map(
        body,
        mesh=mesh,
        in_specs=(split,) + (P(),) * 10 + (split,),
        out_specs=(split,) + (P(),) * 9,
        check_vma=False,
    )
```

```python
import functools
import math

import jax
import jax.numpy as jnp
from jax import lax
from jax.experimental import pallas as pl
from jax.experimental.pallas import tpu as pltpu
from jax.sharding import PartitionSpec as P

EPS = 1e-06
MESH = pl.DeviceIdType.MESH
BF = jnp.bfloat16
F32 = jnp.float32
ROOT = math.sqrt(2.0 / math.pi)
CUBE = 0.044715
FACES = 8
TILES = 32
VMEM = pl.BlockSpec(memory_space=pltpu.VMEM)
SMEM = pl.BlockSpec(memory_space=pltpu.SMEM)
ANY = pl.BlockSpec(memory_space=pl.ANY)


def place():
    return lax.axis_index("face"), lax.axis_index("tile")


def remote(src, dst, send, recv, face, tile):
    return pltpu.make_async_remote_copy(
        src_ref=src, dst_ref=dst, send_sem=send, recv_sem=recv,
        device_id=(face, tile), device_id_type=MESH,
    )


def nt(left, right):
    return lax.dot_general(left, right, (((1,), (1,)), ((), ())), preferred_element_type=F32)


def nn(left, right):
    return lax.dot_general(left, right, (((1,), (0,)), ((), ())), preferred_element_type=F32)


def one_hot(rows, cols, index):
    r = lax.broadcasted_iota(jnp.int32, (rows, cols), 0)
    c = lax.broadcasted_iota(jnp.int32, (rows, cols), 1)
    return jnp.where(c == index(r), 1.0, 0.0).astype(BF)


def fold(v):
    rows, chans = v.shape
    return jnp.sum(v.reshape(rows // 8, 8, chans), 0)


def main_kernel(
    factor,
    nbr_hbm, x_hbm, cot_hbm, kern_hbm, cb_hbm, gain_hbm, nb_hbm, we_hbm, be_hbm, wr_hbm, br_hbm, ls_hbm,
    out_hbm, gath, sgath,
    nbr, x, cot, kern, cb, gain, nb, we, be, wr, br, ls, out,
    top, bot, hbuf, side, pieces, chosen, near_band, far_band, near_out, far_out,
    pad, conv, taps, act, acc_e, acc_r, sums, ksum,
    big, slots1, slotsz, fin, small, sslots1, sslots2, few_ref, sfin,
    load_sem, out_sem, row_send, row_recv, side_send, side_recv, sem,
):
    f, t = place()
    last = TILES - 1
    mirror = last - t
    is_first = t == 0
    is_last = t == last
    has_up = t > 0
    has_down = t < last
    mir_up = jnp.logical_and(mirror < last, mirror + 1 != t)
    mir_down = jnp.logical_and(mirror > 0, mirror - 1 != t)
    edge = jnp.logical_or(is_first, is_last)
    hi = t // 16
    s = t % 16
    z = s // 2
    core = s % 2
    a = hi * 8 + f
    me = a * 2 + core
    others = [lax.rem(f + k, FACES) for k in range(1, FACES)]
    plane = [lax.rem(a + k, 16) for k in range(1, 16)]
    near = [lax.rem(me + k, 32) for k in range(1, 32)]
    line = [lax.rem(s + k, 16) for k in range(1, 16)]
    stack = [lax.rem(z + k, 8) for k in range(1, 8)]

    def plane_id(p):
        return lax.rem(p, 8), p // 8 * 16 + s

    def near_id(q):
        return lax.rem(q // 2, 8), q // 16 * 16 + z * 2 + q % 2

    def drain(ref, which):
        pltpu.make_async_copy(ref, ref, sem.at[which]).wait()

    loads = [
        pltpu.make_async_copy(src, dst, load_sem.at[i])
        for i, (src, dst) in enumerate(
            (
                (x_hbm, x), (kern_hbm, kern), (cb_hbm, cb), (cot_hbm, cot), (we_hbm, we), (wr_hbm, wr),
                (nbr_hbm, nbr), (gain_hbm, gain), (nb_hbm, nb), (be_hbm, be), (br_hbm, br), (ls_hbm, ls),
            )
        )
    ]
    for load in loads:
        load.start()

    barrier = pltpu.get_barrier_semaphore()

    def hello(face, tile):
        pl.semaphore_signal(barrier, inc=1, device_id=(face, tile), device_id_type=MESH)

    @pl.when(edge)
    def _():
        for g in range(FACES):
            hello(g, mirror)

    for q in near:
        hello(*near_id(q))
    for p in line:
        hello(f, hi * 16 + p)
    hello(f, mirror)

    @pl.when(has_up)
    def _():
        hello(f, t - 1)

    @pl.when(has_down)
    def _():
        hello(f, t + 1)

    @pl.when(mir_up)
    def _():
        hello(f, mirror + 1)

    @pl.when(mir_down)
    def _():
        hello(f, mirror - 1)

    loads[0].wait()
    for d in range(3):
        west = x[:, d : d + 1, :].astype(F32).reshape(8, 128)
        east = x[:, 255 - d : 256 - d, :].astype(F32).reshape(8, 128)
        pieces[f, d] = jnp.concatenate([west, east], 0).astype(BF)
    pad[3:11, 8:264, :] = x[...].astype(F32)
    for load in loads[1:3]:
        load.wait()
    for i in range(7):
        for j in range(7):
            taps[i * 7 + j] = jnp.broadcast_to(kern[i, j : j + 1, :], (8, 128))
    bias = jnp.broadcast_to(cb[...].reshape(1, 128), (8, 128))

    def convolve(col, acc, out_rows, in_rows, base=0):
        acc = dict(zip(out_rows, acc))
        for j in range(7):
            for row in in_rows:
                hit = [r for r in out_rows if 0 <= row - r < 7]
                if hit:
                    v = pad[base + row, pl.ds(col + 5 + j, 8), :]
                    for r in hit:
                        acc[r] = acc[r] + taps[(row - r) * 7 + j] * v
        return [acc[r] for r in out_rows]

    @pl.loop(0, 7)
    def _(i):
        for u in range(4):
            col = pl.multiple_of(16 + i * 32 + u * 8, 8)
            for r, v in enumerate(convolve(col, [bias] * 8, range(8), range(3, 11))):
                conv[r, pl.ds(col, 8), :] = v

    one = lambda cond: cond.astype(jnp.int32)
    count = 47 + one(has_up) + one(has_down) + one(mir_up) + one(mir_down) + 8 * one(edge)
    pl.semaphore_wait(barrier, count)

    def columns(c):
        return pl.ds(pl.multiple_of(c * 16, 16), 16)

    def piece_copy(k, g):
        return remote(pieces.at[f], pieces.at[f], sem.at[2], sem.at[3], g, t)

    def up_copy():
        return remote(x.at[pl.ds(0, 3)], bot, row_send.at[0], row_recv.at[0], f, t - 1)

    def down_copy():
        return remote(x.at[pl.ds(5, 3)], top, row_send.at[1], row_recv.at[1], f, t + 1)

    for rows, cond in ((0, is_first), (5, is_last)):

        @pl.when(cond)
        def _(rows=rows):
            three = pl.ds(rows, 3)
            for g in others:
                remote(x.at[three, columns(g), :], near_band.at[f], sem.at[0], sem.at[1], g, t).start()
            for g in range(FACES):
                remote(
                    x.at[three, columns(g + 8), :], far_band.at[f], sem.at[18], sem.at[19], g, mirror
                ).start()
            near_band[f] = x[three, columns(f), :]

    @pl.when(has_up)
    def _():
        up_copy().start()

    @pl.when(has_down)
    def _():
        down_copy().start()

    for load in loads[3:]:
        load.wait()

    def side_copy(slot, tile):
        return remote(chosen, side.at[slot], side_send.at[slot], side_recv.at[slot], f, tile)

    def phase_two():
        for near_side, far_side, cond in ((0, 2, is_last), (2, 0, is_first)):

            @pl.when(cond)
            def _(near_side=near_side, far_side=far_side):
                drain(near_band.at[pl.ds(0, 7)], 1)
                for g in range(FACES):
                    near_out[g] = near_band[nbr[0, near_side, g]]
                    remote(near_out.at[g], hbuf.at[f], sem.at[4], sem.at[5], g, mirror).start()
                drain(far_band, 19)
                for k, g in enumerate(others):
                    far_out[k] = far_band[nbr[0, far_side, g]]
                    remote(far_out.at[k], hbuf.at[f + 8], sem.at[4], sem.at[5], g, t).start()
                hbuf[f + 8] = far_band[nbr[0, far_side, f]]

        drain(pieces.at[pl.ds(0, 7)], 3)
        from_west = pieces[nbr[0, 3, f]]
        from_east = pieces[nbr[0, 1, f]]
        chosen[...] = jnp.concatenate(
            [from_west.astype(F32)[:, 8:16], from_east.astype(F32)[:, 0:8]], 1
        ).astype(BF)
        side_copy(4, mirror).start()

        @pl.when(has_down)
        def _():
            side_copy(0, t + 1).start()

        @pl.when(has_up)
        def _():
            side_copy(2, t - 1).start()

        @pl.when(mir_up)
        def _():
            side_copy(3, mirror + 1).start()

        @pl.when(mir_down)
        def _():
            side_copy(5, mirror - 1).start()

        side[1] = chosen[...]

        @pl.when(mirror + 1 == t)
        def _():
            side[3] = chosen[...]

        @pl.when(mirror - 1 == t)
        def _():
            side[5] = chosen[...]

    def polar(flag, rows):
        drain(hbuf.at[pl.ds(0, 15)], 5)
        turn = one_hot(256, 256, lambda r: 255 - r)
        for d in range(3):
            band = jnp.concatenate([hbuf[k, d] for k in range(16)], 0)
            turned = nn(turn, band)
            pad[rows[d], 8:264, :] = jnp.where(flag == 1, turned, band.astype(F32))

    def finish(out_rows, in_rows):
        @pl.loop(0, 7)
        def _(i):
            for u in range(4):
                col = pl.multiple_of(16 + i * 32 + u * 8, 8)
                acc = [conv[r, pl.ds(col, 8), :] for r in out_rows]
                for r, v in zip(out_rows, convolve(col, acc, out_rows, in_rows)):
                    conv[r, pl.ds(col, 8), :] = v

    def finish_top():
        @pl.when(has_up)
        def _():
            down_copy().wait_recv()
            pad[0:3, 8:264, :] = top[...].astype(F32)

        @pl.when(is_first)
        def _():
            polar(nbr[2, 0, f], (0, 1, 2))

        finish(range(0, 3), range(0, 3))

    def finish_bottom():
        @pl.when(has_down)
        def _():
            up_copy().wait_recv()
            pad[11:14, 8:264, :] = bot[...].astype(F32)

        @pl.when(is_last)
        def _():
            polar(nbr[2, 2, f], (11, 12, 13))

        finish(range(5, 8), range(11, 14))

    acc_e[...] = jnp.zeros_like(acc_e)
    acc_r[...] = jnp.zeros_like(acc_r)
    sums[...] = jnp.zeros_like(sums)
    mean_of = jnp.full((128, 128), 1.0 / 128, BF)
    vec = lambda ref: ref[...].reshape(1, -1)

    def mlp(c, cotangent, rows, between=None):
        count = c.shape[0]
        centred = c - nn(c.astype(BF), mean_of)
        variance = nn((centred * centred).astype(BF), mean_of)
        inverse = lax.rsqrt(variance + EPS)
        normed = centred * inverse
        scaled = (normed * vec(gain) + vec(nb)).astype(BF)
        branch_cot = (cotangent.astype(F32) * vec(ls)).astype(BF)
        hidden = nn(scaled, we[...]) + vec(be)
        active_cot = nt(branch_cot, wr[...])
        square = hidden * hidden
        gate = 0.5 + 0.5 * jnp.tanh(hidden * (ROOT + (ROOT * CUBE) * square))
        active = hidden * gate
        active_low = active.astype(BF)
        slope = gate + active * (1.0 - gate) * (2.0 * ROOT + (6.0 * ROOT * CUBE) * square)
        hidden_cot = (active_cot * slope).astype(BF)
        act[rows, :] = active_low
        left = jnp.concatenate([scaled.T, jnp.ones((16, count), BF)], 0)
        acc_e[...] += nn(left, hidden_cot)
        acc_r[...] += nn(branch_cot.T, active_low)
        if between is not None:
            between()
        scaled_cot = nt(hidden_cot, we[...])
        normed_cot = scaled_cot * vec(gain)
        m1 = nn(normed_cot.astype(BF), mean_of)
        m2 = nn((normed_cot * normed).astype(BF), mean_of)
        conv_cot = inverse * (normed_cot - m1 - normed * m2)
        sums[0] += fold(conv_cot)
        sums[1] += fold(scaled_cot * normed)
        sums[2] += fold(scaled_cot)
        sums[3] += fold(branch_cot.astype(F32))
        return conv_cot

    def kernel_grad(base, rows, cols):
        steps = len(cols) // 4

        @pl.loop(0, 7)
        def _(j):
            def step(k, acc):
                acc = list(acc)
                for u in range(4):
                    col = cols[u] if steps == 1 else pl.multiple_of(cols[0] + k * 32 + u * 8, 8)
                    cots = [conv[base + r, pl.ds(col, 8), :] for r in range(rows)]
                    for row in range(rows + 6):
                        v = pad[base + row, pl.ds(col + 5 + j, 8), :]
                        for i in range(7):
                            if 0 <= row - i < rows:
                                acc[i] = acc[i] + cots[row - i] * v
                return tuple(acc)

            zero = (jnp.zeros((8, 128), F32),) * 7
            acc = step(0, zero) if steps == 1 else lax.fori_loop(0, steps, step, zero)
            for i in range(7):
                ksum[i * 7 + j] += acc[i]

    inner = range(16, 240, 8)
    low_first = t < 16
    base1 = jnp.where(low_first, 5, 0)
    base2 = 5 - base1
    base5 = jnp.where(low_first, 3, 0)
    mid, three1, three2 = pl.ds(3, 2), pl.ds(base1, 3), pl.ds(base2, 3)
    five = pl.ds(base5, 5)

    def inside(ref, rows, count):
        return ref[rows, 16:240, :].reshape(count * 224, 128)

    def outside(ref):
        return jnp.concatenate([ref[five, 0:16, :], ref[five, 240:256, :]], 1).reshape(160, 128)

    got = mlp(inside(conv, mid, 2), inside(cot, mid, 2), pl.ds(0, 448))
    conv[mid, 16:240, :] = got.reshape(2, 224, 128)
    for k, g in enumerate(others):
        piece_copy(k, g).start()
    ksum[...] = jnp.zeros_like(ksum)
    kernel_grad(3, 2, inner)
    phase_two()

    @pl.when(low_first)
    def _():
        finish_bottom()

    @pl.when(jnp.logical_not(low_first))
    def _():
        finish_top()

    got = mlp(inside(conv, three1, 3), inside(cot, three1, 3), pl.ds(448, 672))
    conv[three1, 16:240, :] = got.reshape(3, 224, 128)
    kernel_grad(base1, 3, inner)

    side_copy(4, mirror).wait_recv()

    @pl.when(has_up)
    def _():
        side_copy(0, t - 1).wait_recv()

    @pl.when(has_down)
    def _():
        side_copy(2, t + 1).wait_recv()

    @pl.when(mir_up)
    def _():
        side_copy(3, mirror + 1).wait_recv()

    @pl.when(mir_down)
    def _():
        side_copy(5, mirror - 1).wait_recv()

    @pl.when(is_first)
    def _():
        side[0] = jnp.zeros((3, 16, 128), BF)
        side[3] = jnp.zeros((3, 16, 128), BF)

    @pl.when(is_last)
    def _():
        side[2] = jnp.zeros((3, 16, 128), BF)
        side[5] = jnp.zeros((3, 16, 128), BF)

    turn = one_hot(24, 24, lambda r: r // 8 * 8 + 7 - r % 8)
    for d in range(3):
        slots = [side[i, d].astype(F32) for i in range(6)]
        for first, side_id, col in ((0, 3, 7 - d), (8, 1, 264 + d)):
            straight = jnp.concatenate([slots[i][first : first + 8] for i in (0, 1, 2)], 0)
            turned = jnp.concatenate([slots[i][first : first + 8] for i in (3, 4, 5)], 0)
            turned = nn(turn, turned.astype(BF))
            halo = jnp.where(nbr[2, side_id, f] == 1, turned, straight)
            pad[0:14, col : col + 1, :] = halo[5:19].reshape(14, 1, 128)

    ends = (0, 8, 240, 248)

    def convolve_ends(base, rows):
        for col in ends:
            got = convolve(col, [bias] * rows, range(rows), range(rows + 6), base)
            for r, v in enumerate(got):
                conv[base + r, pl.ds(col, 8), :] = v

    convolve_ends(base5, 5)
    got = mlp(outside(conv), outside(cot), pl.ds(1120, 160)).reshape(5, 32, 128)
    conv[five, 0:16, :] = got[:, 0:16]
    conv[five, 240:256, :] = got[:, 16:32]
    kernel_grad(base5, 5, ends)

    @pl.when(low_first)
    def _():
        finish_top()

    @pl.when(jnp.logical_not(low_first))
    def _():
        finish_bottom()

    convolve_ends(base2, 3)

    def send_large():
        for q in range(4):
            cols = slice(q * 128, q * 128 + 128)
            big[q * 4 : q * 4 + 4] = acc_e[0:128, cols].astype(BF).reshape(4, 32, 128)
            big[16 + q * 4 : 20 + q * 4] = acc_r[:, cols].T.astype(BF).reshape(4, 32, 128)
        for q in near:
            remote(big.at[q], slots1.at[me], sem.at[6], sem.at[7], *near_id(q)).start()

    got = mlp(
        conv[three2, :, :].reshape(768, 128), cot[three2, :, :].reshape(768, 128), pl.ds(1280, 768), send_large
    )
    conv[three2, :, :] = got.reshape(3, 256, 128)
    slots1[me] = big[me]

    scale = jnp.zeros((8, 128), F32)
    for q in range(4):
        cols = slice(q * 128, q * 128 + 128)
        scale = scale + fold(acc_r[:, cols].T * wr[cols, :].astype(F32))
    small[...] = jnp.zeros_like(small)
    totals = [jnp.sum(sums[i], 0, keepdims=True) for i in range(4)]
    totals.append((jnp.sum(scale, 0, keepdims=True) + vec(br) * totals[3]) / vec(ls))
    for i in range(5):
        small[49 + i : 50 + i, :] = totals[i]
    for q in range(4):
        small[54 + q : 55 + q, :] = acc_e[128:129, q * 128 : q * 128 + 128]

    kernel_grad(base2, 3, range(0, 256, 8))
    for i in range(49):
        small[i : i + 1, :] = jnp.sum(ksum[i], 0, keepdims=True)

    for p in plane:
        rows = pl.ds(pl.multiple_of(lax.rem(p, 8) * 8, 8), 8)
        remote(small.at[rows], sslots1.at[a], sem.at[8], sem.at[9], *plane_id(p)).start()
    sslots1[a] = small[pl.ds(pl.multiple_of(f * 8, 8), 8), :]

    def output(rows, residual):
        branch = nn(act[rows, :], wr[...]) + vec(br)
        return (residual.astype(F32) + vec(ls) * branch).astype(BF)

    def output_inside(rows, three, count):
        out[three, 16:240, :] = output(rows, inside(x, three, count)).reshape(count, 224, 128)

    output_inside(pl.ds(0, 448), mid, 2)
    output_inside(pl.ds(448, 672), three1, 3)

    drain(slots1.at[pl.ds(0, 31)], 7)
    total = slots1[0].astype(F32)
    for q in range(1, 32):
        total = total + slots1[q].astype(F32)
    slotsz[z] = total.astype(BF)
    for q in stack:
        remote(
            slotsz.at[z], slotsz.at[z], sem.at[10], sem.at[11], f, hi * 16 + q * 2 + core
        ).start()

    got = output(pl.ds(1120, 160), outside(x)).reshape(5, 32, 128)
    out[five, 0:16, :] = got[:, 0:16]
    out[five, 240:256, :] = got[:, 16:32]
    got = output(pl.ds(1280, 768), x[three2, :, :].reshape(768, 128))
    out[three2, :, :] = got.reshape(3, 256, 128)
    store = pltpu.make_async_copy(out, out_hbm, out_sem.at[0])
    store.start()

    drain(sslots1.at[pl.ds(0, 15)], 9)
    few = sslots1[0]
    for p in range(1, 16):
        few = few + sslots1[p]
    few_ref[...] = few
    for p in line:
        remote(few_ref, sslots2.at[s], sem.at[12], sem.at[13], f, hi * 16 + p).start()
    sslots2[s] = few

    drain(slotsz.at[pl.ds(0, 7)], 11)
    total = slotsz[0].astype(F32)
    for q in range(1, 8):
        total = total + slotsz[q].astype(F32)
    fin[...] = (total * factor).astype(BF)
    for q in near:
        remote(fin, gath.at[me], sem.at[14], sem.at[15], *near_id(q)).start()
    own = pltpu.make_async_copy(fin, gath.at[me], out_sem.at[1])
    own.start()

    drain(sslots2.at[pl.ds(0, 15)], 13)
    few = sslots2[0]
    for p in range(1, 16):
        few = few + sslots2[p]
    sfin[...] = few * factor
    for g in others:
        remote(sfin, sgath.at[f], sem.at[16], sem.at[17], g, t).start()
    own_small = pltpu.make_async_copy(sfin, sgath.at[f], out_sem.at[2])
    own_small.start()
    drain(sgath.at[pl.ds(0, 7)], 17)
    drain(gath.at[pl.ds(0, 31)], 15)

    store.wait()
    own.wait()
    own_small.wait()
    side_copy(4, mirror).wait_send()

    @pl.when(has_up)
    def _():
        side_copy(2, t - 1).wait_send()
        up_copy().wait_send()

    @pl.when(has_down)
    def _():
        side_copy(0, t + 1).wait_send()
        down_copy().wait_send()

    @pl.when(mir_up)
    def _():
        side_copy(3, mirror + 1).wait_send()

    @pl.when(mir_down)
    def _():
        side_copy(5, mirror - 1).wait_send()

    @pl.when(edge)
    def _():
        drain(near_band.at[pl.ds(0, 7)], 0)
        drain(far_band, 18)
        drain(hbuf.at[pl.ds(0, 15)], 4)

    drain(pieces.at[pl.ds(0, 7)], 2)
    drain(slots1.at[pl.ds(0, 31)], 6)
    drain(sslots1.at[pl.ds(0, 15)], 8)
    drain(slotsz.at[pl.ds(0, 7)], 10)
    drain(sslots2.at[pl.ds(0, 15)], 12)
    drain(gath.at[pl.ds(0, 31)], 14)
    drain(sgath.at[pl.ds(0, 7)], 16)


def run_main(factor, neighbours, *operands):
    dma = pltpu.SemaphoreType.DMA
    shape = lambda *dims: jax.ShapeDtypeStruct(dims, BF)
    return pl.pallas_call(
        functools.partial(main_kernel, factor),
        out_shape=(
            shape(8, 256, 128),
            shape(32, 32, 128),
            jax.ShapeDtypeStruct((8, 8, 128), F32),
        ),
        in_specs=[ANY] * 12,
        out_specs=(ANY, ANY, ANY),
        scratch_shapes=[pltpu.SMEM(neighbours.shape, jnp.int32)]
        + [pltpu.VMEM(item.shape, item.dtype) for item in operands]
        + [
            pltpu.VMEM((8, 256, 128), BF),
            pltpu.VMEM((3, 256, 128), BF),
            pltpu.VMEM((3, 256, 128), BF),
            pltpu.VMEM((16, 3, 16, 128), BF),
            pltpu.VMEM((6, 3, 16, 128), BF),
            pltpu.VMEM((8, 3, 16, 128), BF),
            pltpu.VMEM((3, 16, 128), BF),
            pltpu.VMEM((8, 3, 16, 128), BF),
            pltpu.VMEM((8, 3, 16, 128), BF),
            pltpu.VMEM((8, 3, 16, 128), BF),
            pltpu.VMEM((7, 3, 16, 128), BF),
            pltpu.VMEM((14, 272, 128), F32),
            pltpu.VMEM((8, 256, 128), F32),
            pltpu.VMEM((49, 8, 128), F32),
            pltpu.VMEM((2048, 512), BF),
            pltpu.VMEM((144, 512), F32),
            pltpu.VMEM((128, 512), F32),
            pltpu.VMEM((4, 8, 128), F32),
            pltpu.VMEM((49, 8, 128), F32),
            pltpu.VMEM((32, 32, 128), BF),
            pltpu.VMEM((32, 32, 128), BF),
            pltpu.VMEM((8, 32, 128), BF),
            pltpu.VMEM((32, 128), BF),
            pltpu.VMEM((64, 128), F32),
            pltpu.VMEM((16, 8, 128), F32),
            pltpu.VMEM((16, 8, 128), F32),
            pltpu.VMEM((8, 128), F32),
            pltpu.VMEM((8, 128), F32),
            dma((12,)), dma((3,)), dma((2,)), dma((2,)), dma((6,)), dma((6,)), dma((20,)),
        ],
        compiler_params=pltpu.CompilerParams(
            collective_id=0, has_side_effects=True, vmem_limit_bytes=56 * 1024 * 1024
        ),
        name="main",
    )(neighbours, *operands)


def unpack_kernel(
    raw, gath, sgath,
    out, kernel_grad, cb_grad, gain_grad, nb_grad, we_grad, be_grad, wr_grad, br_grad, ls_grad,
    stage, rows_in, few_in, sem,
):
    fetches = [
        pltpu.make_async_copy(src, dst, sem.at[i])
        for i, (src, dst) in enumerate(((raw, stage), (gath, rows_in), (sgath, few_in)))
    ]
    for fetch in fetches:
        fetch.start()
    store = pltpu.make_async_copy(stage, out, sem.at[3])
    fetches[0].wait()
    store.start()
    fetches[1].wait()
    fetches[2].wait()
    rows = rows_in.reshape(1024, 128)
    few = few_in[...].reshape(64, 128)
    for q in range(4):
        we_grad[:, q * 128 : q * 128 + 128] = rows[q * 128 : q * 128 + 128, :].astype(F32)
        be_grad[q * 128 : q * 128 + 128] = few[54 + q]
    wr_grad[...] = rows[512:1024, :].astype(F32)
    for i in range(7):
        kernel_grad[i] = few[i * 7 : i * 7 + 7]
    for i, ref in enumerate((cb_grad, gain_grad, nb_grad, br_grad, ls_grad)):
        ref[...] = few[49 + i]
    store.wait()


def unpack(raw, gath, sgath):
    one = lambda *shape: jax.ShapeDtypeStruct(shape, F32)
    return pl.pallas_call(
        unpack_kernel,
        out_shape=(
            jax.ShapeDtypeStruct(raw.shape, raw.dtype),
            one(7, 7, 128), one(128), one(128), one(128), one(128, 512), one(512),
            one(512, 128), one(128), one(128),
        ),
        in_specs=[ANY, ANY, ANY],
        out_specs=(ANY,) + (VMEM,) * 9,
        scratch_shapes=[
            pltpu.VMEM(raw.shape, raw.dtype),
            pltpu.VMEM(gath.shape, gath.dtype),
            pltpu.VMEM(sgath.shape, sgath.dtype),
            pltpu.SemaphoreType.DMA((4,)),
        ],
        compiler_params=pltpu.CompilerParams(vmem_limit_bytes=56 * 1024 * 1024),
        name="unpack",
    )(raw, gath, sgath)


def body(
    inputs, kernel, conv_bias, norm_gain, norm_bias, expand_weight, expand_bias,
    reduce_weight, reduce_bias, layer_scale, neighbours, cotangent,
):
    factor = 1.0 / math.sqrt(FACES * 256 * 256)
    raw, gath, sgath = run_main(
        factor, jnp.transpose(neighbours, (2, 1, 0)), inputs[0], cotangent[0], kernel, conv_bias, norm_gain, norm_bias,
        expand_weight, expand_bias, reduce_weight, reduce_bias, layer_scale,
    )
    out, *grads = unpack(raw, gath, sgath)
    return (out[None], *grads)


def solution(mesh):
    split = P("face", "tile", None, None)
    return jax.shard_map(
        body,
        mesh=mesh,
        in_specs=(split,) + (P(),) * 10 + (split,),
        out_specs=(split,) + (P(),) * 9,
        check_vma=False,
    )
```

```python
import functools
import math

import jax
import jax.numpy as jnp
from jax import lax
from jax.experimental import pallas as pl
from jax.experimental.pallas import tpu as pltpu
from jax.sharding import PartitionSpec as P

EPS = 1e-06
MESH = pl.DeviceIdType.MESH
BF = jnp.bfloat16
F32 = jnp.float32
ROOT = math.sqrt(2.0 / math.pi)
CUBE = 0.044715
FACES = 8
TILES = 32
VMEM = pl.BlockSpec(memory_space=pltpu.VMEM)
SMEM = pl.BlockSpec(memory_space=pltpu.SMEM)
ANY = pl.BlockSpec(memory_space=pl.ANY)


def place():
    return lax.axis_index("face"), lax.axis_index("tile")


def remote(src, dst, send, recv, face, tile):
    return pltpu.make_async_remote_copy(
        src_ref=src, dst_ref=dst, send_sem=send, recv_sem=recv,
        device_id=(face, tile), device_id_type=MESH,
    )


def nt(left, right):
    return lax.dot_general(left, right, (((1,), (1,)), ((), ())), preferred_element_type=F32)


def nn(left, right):
    return lax.dot_general(left, right, (((1,), (0,)), ((), ())), preferred_element_type=F32)


def one_hot(rows, cols, index):
    r = lax.broadcasted_iota(jnp.int32, (rows, cols), 0)
    c = lax.broadcasted_iota(jnp.int32, (rows, cols), 1)
    return jnp.where(c == index(r), 1.0, 0.0).astype(BF)


def fold(v):
    rows, chans = v.shape
    return jnp.sum(v.reshape(rows // 8, 8, chans), 0)


def main_kernel(
    factor,
    nbr_hbm, x_hbm, cot_hbm, kern_hbm, cb_hbm, gain_hbm, nb_hbm, we_hbm, be_hbm, wr_hbm, br_hbm, ls_hbm,
    out_hbm, gath, sgath,
    nbr, x, cot, kern, cb, gain, nb, we, be, wr, br, ls, out,
    top, bot, hbuf, side, piece, pieces, chosen, near_band, far_band, near_out, far_out,
    pad, conv, taps, act, acc_e, acc_r, sums, ksum,
    big, slots1, slotsz, fin, small, sslots1, sslots2, few_ref, sfin,
    load_sem, out_sem, row_send, row_recv, side_send, side_recv, sem,
):
    f, t = place()
    last = TILES - 1
    mirror = last - t
    is_first = t == 0
    is_last = t == last
    has_up = t > 0
    has_down = t < last
    ward = lax.rem(t + 16, TILES)
    image = last - ward
    ward_up = ward > 0
    ward_down = ward < last
    image_up = jnp.logical_and(image > 0, image - 1 != t)
    image_down = jnp.logical_and(image < last, image + 1 != t)
    origin = [lax.rem(v + TILES, TILES) for v in (t + 15, t + 16, t + 17, 16 - t, 15 - t, 14 - t)]
    own3 = jnp.logical_and(has_up, origin[3] == t)
    own5 = jnp.logical_and(has_down, origin[5] == t)
    true = t >= 0
    valid = [
        has_up, true, has_down, jnp.logical_and(has_up, origin[3] != t), true,
        jnp.logical_and(has_down, origin[5] != t),
    ]
    edge = jnp.logical_or(is_first, is_last)
    hi = t // 16
    s = t % 16
    z = s // 2
    core = s % 2
    a = hi * 8 + f
    me = a * 2 + core
    others = [lax.rem(f + k, FACES) for k in range(1, FACES)]
    plane = [lax.rem(a + k, 16) for k in range(1, 16)]
    near = [lax.rem(me + k, 32) for k in range(1, 32)]
    line = [lax.rem(s + k, 16) for k in range(1, 16)]
    stack = [lax.rem(z + k, 8) for k in range(1, 8)]

    def plane_id(p):
        return lax.rem(p, 8), p // 8 * 16 + s

    def near_id(q):
        return lax.rem(q // 2, 8), q // 16 * 16 + z * 2 + q % 2

    def drain(ref, which):
        pltpu.make_async_copy(ref, ref, sem.at[which]).wait()

    loads = [
        pltpu.make_async_copy(src, dst, load_sem.at[i])
        for i, (src, dst) in enumerate(
            (
                (x_hbm, x), (kern_hbm, kern), (cb_hbm, cb), (cot_hbm, cot), (we_hbm, we), (wr_hbm, wr),
                (nbr_hbm, nbr), (gain_hbm, gain), (nb_hbm, nb), (be_hbm, be), (br_hbm, br), (ls_hbm, ls),
            )
        )
    ]
    for load in loads:
        load.start()

    barrier = pltpu.get_barrier_semaphore()

    def hello(face, tile):
        pl.semaphore_signal(barrier, inc=1, device_id=(face, tile), device_id_type=MESH)

    @pl.when(edge)
    def _():
        for g in range(FACES):
            hello(g, mirror)

    for q in near:
        hello(*near_id(q))
    for p in line:
        hello(f, hi * 16 + p)

    @pl.when(has_up)
    def _():
        hello(f, t - 1)

    @pl.when(has_down)
    def _():
        hello(f, t + 1)

    for tile, cond in zip(origin, valid):

        @pl.when(cond)
        def _(tile=tile):
            hello(f, tile)

    loads[0].wait()
    for d in range(3):
        west = x[:, d : d + 1, :].astype(F32).reshape(8, 128)
        east = x[:, 255 - d : 256 - d, :].astype(F32).reshape(8, 128)
        piece[d] = jnp.concatenate([west, east], 0).astype(BF)
    pad[3:11, 8:264, :] = x[...].astype(F32)
    for load in loads[1:3]:
        load.wait()
    for i in range(7):
        for j in range(7):
            taps[i * 7 + j] = jnp.broadcast_to(kern[i, j : j + 1, :], (8, 128))
    bias = jnp.broadcast_to(cb[...].reshape(1, 128), (8, 128))

    def convolve(col, acc, out_rows, in_rows, base=0):
        acc = dict(zip(out_rows, acc))
        for j in range(7):
            for row in in_rows:
                hit = [r for r in out_rows if 0 <= row - r < 7]
                if hit:
                    v = pad[base + row, pl.ds(col + 5 + j, 8), :]
                    for r in hit:
                        acc[r] = acc[r] + taps[(row - r) * 7 + j] * v
        return [acc[r] for r in out_rows]

    @pl.loop(0, 7)
    def _(i):
        for u in range(4):
            col = pl.multiple_of(16 + i * 32 + u * 8, 8)
            for r, v in enumerate(convolve(col, [bias] * 8, range(8), range(3, 11))):
                conv[r, pl.ds(col, 8), :] = v

    one = lambda cond: cond.astype(jnp.int32)
    targets = one(ward_up) + one(ward_down) + one(image_up) + one(image_down) + 2
    count = 46 + one(has_up) + one(has_down) + targets + 8 * one(edge)
    pl.semaphore_wait(barrier, count)

    def columns(c):
        return pl.ds(pl.multiple_of(c * 16, 16), 16)

    def piece_copy(k, g):
        return remote(piece, pieces.at[f], sem.at[2], sem.at[3], g, ward)

    def up_copy():
        return remote(x.at[pl.ds(0, 3)], bot, row_send.at[0], row_recv.at[0], f, t - 1)

    def down_copy():
        return remote(x.at[pl.ds(5, 3)], top, row_send.at[1], row_recv.at[1], f, t + 1)

    for rows, cond in ((0, is_first), (5, is_last)):

        @pl.when(cond)
        def _(rows=rows):
            three = pl.ds(rows, 3)
            for g in others:
                remote(x.at[three, columns(g), :], near_band.at[f], sem.at[0], sem.at[1], g, t).start()
            for g in range(FACES):
                remote(
                    x.at[three, columns(g + 8), :], far_band.at[f], sem.at[18], sem.at[19], g, mirror
                ).start()
            near_band[f] = x[three, columns(f), :]

    for k, g in enumerate(others):
        piece_copy(k, g).start()

    @pl.when(has_up)
    def _():
        up_copy().start()

    @pl.when(has_down)
    def _():
        down_copy().start()

    for load in loads[3:]:
        load.wait()

    def side_copy(slot, tile):
        return remote(chosen, side.at[slot], side_send.at[slot], side_recv.at[slot], f, tile)

    routes = (
        (0, ward + 1, ward_down), (1, ward, true), (2, ward - 1, ward_up),
        (3, image + 1, image_down), (4, image, true), (5, image - 1, image_up),
    )

    def pass_sides():
        drain(pieces.at[pl.ds(0, 7)], 3)
        from_west = pieces[nbr[0, 3, f]]
        from_east = pieces[nbr[0, 1, f]]
        chosen[...] = jnp.concatenate(
            [from_west.astype(F32)[:, 8:16], from_east.astype(F32)[:, 0:8]], 1
        ).astype(BF)
        for slot, tile, cond in routes:

            @pl.when(cond)
            def _(slot=slot, tile=tile):
                side_copy(slot, tile).start()

        @pl.when(own3)
        def _():
            side[3] = chosen[...]

        @pl.when(own5)
        def _():
            side[5] = chosen[...]

    def pass_bands():
        for near_side, far_side, cond in ((0, 2, is_last), (2, 0, is_first)):

            @pl.when(cond)
            def _(near_side=near_side, far_side=far_side):
                drain(near_band.at[pl.ds(0, 7)], 1)
                for g in range(FACES):
                    near_out[g] = near_band[nbr[0, near_side, g]]
                    remote(near_out.at[g], hbuf.at[f], sem.at[4], sem.at[5], g, mirror).start()
                drain(far_band, 19)
                for k, g in enumerate(others):
                    far_out[k] = far_band[nbr[0, far_side, g]]
                    remote(far_out.at[k], hbuf.at[f + 8], sem.at[4], sem.at[5], g, t).start()
                hbuf[f + 8] = far_band[nbr[0, far_side, f]]

    def polar(flag, rows):
        drain(hbuf.at[pl.ds(0, 15)], 5)
        turn = one_hot(256, 256, lambda r: 255 - r)
        for d in range(3):
            band = jnp.concatenate([hbuf[k, d] for k in range(16)], 0)
            turned = nn(turn, band)
            pad[rows[d], 8:264, :] = jnp.where(flag == 1, turned, band.astype(F32))

    def finish(out_rows, in_rows):
        @pl.loop(0, 7)
        def _(i):
            for u in range(4):
                col = pl.multiple_of(16 + i * 32 + u * 8, 8)
                acc = [conv[r, pl.ds(col, 8), :] for r in out_rows]
                for r, v in zip(out_rows, convolve(col, acc, out_rows, in_rows)):
                    conv[r, pl.ds(col, 8), :] = v

    def finish_top():
        @pl.when(has_up)
        def _():
            down_copy().wait_recv()
            pad[0:3, 8:264, :] = top[...].astype(F32)

        @pl.when(is_first)
        def _():
            polar(nbr[2, 0, f], (0, 1, 2))

        finish(range(0, 3), range(0, 3))

    def finish_bottom():
        @pl.when(has_down)
        def _():
            up_copy().wait_recv()
            pad[11:14, 8:264, :] = bot[...].astype(F32)

        @pl.when(is_last)
        def _():
            polar(nbr[2, 2, f], (11, 12, 13))

        finish(range(5, 8), range(11, 14))

    acc_e[...] = jnp.zeros_like(acc_e)
    acc_r[...] = jnp.zeros_like(acc_r)
    sums[...] = jnp.zeros_like(sums)
    mean_of = jnp.full((128, 128), 1.0 / 128, BF)
    vec = lambda ref: ref[...].reshape(1, -1)

    def mlp(c, cotangent, rows, between=None):
        count = c.shape[0]
        centred = c - nn(c.astype(BF), mean_of)
        variance = nn((centred * centred).astype(BF), mean_of)
        inverse = lax.rsqrt(variance + EPS)
        normed = centred * inverse
        scaled = (normed * vec(gain) + vec(nb)).astype(BF)
        branch_cot = (cotangent.astype(F32) * vec(ls)).astype(BF)
        hidden = nn(scaled, we[...]) + vec(be)
        active_cot = nt(branch_cot, wr[...])
        square = hidden * hidden
        gate = 0.5 + 0.5 * jnp.tanh(hidden * (ROOT + (ROOT * CUBE) * square))
        active = hidden * gate
        active_low = active.astype(BF)
        slope = gate + active * (1.0 - gate) * (2.0 * ROOT + (6.0 * ROOT * CUBE) * square)
        hidden_cot = (active_cot * slope).astype(BF)
        act[rows, :] = active_low
        left = jnp.concatenate([scaled.T, jnp.ones((16, count), BF)], 0)
        acc_e[...] += nn(left, hidden_cot)
        acc_r[...] += nn(branch_cot.T, active_low)
        if between is not None:
            between()
        scaled_cot = nt(hidden_cot, we[...])
        normed_cot = scaled_cot * vec(gain)
        m1 = nn(normed_cot.astype(BF), mean_of)
        m2 = nn((normed_cot * normed).astype(BF), mean_of)
        conv_cot = inverse * (normed_cot - m1 - normed * m2)
        sums[0] += fold(conv_cot)
        sums[1] += fold(scaled_cot * normed)
        sums[2] += fold(scaled_cot)
        sums[3] += fold(branch_cot.astype(F32))
        return conv_cot

    def kernel_grad(base, rows, cols):
        steps = len(cols) // 4

        @pl.loop(0, 7)
        def _(j):
            def step(k, acc):
                acc = list(acc)
                for u in range(4):
                    col = cols[u] if steps == 1 else pl.multiple_of(cols[0] + k * 32 + u * 8, 8)
                    cots = [conv[base + r, pl.ds(col, 8), :] for r in range(rows)]
                    for row in range(rows + 6):
                        v = pad[base + row, pl.ds(col + 5 + j, 8), :]
                        for i in range(7):
                            if 0 <= row - i < rows:
                                acc[i] = acc[i] + cots[row - i] * v
                return tuple(acc)

            zero = (jnp.zeros((8, 128), F32),) * 7
            acc = step(0, zero) if steps == 1 else lax.fori_loop(0, steps, step, zero)
            for i in range(7):
                ksum[i * 7 + j] += acc[i]

    inner = range(16, 240, 8)
    low_first = t < 16
    base1 = jnp.where(low_first, 5, 0)
    base2 = 5 - base1
    base5 = jnp.where(low_first, 3, 0)
    mid, three1, three2 = pl.ds(3, 2), pl.ds(base1, 3), pl.ds(base2, 3)
    five = pl.ds(base5, 5)

    def inside(ref, rows, count):
        return ref[rows, 16:240, :].reshape(count * 224, 128)

    def outside(ref):
        return jnp.concatenate([ref[five, 0:16, :], ref[five, 240:256, :]], 1).reshape(160, 128)

    got = mlp(inside(conv, mid, 2), inside(cot, mid, 2), pl.ds(0, 448))
    conv[mid, 16:240, :] = got.reshape(2, 224, 128)
    ksum[...] = jnp.zeros_like(ksum)
    kernel_grad(3, 2, inner)
    pass_sides()

    @pl.when(low_first)
    def _():
        finish_bottom()

    @pl.when(jnp.logical_not(low_first))
    def _():
        finish_top()

    got = mlp(inside(conv, three1, 3), inside(cot, three1, 3), pl.ds(448, 672))
    conv[three1, 16:240, :] = got.reshape(3, 224, 128)
    pass_bands()
    kernel_grad(base1, 3, inner)

    for slot, cond in enumerate(valid):

        @pl.when(cond)
        def _(slot=slot):
            side_copy(slot, origin[slot]).wait_recv()

    @pl.when(is_first)
    def _():
        side[0] = jnp.zeros((3, 16, 128), BF)
        side[3] = jnp.zeros((3, 16, 128), BF)

    @pl.when(is_last)
    def _():
        side[2] = jnp.zeros((3, 16, 128), BF)
        side[5] = jnp.zeros((3, 16, 128), BF)

    turn = one_hot(24, 24, lambda r: r // 8 * 8 + 7 - r % 8)
    for d in range(3):
        slots = [side[i, d].astype(F32) for i in range(6)]
        for first, side_id, col in ((0, 3, 7 - d), (8, 1, 264 + d)):
            straight = jnp.concatenate([slots[i][first : first + 8] for i in (0, 1, 2)], 0)
            turned = jnp.concatenate([slots[i][first : first + 8] for i in (3, 4, 5)], 0)
            turned = nn(turn, turned.astype(BF))
            halo = jnp.where(nbr[2, side_id, f] == 1, turned, straight)
            pad[0:14, col : col + 1, :] = halo[5:19].reshape(14, 1, 128)

    ends = (0, 8, 240, 248)

    def convolve_ends(base, rows):
        for col in ends:
            got = convolve(col, [bias] * rows, range(rows), range(rows + 6), base)
            for r, v in enumerate(got):
                conv[base + r, pl.ds(col, 8), :] = v

    convolve_ends(base5, 5)
    got = mlp(outside(conv), outside(cot), pl.ds(1120, 160)).reshape(5, 32, 128)
    conv[five, 0:16, :] = got[:, 0:16]
    conv[five, 240:256, :] = got[:, 16:32]
    kernel_grad(base5, 5, ends)

    @pl.when(low_first)
    def _():
        finish_top()

    @pl.when(jnp.logical_not(low_first))
    def _():
        finish_bottom()

    convolve_ends(base2, 3)

    def send_large():
        for q in range(4):
            cols = slice(q * 128, q * 128 + 128)
            big[q * 4 : q * 4 + 4] = acc_e[0:128, cols].astype(BF).reshape(4, 32, 128)
            big[16 + q * 4 : 20 + q * 4] = acc_r[:, cols].T.astype(BF).reshape(4, 32, 128)
        for q in near:
            remote(big.at[q], slots1.at[me], sem.at[6], sem.at[7], *near_id(q)).start()

    got = mlp(
        conv[three2, :, :].reshape(768, 128), cot[three2, :, :].reshape(768, 128), pl.ds(1280, 768), send_large
    )
    conv[three2, :, :] = got.reshape(3, 256, 128)
    slots1[me] = big[me]

    scale = jnp.zeros((8, 128), F32)
    for q in range(4):
        cols = slice(q * 128, q * 128 + 128)
        scale = scale + fold(acc_r[:, cols].T * wr[cols, :].astype(F32))
    small[...] = jnp.zeros_like(small)
    totals = [jnp.sum(sums[i], 0, keepdims=True) for i in range(4)]
    totals.append((jnp.sum(scale, 0, keepdims=True) + vec(br) * totals[3]) / vec(ls))
    for i in range(5):
        small[49 + i : 50 + i, :] = totals[i]
    for q in range(4):
        small[54 + q : 55 + q, :] = acc_e[128:129, q * 128 : q * 128 + 128]

    kernel_grad(base2, 3, range(0, 256, 8))
    for i in range(49):
        small[i : i + 1, :] = jnp.sum(ksum[i], 0, keepdims=True)

    for p in plane:
        rows = pl.ds(pl.multiple_of(lax.rem(p, 8) * 8, 8), 8)
        remote(small.at[rows], sslots1.at[a], sem.at[8], sem.at[9], *plane_id(p)).start()
    sslots1[a] = small[pl.ds(pl.multiple_of(f * 8, 8), 8), :]

    def output(rows, residual):
        branch = nn(act[rows, :], wr[...]) + vec(br)
        return (residual.astype(F32) + vec(ls) * branch).astype(BF)

    def output_inside(rows, three, count):
        out[three, 16:240, :] = output(rows, inside(x, three, count)).reshape(count, 224, 128)

    output_inside(pl.ds(0, 448), mid, 2)
    output_inside(pl.ds(448, 672), three1, 3)

    drain(slots1.at[pl.ds(0, 31)], 7)
    total = slots1[0].astype(F32)
    for q in range(1, 32):
        total = total + slots1[q].astype(F32)
    slotsz[z] = total.astype(BF)
    for q in stack:
        remote(
            slotsz.at[z], slotsz.at[z], sem.at[10], sem.at[11], f, hi * 16 + q * 2 + core
        ).start()

    got = output(pl.ds(1120, 160), outside(x)).reshape(5, 32, 128)
    out[five, 0:16, :] = got[:, 0:16]
    out[five, 240:256, :] = got[:, 16:32]
    got = output(pl.ds(1280, 768), x[three2, :, :].reshape(768, 128))
    out[three2, :, :] = got.reshape(3, 256, 128)
    store = pltpu.make_async_copy(out, out_hbm, out_sem.at[0])
    store.start()

    drain(sslots1.at[pl.ds(0, 15)], 9)
    few = sslots1[0]
    for p in range(1, 16):
        few = few + sslots1[p]
    few_ref[...] = few
    for p in line:
        remote(few_ref, sslots2.at[s], sem.at[12], sem.at[13], f, hi * 16 + p).start()
    sslots2[s] = few

    drain(slotsz.at[pl.ds(0, 7)], 11)
    total = slotsz[0].astype(F32)
    for q in range(1, 8):
        total = total + slotsz[q].astype(F32)
    fin[...] = (total * factor).astype(BF)
    for q in near:
        remote(fin, gath.at[me], sem.at[14], sem.at[15], *near_id(q)).start()
    own = pltpu.make_async_copy(fin, gath.at[me], out_sem.at[1])
    own.start()

    drain(sslots2.at[pl.ds(0, 15)], 13)
    few = sslots2[0]
    for p in range(1, 16):
        few = few + sslots2[p]
    sfin[...] = few * factor
    for g in others:
        remote(sfin, sgath.at[f], sem.at[16], sem.at[17], g, t).start()
    own_small = pltpu.make_async_copy(sfin, sgath.at[f], out_sem.at[2])
    own_small.start()
    drain(sgath.at[pl.ds(0, 7)], 17)
    drain(gath.at[pl.ds(0, 31)], 15)

    store.wait()
    own.wait()
    own_small.wait()
    for slot, tile, cond in routes:

        @pl.when(cond)
        def _(slot=slot, tile=tile):
            side_copy(slot, tile).wait_send()

    @pl.when(has_up)
    def _():
        up_copy().wait_send()

    @pl.when(has_down)
    def _():
        down_copy().wait_send()

    @pl.when(edge)
    def _():
        drain(near_band.at[pl.ds(0, 7)], 0)
        drain(far_band, 18)
        drain(hbuf.at[pl.ds(0, 15)], 4)

    drain(pieces.at[pl.ds(0, 7)], 2)
    drain(slots1.at[pl.ds(0, 31)], 6)
    drain(sslots1.at[pl.ds(0, 15)], 8)
    drain(slotsz.at[pl.ds(0, 7)], 10)
    drain(sslots2.at[pl.ds(0, 15)], 12)
    drain(gath.at[pl.ds(0, 31)], 14)
    drain(sgath.at[pl.ds(0, 7)], 16)


def run_main(factor, neighbours, *operands):
    dma = pltpu.SemaphoreType.DMA
    shape = lambda *dims: jax.ShapeDtypeStruct(dims, BF)
    return pl.pallas_call(
        functools.partial(main_kernel, factor),
        out_shape=(
            shape(8, 256, 128),
            shape(32, 32, 128),
            jax.ShapeDtypeStruct((8, 8, 128), F32),
        ),
        in_specs=[ANY] * 12,
        out_specs=(ANY, ANY, ANY),
        scratch_shapes=[pltpu.SMEM(neighbours.shape, jnp.int32)]
        + [pltpu.VMEM(item.shape, item.dtype) for item in operands]
        + [
            pltpu.VMEM((8, 256, 128), BF),
            pltpu.VMEM((3, 256, 128), BF),
            pltpu.VMEM((3, 256, 128), BF),
            pltpu.VMEM((16, 3, 16, 128), BF),
            pltpu.VMEM((6, 3, 16, 128), BF),
            pltpu.VMEM((3, 16, 128), BF),
            pltpu.VMEM((8, 3, 16, 128), BF),
            pltpu.VMEM((3, 16, 128), BF),
            pltpu.VMEM((8, 3, 16, 128), BF),
            pltpu.VMEM((8, 3, 16, 128), BF),
            pltpu.VMEM((8, 3, 16, 128), BF),
            pltpu.VMEM((7, 3, 16, 128), BF),
            pltpu.VMEM((14, 272, 128), F32),
            pltpu.VMEM((8, 256, 128), F32),
            pltpu.VMEM((49, 8, 128), F32),
            pltpu.VMEM((2048, 512), BF),
            pltpu.VMEM((144, 512), F32),
            pltpu.VMEM((128, 512), F32),
            pltpu.VMEM((4, 8, 128), F32),
            pltpu.VMEM((49, 8, 128), F32),
            pltpu.VMEM((32, 32, 128), BF),
            pltpu.VMEM((32, 32, 128), BF),
            pltpu.VMEM((8, 32, 128), BF),
            pltpu.VMEM((32, 128), BF),
            pltpu.VMEM((64, 128), F32),
            pltpu.VMEM((16, 8, 128), F32),
            pltpu.VMEM((16, 8, 128), F32),
            pltpu.VMEM((8, 128), F32),
            pltpu.VMEM((8, 128), F32),
            dma((12,)), dma((3,)), dma((2,)), dma((2,)), dma((6,)), dma((6,)), dma((20,)),
        ],
        compiler_params=pltpu.CompilerParams(
            collective_id=0, has_side_effects=True, vmem_limit_bytes=56 * 1024 * 1024
        ),
        name="main",
    )(neighbours, *operands)


def unpack_kernel(
    raw, gath, sgath,
    out, kernel_grad, cb_grad, gain_grad, nb_grad, we_grad, be_grad, wr_grad, br_grad, ls_grad,
    stage, rows_in, few_in, sem,
):
    fetches = [
        pltpu.make_async_copy(src, dst, sem.at[i])
        for i, (src, dst) in enumerate(((raw, stage), (gath, rows_in), (sgath, few_in)))
    ]
    for fetch in fetches:
        fetch.start()
    store = pltpu.make_async_copy(stage, out, sem.at[3])
    fetches[0].wait()
    store.start()
    fetches[1].wait()
    fetches[2].wait()
    rows = rows_in.reshape(1024, 128)
    few = few_in[...].reshape(64, 128)
    for q in range(4):
        we_grad[:, q * 128 : q * 128 + 128] = rows[q * 128 : q * 128 + 128, :].astype(F32)
        be_grad[q * 128 : q * 128 + 128] = few[54 + q]
    wr_grad[...] = rows[512:1024, :].astype(F32)
    for i in range(7):
        kernel_grad[i] = few[i * 7 : i * 7 + 7]
    for i, ref in enumerate((cb_grad, gain_grad, nb_grad, br_grad, ls_grad)):
        ref[...] = few[49 + i]
    store.wait()


def unpack(raw, gath, sgath):
    one = lambda *shape: jax.ShapeDtypeStruct(shape, F32)
    return pl.pallas_call(
        unpack_kernel,
        out_shape=(
            jax.ShapeDtypeStruct(raw.shape, raw.dtype),
            one(7, 7, 128), one(128), one(128), one(128), one(128, 512), one(512),
            one(512, 128), one(128), one(128),
        ),
        in_specs=[ANY, ANY, ANY],
        out_specs=(ANY,) + (VMEM,) * 9,
        scratch_shapes=[
            pltpu.VMEM(raw.shape, raw.dtype),
            pltpu.VMEM(gath.shape, gath.dtype),
            pltpu.VMEM(sgath.shape, sgath.dtype),
            pltpu.SemaphoreType.DMA((4,)),
        ],
        compiler_params=pltpu.CompilerParams(vmem_limit_bytes=56 * 1024 * 1024),
        name="unpack",
    )(raw, gath, sgath)


def body(
    inputs, kernel, conv_bias, norm_gain, norm_bias, expand_weight, expand_bias,
    reduce_weight, reduce_bias, layer_scale, neighbours, cotangent,
):
    factor = 1.0 / math.sqrt(FACES * 256 * 256)
    raw, gath, sgath = run_main(
        factor, jnp.transpose(neighbours, (2, 1, 0)), inputs[0], cotangent[0], kernel, conv_bias, norm_gain, norm_bias,
        expand_weight, expand_bias, reduce_weight, reduce_bias, layer_scale,
    )
    out, *grads = unpack(raw, gath, sgath)
    return (out[None], *grads)


def solution(mesh):
    split = P("face", "tile", None, None)
    return jax.shard_map(
        body,
        mesh=mesh,
        in_specs=(split,) + (P(),) * 10 + (split,),
        out_specs=(split,) + (P(),) * 9,
        check_vma=False,
    )
```

```python
import functools
import math

import jax
import jax.numpy as jnp
from jax import lax
from jax.experimental import pallas as pl
from jax.experimental.pallas import tpu as pltpu
from jax.sharding import PartitionSpec as P

EPS = 1e-06
MESH = pl.DeviceIdType.MESH
BF = jnp.bfloat16
F32 = jnp.float32
ROOT = math.sqrt(2.0 / math.pi)
CUBE = 0.044715
FACES = 8
TILES = 32
VMEM = pl.BlockSpec(memory_space=pltpu.VMEM)
SMEM = pl.BlockSpec(memory_space=pltpu.SMEM)
ANY = pl.BlockSpec(memory_space=pl.ANY)


def place():
    return lax.axis_index("face"), lax.axis_index("tile")


def remote(src, dst, send, recv, face, tile):
    return pltpu.make_async_remote_copy(
        src_ref=src, dst_ref=dst, send_sem=send, recv_sem=recv,
        device_id=(face, tile), device_id_type=MESH,
    )


def nt(left, right):
    return lax.dot_general(left, right, (((1,), (1,)), ((), ())), preferred_element_type=F32)


def nn(left, right):
    return lax.dot_general(left, right, (((1,), (0,)), ((), ())), preferred_element_type=F32)


def one_hot(rows, cols, index):
    r = lax.broadcasted_iota(jnp.int32, (rows, cols), 0)
    c = lax.broadcasted_iota(jnp.int32, (rows, cols), 1)
    return jnp.where(c == index(r), 1.0, 0.0).astype(BF)


def fold(v):
    rows, chans = v.shape
    return jnp.sum(v.reshape(rows // 8, 8, chans), 0)


def main_kernel(
    factor,
    nbr_hbm, x_hbm, cot_hbm, kern_hbm, cb_hbm, gain_hbm, nb_hbm, we_hbm, be_hbm, wr_hbm, br_hbm, ls_hbm,
    out_hbm, gath, sgath,
    nbr, x, cot, kern, cb, gain, nb, we, be, wr, br, ls, out,
    top, bot, hbuf, side, piece, pieces, chosen, near_band, far_band, near_out, far_out,
    pad, conv, taps, act, pulled, pulled_wide, acc_e, acc_r, sums, ksum,
    big, slots1, slotsz, fin, small, sslots1, sslots2, few_ref, sfin,
    load_sem, out_sem, row_send, row_recv, side_send, side_recv, sem,
):
    f, t = place()
    last = TILES - 1
    mirror = last - t
    is_first = t == 0
    is_last = t == last
    has_up = t > 0
    has_down = t < last
    ward = lax.rem(t + 16, TILES)
    image = last - ward
    ward_up = ward > 0
    ward_down = ward < last
    image_up = jnp.logical_and(image > 0, image - 1 != t)
    image_down = jnp.logical_and(image < last, image + 1 != t)
    origin = [lax.rem(v + TILES, TILES) for v in (t + 15, t + 16, t + 17, 16 - t, 15 - t, 14 - t)]
    own3 = jnp.logical_and(has_up, origin[3] == t)
    own5 = jnp.logical_and(has_down, origin[5] == t)
    true = t >= 0
    valid = [
        has_up, true, has_down, jnp.logical_and(has_up, origin[3] != t), true,
        jnp.logical_and(has_down, origin[5] != t),
    ]
    edge = jnp.logical_or(is_first, is_last)
    hi = t // 16
    s = t % 16
    z = s // 2
    core = s % 2
    a = hi * 8 + f
    me = a * 2 + core
    others = [lax.rem(f + k, FACES) for k in range(1, FACES)]
    plane = [lax.rem(a + k, 16) for k in range(1, 16)]
    near = [lax.rem(me + k, 32) for k in range(1, 32)]
    line = [lax.rem(s + k, 16) for k in range(1, 16)]
    stack = [lax.rem(z + k, 8) for k in range(1, 8)]

    def plane_id(p):
        return lax.rem(p, 8), p // 8 * 16 + s

    def near_id(q):
        return lax.rem(q // 2, 8), q // 16 * 16 + z * 2 + q % 2

    def drain(ref, which):
        pltpu.make_async_copy(ref, ref, sem.at[which]).wait()

    loads = [
        pltpu.make_async_copy(src, dst, load_sem.at[i])
        for i, (src, dst) in enumerate(
            (
                (x_hbm, x), (kern_hbm, kern), (cb_hbm, cb), (cot_hbm, cot), (we_hbm, we), (wr_hbm, wr),
                (nbr_hbm, nbr), (gain_hbm, gain), (nb_hbm, nb), (be_hbm, be), (br_hbm, br), (ls_hbm, ls),
            )
        )
    ]
    for load in loads:
        load.start()

    barrier = pltpu.get_barrier_semaphore()

    def hello(face, tile):
        pl.semaphore_signal(barrier, inc=1, device_id=(face, tile), device_id_type=MESH)

    @pl.when(edge)
    def _():
        for g in range(FACES):
            hello(g, mirror)

    @pl.when(has_up)
    def _():
        hello(f, t - 1)

    @pl.when(has_down)
    def _():
        hello(f, t + 1)

    for tile, cond in zip(origin, valid):

        @pl.when(cond)
        def _(tile=tile):
            hello(f, tile)

    for p in line:
        hello(f, hi * 16 + p)
    for q in near:
        hello(*near_id(q))

    loads[0].wait()
    for d in range(3):
        west = x[:, d : d + 1, :].astype(F32).reshape(8, 128)
        east = x[:, 255 - d : 256 - d, :].astype(F32).reshape(8, 128)
        piece[d] = jnp.concatenate([west, east], 0).astype(BF)
    pad[3:11, 8:264, :] = x[...].astype(F32)
    for load in loads[1:3]:
        load.wait()
    for i in range(7):
        for j in range(7):
            taps[i * 7 + j] = jnp.broadcast_to(kern[i, j : j + 1, :], (8, 128))
    bias = jnp.broadcast_to(cb[...].reshape(1, 128), (8, 128))

    def convolve(col, acc, out_rows, in_rows, base=0):
        acc = dict(zip(out_rows, acc))
        for j in range(7):
            for row in in_rows:
                hit = [r for r in out_rows if 0 <= row - r < 7]
                if hit:
                    v = pad[base + row, pl.ds(col + 5 + j, 8), :]
                    for r in hit:
                        acc[r] = acc[r] + taps[(row - r) * 7 + j] * v
        return [acc[r] for r in out_rows]

    @pl.loop(0, 7)
    def _(i):
        for u in range(4):
            col = pl.multiple_of(16 + i * 32 + u * 8, 8)
            for r, v in enumerate(convolve(col, [bias] * 8, range(8), range(3, 11))):
                conv[r, pl.ds(col, 8), :] = v

    one = lambda cond: cond.astype(jnp.int32)
    targets = one(ward_up) + one(ward_down) + one(image_up) + one(image_down) + 2
    count = 46 + one(has_up) + one(has_down) + targets + 8 * one(edge)
    pl.semaphore_wait(barrier, count)

    def columns(c):
        return pl.ds(pl.multiple_of(c * 16, 16), 16)

    def piece_copy(k, g):
        return remote(piece, pieces.at[f], sem.at[2], sem.at[3], g, ward)

    def up_copy():
        return remote(x.at[pl.ds(0, 3)], bot, row_send.at[0], row_recv.at[0], f, t - 1)

    def down_copy():
        return remote(x.at[pl.ds(5, 3)], top, row_send.at[1], row_recv.at[1], f, t + 1)

    for rows, cond in ((0, is_first), (5, is_last)):

        @pl.when(cond)
        def _(rows=rows):
            three = pl.ds(rows, 3)
            for g in others:
                remote(x.at[three, columns(g), :], near_band.at[f], sem.at[0], sem.at[1], g, t).start()
            for g in range(FACES):
                remote(
                    x.at[three, columns(g + 8), :], far_band.at[f], sem.at[18], sem.at[19], g, mirror
                ).start()
            near_band[f] = x[three, columns(f), :]

    for k, g in enumerate(others):
        piece_copy(k, g).start()

    @pl.when(has_up)
    def _():
        up_copy().start()

    @pl.when(has_down)
    def _():
        down_copy().start()

    for load in loads[3:]:
        load.wait()

    def side_copy(slot, tile):
        return remote(chosen, side.at[slot], side_send.at[slot], side_recv.at[slot], f, tile)

    routes = (
        (0, ward + 1, ward_down), (1, ward, true), (2, ward - 1, ward_up),
        (3, image + 1, image_down), (4, image, true), (5, image - 1, image_up),
    )

    def pass_sides():
        drain(pieces.at[pl.ds(0, 7)], 3)
        from_west = pieces[nbr[0, 3, f]]
        from_east = pieces[nbr[0, 1, f]]
        chosen[...] = jnp.concatenate(
            [from_west.astype(F32)[:, 8:16], from_east.astype(F32)[:, 0:8]], 1
        ).astype(BF)
        for slot, tile, cond in routes:

            @pl.when(cond)
            def _(slot=slot, tile=tile):
                side_copy(slot, tile).start()

        @pl.when(own3)
        def _():
            side[3] = chosen[...]

        @pl.when(own5)
        def _():
            side[5] = chosen[...]

    def pass_bands():
        for near_side, far_side, cond in ((0, 2, is_last), (2, 0, is_first)):

            @pl.when(cond)
            def _(near_side=near_side, far_side=far_side):
                drain(near_band.at[pl.ds(0, 7)], 1)
                for g in range(FACES):
                    near_out[g] = near_band[nbr[0, near_side, g]]
                    remote(near_out.at[g], hbuf.at[f], sem.at[4], sem.at[5], g, mirror).start()
                drain(far_band, 19)
                for k, g in enumerate(others):
                    far_out[k] = far_band[nbr[0, far_side, g]]
                    remote(far_out.at[k], hbuf.at[f + 8], sem.at[4], sem.at[5], g, t).start()
                hbuf[f + 8] = far_band[nbr[0, far_side, f]]

    def polar(flag, rows):
        drain(hbuf.at[pl.ds(0, 15)], 5)
        turn = one_hot(256, 256, lambda r: 255 - r)
        for d in range(3):
            band = jnp.concatenate([hbuf[k, d] for k in range(16)], 0)
            turned = nn(turn, band)
            pad[rows[d], 8:264, :] = jnp.where(flag == 1, turned, band.astype(F32))

    def finish(out_rows, in_rows):
        @pl.loop(0, 7)
        def _(i):
            for u in range(4):
                col = pl.multiple_of(16 + i * 32 + u * 8, 8)
                acc = [conv[r, pl.ds(col, 8), :] for r in out_rows]
                for r, v in zip(out_rows, convolve(col, acc, out_rows, in_rows)):
                    conv[r, pl.ds(col, 8), :] = v

    def finish_top():
        @pl.when(has_up)
        def _():
            down_copy().wait_recv()
            pad[0:3, 8:264, :] = top[...].astype(F32)

        @pl.when(is_first)
        def _():
            polar(nbr[2, 0, f], (0, 1, 2))

        finish(range(0, 3), range(0, 3))

    def finish_bottom():
        @pl.when(has_down)
        def _():
            up_copy().wait_recv()
            pad[11:14, 8:264, :] = bot[...].astype(F32)

        @pl.when(is_last)
        def _():
            polar(nbr[2, 2, f], (11, 12, 13))

        finish(range(5, 8), range(11, 14))

    acc_e[...] = jnp.zeros_like(acc_e)
    acc_r[...] = jnp.zeros_like(acc_r)
    sums[...] = jnp.zeros_like(sums)
    mean_of = jnp.full((128, 128), 1.0 / 128, BF)
    vec = lambda ref: ref[...].reshape(1, -1)

    def pull_back(cotangent):
        branch_cot = (cotangent.astype(F32) * vec(ls)).astype(BF)
        sums[3] += fold(branch_cot.astype(F32))
        return branch_cot, nt(branch_cot, wr[...])

    def mlp(c, pulled, rows, between=None):
        count = c.shape[0]
        centred = c - nn(c.astype(BF), mean_of)
        variance = nn((centred * centred).astype(BF), mean_of)
        inverse = lax.rsqrt(variance + EPS)
        normed = centred * inverse
        scaled = (normed * vec(gain) + vec(nb)).astype(BF)
        hidden = nn(scaled, we[...]) + vec(be)
        branch_cot, active_cot = pulled
        square = hidden * hidden
        gate = 0.5 + 0.5 * jnp.tanh(hidden * (ROOT + (ROOT * CUBE) * square))
        active = hidden * gate
        active_low = active.astype(BF)
        slope = gate + active * (1.0 - gate) * (2.0 * ROOT + (6.0 * ROOT * CUBE) * square)
        hidden_cot = (active_cot * slope).astype(BF)
        act[rows, :] = active_low
        left = jnp.concatenate([scaled.T, jnp.ones((16, count), BF)], 0)
        acc_e[...] += nn(left, hidden_cot)
        acc_r[...] += nn(branch_cot.T, active_low)
        if between is not None:
            between()
        scaled_cot = nt(hidden_cot, we[...])
        normed_cot = scaled_cot * vec(gain)
        m1 = nn(normed_cot.astype(BF), mean_of)
        m2 = nn((normed_cot * normed).astype(BF), mean_of)
        conv_cot = inverse * (normed_cot - m1 - normed * m2)
        sums[0] += fold(conv_cot)
        sums[1] += fold(scaled_cot * normed)
        sums[2] += fold(scaled_cot)
        return conv_cot

    def kernel_grad(base, rows, cols):
        steps = len(cols) // 4

        @pl.loop(0, 7)
        def _(j):
            def step(k, acc):
                acc = list(acc)
                for u in range(4):
                    col = cols[u] if steps == 1 else pl.multiple_of(cols[0] + k * 32 + u * 8, 8)
                    cots = [conv[base + r, pl.ds(col, 8), :] for r in range(rows)]
                    for row in range(rows + 6):
                        v = pad[base + row, pl.ds(col + 5 + j, 8), :]
                        for i in range(7):
                            if 0 <= row - i < rows:
                                acc[i] = acc[i] + cots[row - i] * v
                return tuple(acc)

            zero = (jnp.zeros((8, 128), F32),) * 7
            acc = step(0, zero) if steps == 1 else lax.fori_loop(0, steps, step, zero)
            for i in range(7):
                ksum[i * 7 + j] += acc[i]

    inner = range(16, 240, 8)
    low_first = t < 16
    base1 = jnp.where(low_first, 5, 0)
    base2 = 5 - base1
    base5 = jnp.where(low_first, 3, 0)
    mid, three1, three2 = pl.ds(3, 2), pl.ds(base1, 3), pl.ds(base2, 3)
    five = pl.ds(base5, 5)

    def inside(ref, rows, count):
        return ref[rows, 16:240, :].reshape(count * 224, 128)

    def outside(ref):
        return jnp.concatenate([ref[five, 0:16, :], ref[five, 240:256, :]], 1).reshape(160, 128)

    got = mlp(inside(conv, mid, 2), pull_back(inside(cot, mid, 2)), pl.ds(0, 448))
    conv[mid, 16:240, :] = got.reshape(2, 224, 128)
    ksum[...] = jnp.zeros_like(ksum)
    kernel_grad(3, 2, inner)
    pass_sides()

    @pl.when(low_first)
    def _():
        finish_bottom()

    @pl.when(jnp.logical_not(low_first))
    def _():
        finish_top()

    pass_bands()
    got = mlp(inside(conv, three1, 3), pull_back(inside(cot, three1, 3)), pl.ds(448, 672))
    conv[three1, 16:240, :] = got.reshape(3, 224, 128)
    kernel_grad(base1, 3, inner)

    for slot, cond in enumerate(valid):

        @pl.when(cond)
        def _(slot=slot):
            side_copy(slot, origin[slot]).wait_recv()

    @pl.when(is_first)
    def _():
        side[0] = jnp.zeros((3, 16, 128), BF)
        side[3] = jnp.zeros((3, 16, 128), BF)

    @pl.when(is_last)
    def _():
        side[2] = jnp.zeros((3, 16, 128), BF)
        side[5] = jnp.zeros((3, 16, 128), BF)

    turn = one_hot(24, 24, lambda r: r // 8 * 8 + 7 - r % 8)
    for d in range(3):
        slots = [side[i, d].astype(F32) for i in range(6)]
        for first, side_id, col in ((0, 3, 7 - d), (8, 1, 264 + d)):
            straight = jnp.concatenate([slots[i][first : first + 8] for i in (0, 1, 2)], 0)
            turned = jnp.concatenate([slots[i][first : first + 8] for i in (3, 4, 5)], 0)
            turned = nn(turn, turned.astype(BF))
            halo = jnp.where(nbr[2, side_id, f] == 1, turned, straight)
            pad[0:14, col : col + 1, :] = halo[5:19].reshape(14, 1, 128)

    ends = (0, 8, 240, 248)

    def convolve_ends(base, rows):
        for col in ends:
            got = convolve(col, [bias] * rows, range(rows), range(rows + 6), base)
            for r, v in enumerate(got):
                conv[base + r, pl.ds(col, 8), :] = v

    convolve_ends(base5, 5)
    got = mlp(outside(conv), pull_back(outside(cot)), pl.ds(1120, 160)).reshape(5, 32, 128)
    conv[five, 0:16, :] = got[:, 0:16]
    conv[five, 240:256, :] = got[:, 16:32]
    kernel_grad(base5, 5, ends)

    pulled[...], pulled_wide[...] = pull_back(cot[three2, :, :].reshape(768, 128))

    @pl.when(low_first)
    def _():
        finish_top()

    @pl.when(jnp.logical_not(low_first))
    def _():
        finish_bottom()

    convolve_ends(base2, 3)

    def send_large():
        for q in range(4):
            cols = slice(q * 128, q * 128 + 128)
            big[q * 4 : q * 4 + 4] = acc_e[0:128, cols].astype(BF).reshape(4, 32, 128)
            big[16 + q * 4 : 20 + q * 4] = acc_r[:, cols].T.astype(BF).reshape(4, 32, 128)
        for q in near:
            remote(big.at[q], slots1.at[me], sem.at[6], sem.at[7], *near_id(q)).start()

    got = mlp(
        conv[three2, :, :].reshape(768, 128), (pulled[...], pulled_wide[...]), pl.ds(1280, 768), send_large
    )
    conv[three2, :, :] = got.reshape(3, 256, 128)
    slots1[me] = big[me]

    scale = jnp.zeros((8, 128), F32)
    for q in range(4):
        cols = slice(q * 128, q * 128 + 128)
        scale = scale + fold(acc_r[:, cols].T * wr[cols, :].astype(F32))
    small[...] = jnp.zeros_like(small)
    totals = [jnp.sum(sums[i], 0, keepdims=True) for i in range(4)]
    totals.append((jnp.sum(scale, 0, keepdims=True) + vec(br) * totals[3]) / vec(ls))
    for i in range(5):
        small[49 + i : 50 + i, :] = totals[i]
    for q in range(4):
        small[54 + q : 55 + q, :] = acc_e[128:129, q * 128 : q * 128 + 128]

    kernel_grad(base2, 3, range(0, 256, 8))
    for i in range(49):
        small[i : i + 1, :] = jnp.sum(ksum[i], 0, keepdims=True)

    for p in plane:
        rows = pl.ds(pl.multiple_of(lax.rem(p, 8) * 8, 8), 8)
        remote(small.at[rows], sslots1.at[a], sem.at[8], sem.at[9], *plane_id(p)).start()
    sslots1[a] = small[pl.ds(pl.multiple_of(f * 8, 8), 8), :]

    def output(rows, residual):
        branch = nn(act[rows, :], wr[...]) + vec(br)
        return (residual.astype(F32) + vec(ls) * branch).astype(BF)

    def output_inside(rows, three, count):
        out[three, 16:240, :] = output(rows, inside(x, three, count)).reshape(count, 224, 128)

    output_inside(pl.ds(0, 448), mid, 2)
    output_inside(pl.ds(448, 672), three1, 3)

    drain(slots1.at[pl.ds(0, 31)], 7)
    total = slots1[0].astype(F32)
    for q in range(1, 32):
        total = total + slots1[q].astype(F32)
    slotsz[z] = total.astype(BF)
    for q in stack:
        remote(
            slotsz.at[z], slotsz.at[z], sem.at[10], sem.at[11], f, hi * 16 + q * 2 + core
        ).start()

    got = output(pl.ds(1120, 160), outside(x)).reshape(5, 32, 128)
    out[five, 0:16, :] = got[:, 0:16]
    out[five, 240:256, :] = got[:, 16:32]
    got = output(pl.ds(1280, 768), x[three2, :, :].reshape(768, 128))
    out[three2, :, :] = got.reshape(3, 256, 128)
    store = pltpu.make_async_copy(out, out_hbm, out_sem.at[0])
    store.start()

    drain(sslots1.at[pl.ds(0, 15)], 9)
    few = sslots1[0]
    for p in range(1, 16):
        few = few + sslots1[p]
    few_ref[...] = few
    for p in line:
        remote(few_ref, sslots2.at[s], sem.at[12], sem.at[13], f, hi * 16 + p).start()
    sslots2[s] = few

    drain(slotsz.at[pl.ds(0, 7)], 11)
    total = slotsz[0].astype(F32)
    for q in range(1, 8):
        total = total + slotsz[q].astype(F32)
    fin[...] = (total * factor).astype(BF)
    for q in near:
        remote(fin, gath.at[me], sem.at[14], sem.at[15], *near_id(q)).start()
    own = pltpu.make_async_copy(fin, gath.at[me], out_sem.at[1])
    own.start()

    drain(sslots2.at[pl.ds(0, 15)], 13)
    few = sslots2[0]
    for p in range(1, 16):
        few = few + sslots2[p]
    sfin[...] = few * factor
    for g in others:
        remote(sfin, sgath.at[f], sem.at[16], sem.at[17], g, t).start()
    own_small = pltpu.make_async_copy(sfin, sgath.at[f], out_sem.at[2])
    own_small.start()
    drain(sgath.at[pl.ds(0, 7)], 17)
    drain(gath.at[pl.ds(0, 31)], 15)

    store.wait()
    own.wait()
    own_small.wait()
    for slot, tile, cond in routes:

        @pl.when(cond)
        def _(slot=slot, tile=tile):
            side_copy(slot, tile).wait_send()

    @pl.when(has_up)
    def _():
        up_copy().wait_send()

    @pl.when(has_down)
    def _():
        down_copy().wait_send()

    @pl.when(edge)
    def _():
        drain(near_band.at[pl.ds(0, 7)], 0)
        drain(far_band, 18)
        drain(hbuf.at[pl.ds(0, 15)], 4)

    drain(pieces.at[pl.ds(0, 7)], 2)
    drain(slots1.at[pl.ds(0, 31)], 6)
    drain(sslots1.at[pl.ds(0, 15)], 8)
    drain(slotsz.at[pl.ds(0, 7)], 10)
    drain(sslots2.at[pl.ds(0, 15)], 12)
    drain(gath.at[pl.ds(0, 31)], 14)
    drain(sgath.at[pl.ds(0, 7)], 16)


def run_main(factor, neighbours, *operands):
    dma = pltpu.SemaphoreType.DMA
    shape = lambda *dims: jax.ShapeDtypeStruct(dims, BF)
    return pl.pallas_call(
        functools.partial(main_kernel, factor),
        out_shape=(
            shape(8, 256, 128),
            shape(32, 32, 128),
            jax.ShapeDtypeStruct((8, 8, 128), F32),
        ),
        in_specs=[ANY] * 12,
        out_specs=(ANY, ANY, ANY),
        scratch_shapes=[pltpu.SMEM(neighbours.shape, jnp.int32)]
        + [pltpu.VMEM(item.shape, item.dtype) for item in operands]
        + [
            pltpu.VMEM((8, 256, 128), BF),
            pltpu.VMEM((3, 256, 128), BF),
            pltpu.VMEM((3, 256, 128), BF),
            pltpu.VMEM((16, 3, 16, 128), BF),
            pltpu.VMEM((6, 3, 16, 128), BF),
            pltpu.VMEM((3, 16, 128), BF),
            pltpu.VMEM((8, 3, 16, 128), BF),
            pltpu.VMEM((3, 16, 128), BF),
            pltpu.VMEM((8, 3, 16, 128), BF),
            pltpu.VMEM((8, 3, 16, 128), BF),
            pltpu.VMEM((8, 3, 16, 128), BF),
            pltpu.VMEM((7, 3, 16, 128), BF),
            pltpu.VMEM((14, 272, 128), F32),
            pltpu.VMEM((8, 256, 128), F32),
            pltpu.VMEM((49, 8, 128), F32),
            pltpu.VMEM((2048, 512), BF),
            pltpu.VMEM((768, 128), BF),
            pltpu.VMEM((768, 512), F32),
            pltpu.VMEM((144, 512), F32),
            pltpu.VMEM((128, 512), F32),
            pltpu.VMEM((4, 8, 128), F32),
            pltpu.VMEM((49, 8, 128), F32),
            pltpu.VMEM((32, 32, 128), BF),
            pltpu.VMEM((32, 32, 128), BF),
            pltpu.VMEM((8, 32, 128), BF),
            pltpu.VMEM((32, 128), BF),
            pltpu.VMEM((64, 128), F32),
            pltpu.VMEM((16, 8, 128), F32),
            pltpu.VMEM((16, 8, 128), F32),
            pltpu.VMEM((8, 128), F32),
            pltpu.VMEM((8, 128), F32),
            dma((12,)), dma((3,)), dma((2,)), dma((2,)), dma((6,)), dma((6,)), dma((20,)),
        ],
        compiler_params=pltpu.CompilerParams(
            collective_id=0, has_side_effects=True, vmem_limit_bytes=56 * 1024 * 1024
        ),
        name="main",
    )(neighbours, *operands)


def unpack_kernel(
    raw, gath, sgath,
    out, kernel_grad, cb_grad, gain_grad, nb_grad, we_grad, be_grad, wr_grad, br_grad, ls_grad,
    stage, rows_in, few_in, sem,
):
    fetches = [
        pltpu.make_async_copy(src, dst, sem.at[i])
        for i, (src, dst) in enumerate(((gath, rows_in), (sgath, few_in)))
    ]
    parts = [pl.ds(i * 2, 2) for i in range(4)]
    loads = [
        pltpu.make_async_copy(raw.at[part], stage.at[part], sem.at[2 + i])
        for i, part in enumerate(parts)
    ]
    stores = [
        pltpu.make_async_copy(stage.at[part], out.at[part], sem.at[6 + i])
        for i, part in enumerate(parts)
    ]
    for fetch in fetches + loads:
        fetch.start()
    for fetch in fetches:
        fetch.wait()
    rows = rows_in.reshape(1024, 128)
    few = few_in[...].reshape(64, 128)
    for q in range(4):
        we_grad[:, q * 128 : q * 128 + 128] = rows[q * 128 : q * 128 + 128, :].astype(F32)
        be_grad[q * 128 : q * 128 + 128] = few[54 + q]
    wr_grad[...] = rows[512:1024, :].astype(F32)
    for i in range(7):
        kernel_grad[i] = few[i * 7 : i * 7 + 7]
    for i, ref in enumerate((cb_grad, gain_grad, nb_grad, br_grad, ls_grad)):
        ref[...] = few[49 + i]
    for load, store in zip(loads, stores):
        load.wait()
        store.start()
    for store in stores:
        store.wait()


def unpack(raw, gath, sgath):
    one = lambda *shape: jax.ShapeDtypeStruct(shape, F32)
    return pl.pallas_call(
        unpack_kernel,
        out_shape=(
            jax.ShapeDtypeStruct(raw.shape, raw.dtype),
            one(7, 7, 128), one(128), one(128), one(128), one(128, 512), one(512),
            one(512, 128), one(128), one(128),
        ),
        in_specs=[ANY, ANY, ANY],
        out_specs=(ANY,) + (VMEM,) * 9,
        scratch_shapes=[
            pltpu.VMEM(raw.shape, raw.dtype),
            pltpu.VMEM(gath.shape, gath.dtype),
            pltpu.VMEM(sgath.shape, sgath.dtype),
            pltpu.SemaphoreType.DMA((10,)),
        ],
        compiler_params=pltpu.CompilerParams(vmem_limit_bytes=56 * 1024 * 1024),
        name="unpack",
    )(raw, gath, sgath)


def body(
    inputs, kernel, conv_bias, norm_gain, norm_bias, expand_weight, expand_bias,
    reduce_weight, reduce_bias, layer_scale, neighbours, cotangent,
):
    factor = 1.0 / math.sqrt(FACES * 256 * 256)
    raw, gath, sgath = run_main(
        factor, jnp.transpose(neighbours, (2, 1, 0)), inputs[0], cotangent[0], kernel, conv_bias, norm_gain, norm_bias,
        expand_weight, expand_bias, reduce_weight, reduce_bias, layer_scale,
    )
    out, *grads = unpack(raw, gath, sgath)
    return (out[None], *grads)


def solution(mesh):
    split = P("face", "tile", None, None)
    return jax.shard_map(
        body,
        mesh=mesh,
        in_specs=(split,) + (P(),) * 10 + (split,),
        out_specs=(split,) + (P(),) * 9,
        check_vma=False,
    )
```

```python
import functools
import math

import jax
import jax.numpy as jnp
from jax import lax
from jax.experimental import pallas as pl
from jax.experimental.pallas import tpu as pltpu
from jax.sharding import PartitionSpec as P

EPS = 1e-06
MESH = pl.DeviceIdType.MESH
BF = jnp.bfloat16
F32 = jnp.float32
ROOT = math.sqrt(2.0 / math.pi)
CUBE = 0.044715
FACES = 8
TILES = 32
VMEM = pl.BlockSpec(memory_space=pltpu.VMEM)
SMEM = pl.BlockSpec(memory_space=pltpu.SMEM)
ANY = pl.BlockSpec(memory_space=pl.ANY)


def place():
    return lax.axis_index("face"), lax.axis_index("tile")


def remote(src, dst, send, recv, face, tile):
    return pltpu.make_async_remote_copy(
        src_ref=src, dst_ref=dst, send_sem=send, recv_sem=recv,
        device_id=(face, tile), device_id_type=MESH,
    )


def nt(left, right):
    return lax.dot_general(left, right, (((1,), (1,)), ((), ())), preferred_element_type=F32)


def nn(left, right):
    return lax.dot_general(left, right, (((1,), (0,)), ((), ())), preferred_element_type=F32)


def one_hot(rows, cols, index):
    r = lax.broadcasted_iota(jnp.int32, (rows, cols), 0)
    c = lax.broadcasted_iota(jnp.int32, (rows, cols), 1)
    return jnp.where(c == index(r), 1.0, 0.0).astype(BF)


def fold(v):
    rows, chans = v.shape
    return jnp.sum(v.reshape(rows // 8, 8, chans), 0)


def main_kernel(
    factor,
    nbr_hbm, x_hbm, cot_hbm, kern_hbm, cb_hbm, gain_hbm, nb_hbm, we_hbm, be_hbm, wr_hbm, br_hbm, ls_hbm,
    out_hbm, gath, sgath,
    nbr, x, cot, kern, cb, gain, nb, we, be, wr, br, ls, out,
    top, bot, hbuf, side, piece, pieces, chosen, near_band, far_band, near_out, far_out,
    pad, conv, taps, act, pulled, pulled_wide, acc_e, acc_r, sums, ksum,
    big, slots1, slotsz, fin, small, sslots1, sslots2, few_ref, sfin,
    load_sem, out_sem, row_send, row_recv, side_send, side_recv, sem,
):
    f, t = place()
    last = TILES - 1
    mirror = last - t
    is_first = t == 0
    is_last = t == last
    has_up = t > 0
    has_down = t < last
    ward = lax.rem(t + 16, TILES)
    image = last - ward
    ward_up = ward > 0
    ward_down = ward < last
    image_up = jnp.logical_and(image > 0, image - 1 != t)
    image_down = jnp.logical_and(image < last, image + 1 != t)
    origin = [lax.rem(v + TILES, TILES) for v in (t + 15, t + 16, t + 17, 16 - t, 15 - t, 14 - t)]
    own3 = jnp.logical_and(has_up, origin[3] == t)
    own5 = jnp.logical_and(has_down, origin[5] == t)
    true = t >= 0
    valid = [
        has_up, true, has_down, jnp.logical_and(has_up, origin[3] != t), true,
        jnp.logical_and(has_down, origin[5] != t),
    ]
    edge = jnp.logical_or(is_first, is_last)
    hi = t // 16
    s = t % 16
    z = s // 2
    core = s % 2
    a = hi * 8 + f
    me = core * 16 + a
    twin = t + 1 - 2 * core
    others = [lax.rem(f + k, FACES) for k in range(1, FACES)]
    plane = [lax.rem(a + k, 16) for k in range(1, 16)]
    near = [lax.rem(me + k, 32) for k in range(1, 32)]
    line = [lax.rem(s + k, 16) for k in range(1, 16)]
    stack = [lax.rem(z + k, 8) for k in range(1, 8)]

    def plane_id(p):
        return lax.rem(p, 8), p // 8 * 16 + s

    def near_id(q):
        return lax.rem(q, 8), q % 16 // 8 * 16 + z * 2 + q // 16

    def drain(ref, which):
        pltpu.make_async_copy(ref, ref, sem.at[which]).wait()

    loads = [
        pltpu.make_async_copy(src, dst, load_sem.at[i])
        for i, (src, dst) in enumerate(
            (
                (x_hbm, x), (kern_hbm, kern), (cb_hbm, cb), (cot_hbm, cot), (we_hbm, we), (wr_hbm, wr),
                (nbr_hbm, nbr), (gain_hbm, gain), (nb_hbm, nb), (be_hbm, be), (br_hbm, br), (ls_hbm, ls),
            )
        )
    ]
    for load in loads:
        load.start()

    barrier = pltpu.get_barrier_semaphore()

    def hello(face, tile):
        pl.semaphore_signal(barrier, inc=1, device_id=(face, tile), device_id_type=MESH)

    @pl.when(edge)
    def _():
        for g in range(FACES):
            hello(g, mirror)

    @pl.when(has_up)
    def _():
        hello(f, t - 1)

    @pl.when(has_down)
    def _():
        hello(f, t + 1)

    for tile, cond in zip(origin, valid):

        @pl.when(cond)
        def _(tile=tile):
            hello(f, tile)

    for p in line:
        hello(f, hi * 16 + p)
    for q in near:
        hello(*near_id(q))

    loads[0].wait()
    for d in range(3):
        west = x[:, d : d + 1, :].astype(F32).reshape(8, 128)
        east = x[:, 255 - d : 256 - d, :].astype(F32).reshape(8, 128)
        piece[d] = jnp.concatenate([west, east], 0).astype(BF)
    pad[3:11, 8:264, :] = x[...].astype(F32)
    for load in loads[1:3]:
        load.wait()
    for i in range(7):
        for j in range(7):
            taps[i * 7 + j] = jnp.broadcast_to(kern[i, j : j + 1, :], (8, 128))
    bias = jnp.broadcast_to(cb[...].reshape(1, 128), (8, 128))

    def convolve(col, acc, out_rows, in_rows, base=0):
        acc = dict(zip(out_rows, acc))
        for j in range(7):
            for row in in_rows:
                hit = [r for r in out_rows if 0 <= row - r < 7]
                if hit:
                    v = pad[base + row, pl.ds(col + 5 + j, 8), :]
                    for r in hit:
                        acc[r] = acc[r] + taps[(row - r) * 7 + j] * v
        return [acc[r] for r in out_rows]

    @pl.loop(0, 7)
    def _(i):
        for u in range(4):
            col = pl.multiple_of(16 + i * 32 + u * 8, 8)
            for r, v in enumerate(convolve(col, [bias] * 8, range(8), range(3, 11))):
                conv[r, pl.ds(col, 8), :] = v

    one = lambda cond: cond.astype(jnp.int32)
    targets = one(ward_up) + one(ward_down) + one(image_up) + one(image_down) + 2
    count = 46 + one(has_up) + one(has_down) + targets + 8 * one(edge)
    pl.semaphore_wait(barrier, count)

    def columns(c):
        return pl.ds(pl.multiple_of(c * 16, 16), 16)

    def piece_copy(k, g):
        return remote(piece, pieces.at[f], sem.at[2], sem.at[3], g, ward)

    def up_copy():
        return remote(x.at[pl.ds(0, 3)], bot, row_send.at[0], row_recv.at[0], f, t - 1)

    def down_copy():
        return remote(x.at[pl.ds(5, 3)], top, row_send.at[1], row_recv.at[1], f, t + 1)

    for rows, cond in ((0, is_first), (5, is_last)):

        @pl.when(cond)
        def _(rows=rows):
            three = pl.ds(rows, 3)
            for g in others:
                remote(x.at[three, columns(g), :], near_band.at[f], sem.at[0], sem.at[1], g, t).start()
            for g in range(FACES):
                remote(
                    x.at[three, columns(g + 8), :], far_band.at[f], sem.at[18], sem.at[19], g, mirror
                ).start()
            near_band[f] = x[three, columns(f), :]

    for k, g in enumerate(others):
        piece_copy(k, g).start()

    @pl.when(has_up)
    def _():
        up_copy().start()

    @pl.when(has_down)
    def _():
        down_copy().start()

    for load in loads[3:]:
        load.wait()

    def side_copy(slot, tile):
        return remote(chosen, side.at[slot], side_send.at[slot], side_recv.at[slot], f, tile)

    routes = (
        (0, ward + 1, ward_down), (1, ward, true), (2, ward - 1, ward_up),
        (3, image + 1, image_down), (4, image, true), (5, image - 1, image_up),
    )

    def pass_sides():
        drain(pieces.at[pl.ds(0, 7)], 3)
        from_west = pieces[nbr[0, 3, f]]
        from_east = pieces[nbr[0, 1, f]]
        chosen[...] = jnp.concatenate(
            [from_west.astype(F32)[:, 8:16], from_east.astype(F32)[:, 0:8]], 1
        ).astype(BF)
        for slot, tile, cond in routes:

            @pl.when(cond)
            def _(slot=slot, tile=tile):
                side_copy(slot, tile).start()

        @pl.when(own3)
        def _():
            side[3] = chosen[...]

        @pl.when(own5)
        def _():
            side[5] = chosen[...]

    def pass_bands():
        for near_side, far_side, cond in ((0, 2, is_last), (2, 0, is_first)):

            @pl.when(cond)
            def _(near_side=near_side, far_side=far_side):
                drain(near_band.at[pl.ds(0, 7)], 1)
                for g in range(FACES):
                    near_out[g] = near_band[nbr[0, near_side, g]]
                    remote(near_out.at[g], hbuf.at[f], sem.at[4], sem.at[5], g, mirror).start()
                drain(far_band, 19)
                for k, g in enumerate(others):
                    far_out[k] = far_band[nbr[0, far_side, g]]
                    remote(far_out.at[k], hbuf.at[f + 8], sem.at[4], sem.at[5], g, t).start()
                hbuf[f + 8] = far_band[nbr[0, far_side, f]]

    def polar(flag, rows):
        drain(hbuf.at[pl.ds(0, 15)], 5)
        turn = one_hot(256, 256, lambda r: 255 - r)
        for d in range(3):
            band = jnp.concatenate([hbuf[k, d] for k in range(16)], 0)
            turned = nn(turn, band)
            pad[rows[d], 8:264, :] = jnp.where(flag == 1, turned, band.astype(F32))

    def finish(out_rows, in_rows):
        @pl.loop(0, 7)
        def _(i):
            for u in range(4):
                col = pl.multiple_of(16 + i * 32 + u * 8, 8)
                acc = [conv[r, pl.ds(col, 8), :] for r in out_rows]
                for r, v in zip(out_rows, convolve(col, acc, out_rows, in_rows)):
                    conv[r, pl.ds(col, 8), :] = v

    def finish_top():
        @pl.when(has_up)
        def _():
            down_copy().wait_recv()
            pad[0:3, 8:264, :] = top[...].astype(F32)

        @pl.when(is_first)
        def _():
            polar(nbr[2, 0, f], (0, 1, 2))

        finish(range(0, 3), range(0, 3))

    def finish_bottom():
        @pl.when(has_down)
        def _():
            up_copy().wait_recv()
            pad[11:14, 8:264, :] = bot[...].astype(F32)

        @pl.when(is_last)
        def _():
            polar(nbr[2, 2, f], (11, 12, 13))

        finish(range(5, 8), range(11, 14))

    acc_e[...] = jnp.zeros_like(acc_e)
    acc_r[...] = jnp.zeros_like(acc_r)
    sums[...] = jnp.zeros_like(sums)
    mean_of = jnp.full((128, 128), 1.0 / 128, BF)
    vec = lambda ref: ref[...].reshape(1, -1)

    def pull_back(cotangent):
        branch_cot = (cotangent.astype(F32) * vec(ls)).astype(BF)
        sums[3] += fold(branch_cot.astype(F32))
        return branch_cot, nt(branch_cot, wr[...])

    def mlp(c, pulled, rows, between=None):
        count = c.shape[0]
        centred = c - nn(c.astype(BF), mean_of)
        variance = nn((centred * centred).astype(BF), mean_of)
        inverse = lax.rsqrt(variance + EPS)
        normed = centred * inverse
        scaled = (normed * vec(gain) + vec(nb)).astype(BF)
        hidden = nn(scaled, we[...]) + vec(be)
        branch_cot, active_cot = pulled
        square = hidden * hidden
        gate = 0.5 + 0.5 * jnp.tanh(hidden * (ROOT + (ROOT * CUBE) * square))
        active = hidden * gate
        active_low = active.astype(BF)
        slope = gate + active * (1.0 - gate) * (2.0 * ROOT + (6.0 * ROOT * CUBE) * square)
        hidden_cot = (active_cot * slope).astype(BF)
        act[rows, :] = active_low
        left = jnp.concatenate([scaled.T, jnp.ones((16, count), BF)], 0)
        acc_e[...] += nn(left, hidden_cot)
        acc_r[...] += nn(branch_cot.T, active_low)
        if between is not None:
            between()
        scaled_cot = nt(hidden_cot, we[...])
        normed_cot = scaled_cot * vec(gain)
        m1 = nn(normed_cot.astype(BF), mean_of)
        m2 = nn((normed_cot * normed).astype(BF), mean_of)
        conv_cot = inverse * (normed_cot - m1 - normed * m2)
        sums[0] += fold(conv_cot)
        sums[1] += fold(scaled_cot * normed)
        sums[2] += fold(scaled_cot)
        return conv_cot

    def kernel_grad(base, rows, cols):
        steps = len(cols) // 4

        @pl.loop(0, 7)
        def _(j):
            def step(k, acc):
                acc = list(acc)
                for u in range(4):
                    col = cols[u] if steps == 1 else pl.multiple_of(cols[0] + k * 32 + u * 8, 8)
                    cots = [conv[base + r, pl.ds(col, 8), :] for r in range(rows)]
                    for row in range(rows + 6):
                        v = pad[base + row, pl.ds(col + 5 + j, 8), :]
                        for i in range(7):
                            if 0 <= row - i < rows:
                                acc[i] = acc[i] + cots[row - i] * v
                return tuple(acc)

            zero = (jnp.zeros((8, 128), F32),) * 7
            acc = step(0, zero) if steps == 1 else lax.fori_loop(0, steps, step, zero)
            for i in range(7):
                ksum[i * 7 + j] += acc[i]

    inner = range(16, 240, 8)
    low_first = t < 16
    base1 = jnp.where(low_first, 5, 0)
    base2 = 5 - base1
    base5 = jnp.where(low_first, 3, 0)
    mid, three1, three2 = pl.ds(3, 2), pl.ds(base1, 3), pl.ds(base2, 3)
    five = pl.ds(base5, 5)

    def inside(ref, rows, count):
        return ref[rows, 16:240, :].reshape(count * 224, 128)

    def outside(ref):
        return jnp.concatenate([ref[five, 0:16, :], ref[five, 240:256, :]], 1).reshape(160, 128)

    def put_outside(ref, value):
        value = value.reshape(5, 32, 128)
        ref[five, 0:16, :] = value[:, 0:16]
        ref[five, 240:256, :] = value[:, 16:32]

    got = mlp(inside(conv, mid, 2), pull_back(inside(cot, mid, 2)), pl.ds(0, 448))
    conv[mid, 16:240, :] = got.reshape(2, 224, 128)
    ksum[...] = jnp.zeros_like(ksum)
    kernel_grad(3, 2, inner)
    later = (inside(cot, three1, 3), outside(cot), cot[three2, :, :].reshape(768, 128))
    pulled[...], pulled_wide[...] = pull_back(jnp.concatenate(later, 0))
    pass_sides()

    @pl.when(low_first)
    def _():
        finish_bottom()

    @pl.when(jnp.logical_not(low_first))
    def _():
        finish_top()

    pass_bands()
    got = mlp(inside(conv, three1, 3), (pulled[0:672, :], pulled_wide[0:672, :]), pl.ds(448, 672))
    conv[three1, 16:240, :] = got.reshape(3, 224, 128)
    kernel_grad(base1, 3, inner)

    for slot, cond in enumerate(valid):

        @pl.when(cond)
        def _(slot=slot):
            side_copy(slot, origin[slot]).wait_recv()

    @pl.when(is_first)
    def _():
        side[0] = jnp.zeros((3, 16, 128), BF)
        side[3] = jnp.zeros((3, 16, 128), BF)

    @pl.when(is_last)
    def _():
        side[2] = jnp.zeros((3, 16, 128), BF)
        side[5] = jnp.zeros((3, 16, 128), BF)

    turn = one_hot(24, 24, lambda r: r // 8 * 8 + 7 - r % 8)
    for d in range(3):
        slots = [side[i, d].astype(F32) for i in range(6)]
        for first, side_id, col in ((0, 3, 7 - d), (8, 1, 264 + d)):
            straight = jnp.concatenate([slots[i][first : first + 8] for i in (0, 1, 2)], 0)
            turned = jnp.concatenate([slots[i][first : first + 8] for i in (3, 4, 5)], 0)
            turned = nn(turn, turned.astype(BF))
            halo = jnp.where(nbr[2, side_id, f] == 1, turned, straight)
            pad[0:14, col : col + 1, :] = halo[5:19].reshape(14, 1, 128)

    ends = (0, 8, 240, 248)

    def convolve_ends(base, rows):
        for col in ends:
            got = convolve(col, [bias] * rows, range(rows), range(rows + 6), base)
            for r, v in enumerate(got):
                conv[base + r, pl.ds(col, 8), :] = v

    convolve_ends(base5, 5)

    @pl.when(low_first)
    def _():
        finish_top()

    @pl.when(jnp.logical_not(low_first))
    def _():
        finish_bottom()

    convolve_ends(base2, 3)

    def send_large():
        for q in range(4):
            cols = slice(q * 128, q * 128 + 128)
            big[q * 4 : q * 4 + 4] = acc_e[0:128, cols].astype(BF).reshape(4, 32, 128)
            big[16 + q * 4 : 20 + q * 4] = acc_r[:, cols].T.astype(BF).reshape(4, 32, 128)
        for q in near:
            remote(big.at[q], slots1.at[me], sem.at[6], sem.at[7], *near_id(q)).start()

    got = mlp(
        jnp.concatenate([outside(conv), conv[three2, :, :].reshape(768, 128)], 0),
        (pulled[672:1600, :], pulled_wide[672:1600, :]), pl.ds(1120, 928), send_large,
    )
    put_outside(conv, got[0:160])
    conv[three2, :, :] = got[160:928].reshape(3, 256, 128)
    slots1[me] = big[me]

    scale = jnp.zeros((8, 128), F32)
    for q in range(4):
        cols = slice(q * 128, q * 128 + 128)
        scale = scale + fold(acc_r[:, cols].T * wr[cols, :].astype(F32))
    small[...] = jnp.zeros_like(small)
    totals = [jnp.sum(sums[i], 0, keepdims=True) for i in range(4)]
    totals.append((jnp.sum(scale, 0, keepdims=True) + vec(br) * totals[3]) / vec(ls))
    for i in range(5):
        small[49 + i : 50 + i, :] = totals[i]
    for q in range(4):
        small[54 + q : 55 + q, :] = acc_e[128:129, q * 128 : q * 128 + 128]

    kernel_grad(base2, 3, range(0, 256, 8))
    kernel_grad(base5, 5, ends)
    for i in range(49):
        small[i : i + 1, :] = jnp.sum(ksum[i], 0, keepdims=True)

    for p in plane:
        rows = pl.ds(pl.multiple_of(lax.rem(p, 8) * 8, 8), 8)
        remote(small.at[rows], sslots1.at[a], sem.at[8], sem.at[9], *plane_id(p)).start()
    sslots1[a] = small[pl.ds(pl.multiple_of(f * 8, 8), 8), :]

    def output(rows, residual):
        branch = nn(act[rows, :], wr[...]) + vec(br)
        return (residual.astype(F32) + vec(ls) * branch).astype(BF)

    def output_inside(rows, three, count):
        out[three, 16:240, :] = output(rows, inside(x, three, count)).reshape(count, 224, 128)

    output_inside(pl.ds(0, 448), mid, 2)
    output_inside(pl.ds(448, 672), three1, 3)

    drain(slots1.at[pl.ds(0, 31)], 7)
    total = slots1[0].astype(F32)
    for q in range(1, 32):
        total = total + slots1[q].astype(F32)
    slotsz[z] = total.astype(BF)
    for q in stack:
        remote(
            slotsz.at[z], slotsz.at[z], sem.at[10], sem.at[11], f, hi * 16 + q * 2 + core
        ).start()

    put_outside(out, output(pl.ds(1120, 160), outside(x)))
    got = output(pl.ds(1280, 768), x[three2, :, :].reshape(768, 128))
    out[three2, :, :] = got.reshape(3, 256, 128)
    store = pltpu.make_async_copy(out, out_hbm, out_sem.at[0])
    store.start()

    drain(sslots1.at[pl.ds(0, 15)], 9)
    few = sslots1[0]
    for p in range(1, 16):
        few = few + sslots1[p]
    few_ref[...] = few
    for p in line:
        remote(few_ref, sslots2.at[s], sem.at[12], sem.at[13], f, hi * 16 + p).start()
    sslots2[s] = few

    drain(slotsz.at[pl.ds(0, 7)], 11)
    total = slotsz[0].astype(F32)
    for q in range(1, 8):
        total = total + slotsz[q].astype(F32)
    fin[a] = (total * factor).astype(BF)
    for p in plane:
        remote(fin.at[a], fin.at[a], sem.at[14], sem.at[15], *plane_id(p)).start()

    drain(sslots2.at[pl.ds(0, 15)], 13)
    few = sslots2[0]
    for p in range(1, 16):
        few = few + sslots2[p]
    sfin[...] = few * factor
    for g in others:
        remote(sfin, sgath.at[f], sem.at[16], sem.at[17], g, t).start()
    own_small = pltpu.make_async_copy(sfin, sgath.at[f], out_sem.at[2])
    own_small.start()
    drain(fin.at[pl.ds(0, 15)], 15)
    mine = gath.at[pl.ds(pl.multiple_of(core * 16, 16), 16)]
    remote(fin, mine, sem.at[20], sem.at[21], f, twin).start()
    own = pltpu.make_async_copy(fin, mine, out_sem.at[1])
    own.start()
    drain(sgath.at[pl.ds(0, 7)], 17)
    drain(gath.at[pl.ds(0, 16)], 21)

    store.wait()
    own.wait()
    own_small.wait()
    for slot, tile, cond in routes:

        @pl.when(cond)
        def _(slot=slot, tile=tile):
            side_copy(slot, tile).wait_send()

    @pl.when(has_up)
    def _():
        up_copy().wait_send()

    @pl.when(has_down)
    def _():
        down_copy().wait_send()

    @pl.when(edge)
    def _():
        drain(near_band.at[pl.ds(0, 7)], 0)
        drain(far_band, 18)
        drain(hbuf.at[pl.ds(0, 15)], 4)

    drain(pieces.at[pl.ds(0, 7)], 2)
    drain(slots1.at[pl.ds(0, 31)], 6)
    drain(sslots1.at[pl.ds(0, 15)], 8)
    drain(slotsz.at[pl.ds(0, 7)], 10)
    drain(sslots2.at[pl.ds(0, 15)], 12)
    drain(fin.at[pl.ds(0, 15)], 14)
    drain(fin, 20)
    drain(sgath.at[pl.ds(0, 7)], 16)


def run_main(factor, neighbours, *operands):
    dma = pltpu.SemaphoreType.DMA
    shape = lambda *dims: jax.ShapeDtypeStruct(dims, BF)
    return pl.pallas_call(
        functools.partial(main_kernel, factor),
        out_shape=(
            shape(8, 256, 128),
            shape(32, 32, 128),
            jax.ShapeDtypeStruct((8, 8, 128), F32),
        ),
        in_specs=[ANY] * 12,
        out_specs=(ANY, ANY, ANY),
        scratch_shapes=[pltpu.SMEM(neighbours.shape, jnp.int32)]
        + [pltpu.VMEM(item.shape, item.dtype) for item in operands]
        + [
            pltpu.VMEM((8, 256, 128), BF),
            pltpu.VMEM((3, 256, 128), BF),
            pltpu.VMEM((3, 256, 128), BF),
            pltpu.VMEM((16, 3, 16, 128), BF),
            pltpu.VMEM((6, 3, 16, 128), BF),
            pltpu.VMEM((3, 16, 128), BF),
            pltpu.VMEM((8, 3, 16, 128), BF),
            pltpu.VMEM((3, 16, 128), BF),
            pltpu.VMEM((8, 3, 16, 128), BF),
            pltpu.VMEM((8, 3, 16, 128), BF),
            pltpu.VMEM((8, 3, 16, 128), BF),
            pltpu.VMEM((7, 3, 16, 128), BF),
            pltpu.VMEM((14, 272, 128), F32),
            pltpu.VMEM((8, 256, 128), F32),
            pltpu.VMEM((49, 8, 128), F32),
            pltpu.VMEM((2048, 512), BF),
            pltpu.VMEM((1600, 128), BF),
            pltpu.VMEM((1600, 512), F32),
            pltpu.VMEM((144, 512), F32),
            pltpu.VMEM((128, 512), F32),
            pltpu.VMEM((4, 8, 128), F32),
            pltpu.VMEM((49, 8, 128), F32),
            pltpu.VMEM((32, 32, 128), BF),
            pltpu.VMEM((32, 32, 128), BF),
            pltpu.VMEM((8, 32, 128), BF),
            pltpu.VMEM((16, 32, 128), BF),
            pltpu.VMEM((64, 128), F32),
            pltpu.VMEM((16, 8, 128), F32),
            pltpu.VMEM((16, 8, 128), F32),
            pltpu.VMEM((8, 128), F32),
            pltpu.VMEM((8, 128), F32),
            dma((12,)), dma((3,)), dma((2,)), dma((2,)), dma((6,)), dma((6,)), dma((22,)),
        ],
        compiler_params=pltpu.CompilerParams(
            collective_id=0, has_side_effects=True, vmem_limit_bytes=56 * 1024 * 1024
        ),
        name="main",
    )(neighbours, *operands)


def unpack_kernel(
    raw, gath, sgath,
    out, kernel_grad, cb_grad, gain_grad, nb_grad, we_grad, be_grad, wr_grad, br_grad, ls_grad,
    stage, rows_in, few_in, sem,
):
    fetches = [
        pltpu.make_async_copy(src, dst, sem.at[i])
        for i, (src, dst) in enumerate(((gath, rows_in), (sgath, few_in)))
    ]
    parts = [pl.ds(i * 2, 2) for i in range(4)]
    loads = [
        pltpu.make_async_copy(raw.at[part], stage.at[part], sem.at[2 + i])
        for i, part in enumerate(parts)
    ]
    stores = [
        pltpu.make_async_copy(stage.at[part], out.at[part], sem.at[6 + i])
        for i, part in enumerate(parts)
    ]
    for fetch in fetches + loads:
        fetch.start()
    for fetch in fetches:
        fetch.wait()
    rows = rows_in.reshape(1024, 128)
    few = few_in[...].reshape(64, 128)
    for q in range(4):
        we_grad[:, q * 128 : q * 128 + 128] = rows[q * 128 : q * 128 + 128, :].astype(F32)
        be_grad[q * 128 : q * 128 + 128] = few[54 + q]
    wr_grad[...] = rows[512:1024, :].astype(F32)
    for i in range(7):
        kernel_grad[i] = few[i * 7 : i * 7 + 7]
    for i, ref in enumerate((cb_grad, gain_grad, nb_grad, br_grad, ls_grad)):
        ref[...] = few[49 + i]
    for load, store in zip(loads, stores):
        load.wait()
        store.start()
    for store in stores:
        store.wait()


def unpack(raw, gath, sgath):
    one = lambda *shape: jax.ShapeDtypeStruct(shape, F32)
    return pl.pallas_call(
        unpack_kernel,
        out_shape=(
            jax.ShapeDtypeStruct(raw.shape, raw.dtype),
            one(7, 7, 128), one(128), one(128), one(128), one(128, 512), one(512),
            one(512, 128), one(128), one(128),
        ),
        in_specs=[ANY, ANY, ANY],
        out_specs=(ANY,) + (VMEM,) * 9,
        scratch_shapes=[
            pltpu.VMEM(raw.shape, raw.dtype),
            pltpu.VMEM(gath.shape, gath.dtype),
            pltpu.VMEM(sgath.shape, sgath.dtype),
            pltpu.SemaphoreType.DMA((10,)),
        ],
        compiler_params=pltpu.CompilerParams(vmem_limit_bytes=56 * 1024 * 1024),
        name="unpack",
    )(raw, gath, sgath)


def body(
    inputs, kernel, conv_bias, norm_gain, norm_bias, expand_weight, expand_bias,
    reduce_weight, reduce_bias, layer_scale, neighbours, cotangent,
):
    factor = 1.0 / math.sqrt(FACES * 256 * 256)
    raw, gath, sgath = run_main(
        factor, jnp.transpose(neighbours, (2, 1, 0)), inputs[0], cotangent[0], kernel, conv_bias, norm_gain, norm_bias,
        expand_weight, expand_bias, reduce_weight, reduce_bias, layer_scale,
    )
    out, *grads = unpack(raw, gath, sgath)
    return (out[None], *grads)


def solution(mesh):
    split = P("face", "tile", None, None)
    return jax.shard_map(
        body,
        mesh=mesh,
        in_specs=(split,) + (P(),) * 10 + (split,),
        out_specs=(split,) + (P(),) * 9,
        check_vma=False,
    )
```

```python
import functools
import math

import jax
import jax.numpy as jnp
from jax import lax
from jax.experimental import pallas as pl
from jax.experimental.pallas import tpu as pltpu
from jax.sharding import PartitionSpec as P

EPS = 1e-06
MESH = pl.DeviceIdType.MESH
BF = jnp.bfloat16
F32 = jnp.float32
ROOT = math.sqrt(2.0 / math.pi)
CUBE = 0.044715
FACES = 8
TILES = 32


def ring(step, size):
    return min(step, size - step)


FACE_STEPS = sorted(
    ((dy, dx) for dy in range(2) for dx in range(4) if dy or dx), key=lambda d: -2 * d[0] - ring(d[1], 4)
)
PLANE_STEPS = sorted(
    ((dy, dx) for dy in range(4) for dx in range(4) if dy or dx), key=lambda d: -ring(d[0], 4) - ring(d[1], 4)
)
STACK_STEPS = sorted(range(1, 8), key=lambda d: -ring(d, 8))
VMEM = pl.BlockSpec(memory_space=pltpu.VMEM)
SMEM = pl.BlockSpec(memory_space=pltpu.SMEM)
ANY = pl.BlockSpec(memory_space=pl.ANY)


def place():
    return lax.axis_index("face"), lax.axis_index("tile")


def remote(src, dst, send, recv, face, tile):
    return pltpu.make_async_remote_copy(
        src_ref=src, dst_ref=dst, send_sem=send, recv_sem=recv,
        device_id=(face, tile), device_id_type=MESH,
    )


def nt(left, right):
    return lax.dot_general(left, right, (((1,), (1,)), ((), ())), preferred_element_type=F32)


def nn(left, right):
    return lax.dot_general(left, right, (((1,), (0,)), ((), ())), preferred_element_type=F32)


def one_hot(rows, cols, index):
    r = lax.broadcasted_iota(jnp.int32, (rows, cols), 0)
    c = lax.broadcasted_iota(jnp.int32, (rows, cols), 1)
    return jnp.where(c == index(r), 1.0, 0.0).astype(BF)


def fold(v):
    rows, chans = v.shape
    return jnp.sum(v.reshape(rows // 8, 8, chans), 0)


def main_kernel(
    factor,
    nbr_hbm, x_hbm, cot_hbm, kern_hbm, cb_hbm, gain_hbm, nb_hbm, we_hbm, be_hbm, wr_hbm, br_hbm, ls_hbm,
    out_hbm, gath, sgath,
    nbr, x, cot, kern, cb, gain, nb, we, be, wr, br, ls, out,
    top, bot, hbuf, side, piece, pieces, chosen, near_band, far_band, near_out, far_out,
    pad, conv, taps, act, pulled, pulled_wide, acc_e, acc_r, sums, ksum,
    big, slots1, slotsz, fin, small, sslots1, sslots2, few_ref, sfin,
    load_sem, out_sem, row_send, row_recv, side_send, side_recv, sem,
):
    f, t = place()
    last = TILES - 1
    mirror = last - t
    is_first = t == 0
    is_last = t == last
    has_up = t > 0
    has_down = t < last
    ward = lax.rem(t + 16, TILES)
    image = last - ward
    ward_up = ward > 0
    ward_down = ward < last
    image_up = jnp.logical_and(image > 0, image - 1 != t)
    image_down = jnp.logical_and(image < last, image + 1 != t)
    origin = [lax.rem(v + TILES, TILES) for v in (t + 15, t + 16, t + 17, 16 - t, 15 - t, 14 - t)]
    own3 = jnp.logical_and(has_up, origin[3] == t)
    own5 = jnp.logical_and(has_down, origin[5] == t)
    true = t >= 0
    valid = [
        has_up, true, has_down, jnp.logical_and(has_up, origin[3] != t), true,
        jnp.logical_and(has_down, origin[5] != t),
    ]
    edge = jnp.logical_or(is_first, is_last)
    hi = t // 16
    s = t % 16
    z = s // 2
    core = s % 2
    a = hi * 8 + f
    me = core * 16 + a
    twin = t + 1 - 2 * core
    yh, across = f // 4, f % 4
    row = yh * 2 + hi

    def plane_at(dy, dx):
        to = lax.rem(row + dy, 4)
        return to % 2 * 8 + to // 2 * 4 + lax.rem(across + dx, 4)

    others = [lax.rem(yh + dy, 2) * 4 + lax.rem(across + dx, 4) for dy, dx in FACE_STEPS]
    plane = [plane_at(dy, dx) for dy, dx in PLANE_STEPS]
    near = [c * 16 + p for p in plane for c in (core, 1 - core)] + [(1 - core) * 16 + a]
    stack = [lax.rem(z + dz, 8) for dz in STACK_STEPS]
    line = [q * 2 + c for q in stack for c in (core, 1 - core)] + [z * 2 + 1 - core]

    def plane_id(p):
        return lax.rem(p, 8), p // 8 * 16 + s

    def near_id(q):
        return lax.rem(q, 8), q % 16 // 8 * 16 + z * 2 + q // 16

    def drain(ref, which):
        pltpu.make_async_copy(ref, ref, sem.at[which]).wait()

    loads = [
        pltpu.make_async_copy(src, dst, load_sem.at[i])
        for i, (src, dst) in enumerate(
            (
                (x_hbm, x), (kern_hbm, kern), (cb_hbm, cb), (cot_hbm, cot), (we_hbm, we), (wr_hbm, wr),
                (nbr_hbm, nbr), (gain_hbm, gain), (nb_hbm, nb), (be_hbm, be), (br_hbm, br), (ls_hbm, ls),
            )
        )
    ]
    for load in loads:
        load.start()

    barrier = pltpu.get_barrier_semaphore()

    def hello(face, tile):
        pl.semaphore_signal(barrier, inc=1, device_id=(face, tile), device_id_type=MESH)

    @pl.when(edge)
    def _():
        for g in range(FACES):
            hello(g, mirror)

    @pl.when(has_up)
    def _():
        hello(f, t - 1)

    @pl.when(has_down)
    def _():
        hello(f, t + 1)

    for tile, cond in zip(origin, valid):

        @pl.when(cond)
        def _(tile=tile):
            hello(f, tile)

    for p in line:
        hello(f, hi * 16 + p)
    for q in near:
        hello(*near_id(q))

    loads[0].wait()
    for d in range(3):
        west = x[:, d : d + 1, :].astype(F32).reshape(8, 128)
        east = x[:, 255 - d : 256 - d, :].astype(F32).reshape(8, 128)
        piece[d] = jnp.concatenate([west, east], 0).astype(BF)
    pad[3:11, 8:264, :] = x[...].astype(F32)
    for load in loads[1:3]:
        load.wait()
    for i in range(7):
        for j in range(7):
            taps[i * 7 + j] = jnp.broadcast_to(kern[i, j : j + 1, :], (8, 128))
    bias = jnp.broadcast_to(cb[...].reshape(1, 128), (8, 128))

    def convolve(col, acc, out_rows, in_rows, base=0):
        acc = dict(zip(out_rows, acc))
        for j in range(7):
            for row in in_rows:
                hit = [r for r in out_rows if 0 <= row - r < 7]
                if hit:
                    v = pad[base + row, pl.ds(col + 5 + j, 8), :]
                    for r in hit:
                        acc[r] = acc[r] + taps[(row - r) * 7 + j] * v
        return [acc[r] for r in out_rows]

    @pl.loop(0, 7)
    def _(i):
        for u in range(4):
            col = pl.multiple_of(16 + i * 32 + u * 8, 8)
            for r, v in enumerate(convolve(col, [bias] * 8, range(8), range(3, 11))):
                conv[r, pl.ds(col, 8), :] = v

    one = lambda cond: cond.astype(jnp.int32)
    targets = one(ward_up) + one(ward_down) + one(image_up) + one(image_down) + 2
    count = 46 + one(has_up) + one(has_down) + targets + 8 * one(edge)
    pl.semaphore_wait(barrier, count)

    def columns(c):
        return pl.ds(pl.multiple_of(c * 16, 16), 16)

    def piece_copy(k, g):
        return remote(piece, pieces.at[f], sem.at[2], sem.at[3], g, ward)

    def up_copy():
        return remote(x.at[pl.ds(0, 3)], bot, row_send.at[0], row_recv.at[0], f, t - 1)

    def down_copy():
        return remote(x.at[pl.ds(5, 3)], top, row_send.at[1], row_recv.at[1], f, t + 1)

    for rows, cond in ((0, is_first), (5, is_last)):

        @pl.when(cond)
        def _(rows=rows):
            three = pl.ds(rows, 3)
            for g in others:
                remote(x.at[three, columns(g), :], near_band.at[f], sem.at[0], sem.at[1], g, t).start()
            for g in others + [f]:
                remote(
                    x.at[three, columns(g + 8), :], far_band.at[f], sem.at[18], sem.at[19], g, mirror
                ).start()
            near_band[f] = x[three, columns(f), :]

    for k, g in enumerate(others):
        piece_copy(k, g).start()

    @pl.when(has_up)
    def _():
        up_copy().start()

    @pl.when(has_down)
    def _():
        down_copy().start()

    for load in loads[3:]:
        load.wait()

    def side_copy(slot, tile):
        return remote(chosen, side.at[slot], side_send.at[slot], side_recv.at[slot], f, tile)

    routes = (
        (0, ward + 1, ward_down), (1, ward, true), (2, ward - 1, ward_up),
        (3, image + 1, image_down), (4, image, true), (5, image - 1, image_up),
    )

    def pass_sides():
        drain(pieces.at[pl.ds(0, 7)], 3)
        from_west = pieces[nbr[0, 3, f]]
        from_east = pieces[nbr[0, 1, f]]
        chosen[...] = jnp.concatenate(
            [from_west.astype(F32)[:, 8:16], from_east.astype(F32)[:, 0:8]], 1
        ).astype(BF)
        for slot, tile, cond in routes:

            @pl.when(cond)
            def _(slot=slot, tile=tile):
                side_copy(slot, tile).start()

        @pl.when(own3)
        def _():
            side[3] = chosen[...]

        @pl.when(own5)
        def _():
            side[5] = chosen[...]

    def pass_bands():
        for near_side, far_side, cond in ((0, 2, is_last), (2, 0, is_first)):

            @pl.when(cond)
            def _(near_side=near_side, far_side=far_side):
                drain(near_band.at[pl.ds(0, 7)], 1)
                for g in others + [f]:
                    near_out[g] = near_band[nbr[0, near_side, g]]
                    remote(near_out.at[g], hbuf.at[f], sem.at[4], sem.at[5], g, mirror).start()
                drain(far_band, 19)
                for k, g in enumerate(others):
                    far_out[k] = far_band[nbr[0, far_side, g]]
                    remote(far_out.at[k], hbuf.at[f + 8], sem.at[4], sem.at[5], g, t).start()
                hbuf[f + 8] = far_band[nbr[0, far_side, f]]

    def polar(flag, rows):
        drain(hbuf.at[pl.ds(0, 15)], 5)
        turn = one_hot(256, 256, lambda r: 255 - r)
        for d in range(3):
            band = jnp.concatenate([hbuf[k, d] for k in range(16)], 0)
            turned = nn(turn, band)
            pad[rows[d], 8:264, :] = jnp.where(flag == 1, turned, band.astype(F32))

    def finish(out_rows, in_rows):
        @pl.loop(0, 7)
        def _(i):
            for u in range(4):
                col = pl.multiple_of(16 + i * 32 + u * 8, 8)
                acc = [conv[r, pl.ds(col, 8), :] for r in out_rows]
                for r, v in zip(out_rows, convolve(col, acc, out_rows, in_rows)):
                    conv[r, pl.ds(col, 8), :] = v

    def finish_top():
        @pl.when(has_up)
        def _():
            down_copy().wait_recv()
            pad[0:3, 8:264, :] = top[...].astype(F32)

        @pl.when(is_first)
        def _():
            polar(nbr[2, 0, f], (0, 1, 2))

        finish(range(0, 3), range(0, 3))

    def finish_bottom():
        @pl.when(has_down)
        def _():
            up_copy().wait_recv()
            pad[11:14, 8:264, :] = bot[...].astype(F32)

        @pl.when(is_last)
        def _():
            polar(nbr[2, 2, f], (11, 12, 13))

        finish(range(5, 8), range(11, 14))

    acc_e[...] = jnp.zeros_like(acc_e)
    acc_r[...] = jnp.zeros_like(acc_r)
    sums[...] = jnp.zeros_like(sums)
    mean_of = jnp.full((128, 128), 1.0 / 128, BF)
    vec = lambda ref: ref[...].reshape(1, -1)

    def pull_back(cotangent):
        branch_cot = (cotangent.astype(F32) * vec(ls)).astype(BF)
        sums[3] += fold(branch_cot.astype(F32))
        return branch_cot, nt(branch_cot, wr[...])

    def mlp(c, pulled, rows, between=None):
        count = c.shape[0]
        centred = c - nn(c.astype(BF), mean_of)
        variance = nn((centred * centred).astype(BF), mean_of)
        inverse = lax.rsqrt(variance + EPS)
        normed = centred * inverse
        scaled = (normed * vec(gain) + vec(nb)).astype(BF)
        hidden = nn(scaled, we[...]) + vec(be)
        branch_cot, active_cot = pulled
        square = hidden * hidden
        gate = 0.5 + 0.5 * jnp.tanh(hidden * (ROOT + (ROOT * CUBE) * square))
        active = hidden * gate
        active_low = active.astype(BF)
        slope = gate + active * (1.0 - gate) * (2.0 * ROOT + (6.0 * ROOT * CUBE) * square)
        hidden_cot = (active_cot * slope).astype(BF)
        act[rows, :] = active_low
        left = jnp.concatenate([scaled.T, jnp.ones((16, count), BF)], 0)
        acc_e[...] += nn(left, hidden_cot)
        acc_r[...] += nn(branch_cot.T, active_low)
        if between is not None:
            between()
        scaled_cot = nt(hidden_cot, we[...])
        normed_cot = scaled_cot * vec(gain)
        m1 = nn(normed_cot.astype(BF), mean_of)
        m2 = nn((normed_cot * normed).astype(BF), mean_of)
        conv_cot = inverse * (normed_cot - m1 - normed * m2)
        sums[0] += fold(conv_cot)
        sums[1] += fold(scaled_cot * normed)
        sums[2] += fold(scaled_cot)
        return conv_cot

    def kernel_grad(base, rows, cols):
        steps = len(cols) // 4

        @pl.loop(0, 7)
        def _(j):
            def step(k, acc):
                acc = list(acc)
                for u in range(4):
                    col = cols[u] if steps == 1 else pl.multiple_of(cols[0] + k * 32 + u * 8, 8)
                    cots = [conv[base + r, pl.ds(col, 8), :] for r in range(rows)]
                    for row in range(rows + 6):
                        v = pad[base + row, pl.ds(col + 5 + j, 8), :]
                        for i in range(7):
                            if 0 <= row - i < rows:
                                acc[i] = acc[i] + cots[row - i] * v
                return tuple(acc)

            zero = (jnp.zeros((8, 128), F32),) * 7
            acc = step(0, zero) if steps == 1 else lax.fori_loop(0, steps, step, zero)
            for i in range(7):
                ksum[i * 7 + j] += acc[i]

    inner = range(16, 240, 8)
    low_first = t < 16
    base1 = jnp.where(low_first, 5, 0)
    base2 = 5 - base1
    base5 = jnp.where(low_first, 3, 0)
    mid, three1, three2 = pl.ds(3, 2), pl.ds(base1, 3), pl.ds(base2, 3)
    five = pl.ds(base5, 5)

    def inside(ref, rows, count):
        return ref[rows, 16:240, :].reshape(count * 224, 128)

    def outside(ref):
        return jnp.concatenate([ref[five, 0:16, :], ref[five, 240:256, :]], 1).reshape(160, 128)

    def put_outside(ref, value):
        value = value.reshape(5, 32, 128)
        ref[five, 0:16, :] = value[:, 0:16]
        ref[five, 240:256, :] = value[:, 16:32]

    got = mlp(inside(conv, mid, 2), pull_back(inside(cot, mid, 2)), pl.ds(0, 448))
    conv[mid, 16:240, :] = got.reshape(2, 224, 128)
    ksum[...] = jnp.zeros_like(ksum)
    kernel_grad(3, 2, inner)
    later = (inside(cot, three1, 3), outside(cot), cot[three2, :, :].reshape(768, 128))
    pulled[...], pulled_wide[...] = pull_back(jnp.concatenate(later, 0))
    pass_sides()

    @pl.when(low_first)
    def _():
        finish_bottom()

    @pl.when(jnp.logical_not(low_first))
    def _():
        finish_top()

    pass_bands()
    got = mlp(inside(conv, three1, 3), (pulled[0:672, :], pulled_wide[0:672, :]), pl.ds(448, 672))
    conv[three1, 16:240, :] = got.reshape(3, 224, 128)
    kernel_grad(base1, 3, inner)

    for slot, cond in enumerate(valid):

        @pl.when(cond)
        def _(slot=slot):
            side_copy(slot, origin[slot]).wait_recv()

    @pl.when(is_first)
    def _():
        side[0] = jnp.zeros((3, 16, 128), BF)
        side[3] = jnp.zeros((3, 16, 128), BF)

    @pl.when(is_last)
    def _():
        side[2] = jnp.zeros((3, 16, 128), BF)
        side[5] = jnp.zeros((3, 16, 128), BF)

    turn = one_hot(24, 24, lambda r: r // 8 * 8 + 7 - r % 8)
    for d in range(3):
        slots = [side[i, d].astype(F32) for i in range(6)]
        for first, side_id, col in ((0, 3, 7 - d), (8, 1, 264 + d)):
            straight = jnp.concatenate([slots[i][first : first + 8] for i in (0, 1, 2)], 0)
            turned = jnp.concatenate([slots[i][first : first + 8] for i in (3, 4, 5)], 0)
            turned = nn(turn, turned.astype(BF))
            halo = jnp.where(nbr[2, side_id, f] == 1, turned, straight)
            pad[0:14, col : col + 1, :] = halo[5:19].reshape(14, 1, 128)

    ends = (0, 8, 240, 248)

    def convolve_ends(base, rows):
        for col in ends:
            got = convolve(col, [bias] * rows, range(rows), range(rows + 6), base)
            for r, v in enumerate(got):
                conv[base + r, pl.ds(col, 8), :] = v

    convolve_ends(base5, 5)

    @pl.when(edge)
    def _():
        put_outside(conv, mlp(outside(conv), (pulled[672:832, :], pulled_wide[672:832, :]), pl.ds(1120, 160)))
        kernel_grad(base5, 5, ends)

    @pl.when(low_first)
    def _():
        finish_top()

    @pl.when(jnp.logical_not(low_first))
    def _():
        finish_bottom()

    convolve_ends(base2, 3)

    def send_large():
        for q in range(4):
            cols = slice(q * 128, q * 128 + 128)
            big[q * 4 : q * 4 + 4] = acc_e[0:128, cols].astype(BF).reshape(4, 32, 128)
            big[16 + q * 4 : 20 + q * 4] = acc_r[:, cols].T.astype(BF).reshape(4, 32, 128)
        for q in near:
            remote(big.at[q], slots1.at[me], sem.at[6], sem.at[7], *near_id(q)).start()

    def last_rows():
        return conv[three2, :, :].reshape(768, 128)

    @pl.when(edge)
    def _():
        got = mlp(last_rows(), (pulled[832:1600, :], pulled_wide[832:1600, :]), pl.ds(1280, 768), send_large)
        conv[three2, :, :] = got.reshape(3, 256, 128)

    @pl.when(jnp.logical_not(edge))
    def _():
        got = mlp(
            jnp.concatenate([outside(conv), last_rows()], 0),
            (pulled[672:1600, :], pulled_wide[672:1600, :]), pl.ds(1120, 928), send_large,
        )
        put_outside(conv, got[0:160])
        conv[three2, :, :] = got[160:928].reshape(3, 256, 128)

    slots1[me] = big[me]

    scale = jnp.zeros((8, 128), F32)
    for q in range(4):
        cols = slice(q * 128, q * 128 + 128)
        scale = scale + fold(acc_r[:, cols].T * wr[cols, :].astype(F32))
    small[...] = jnp.zeros_like(small)
    totals = [jnp.sum(sums[i], 0, keepdims=True) for i in range(4)]
    totals.append((jnp.sum(scale, 0, keepdims=True) + vec(br) * totals[3]) / vec(ls))
    for i in range(5):
        small[49 + i : 50 + i, :] = totals[i]
    for q in range(4):
        small[54 + q : 55 + q, :] = acc_e[128:129, q * 128 : q * 128 + 128]

    kernel_grad(base2, 3, range(0, 256, 8))

    @pl.when(jnp.logical_not(edge))
    def _():
        kernel_grad(base5, 5, ends)

    for i in range(49):
        small[i : i + 1, :] = jnp.sum(ksum[i], 0, keepdims=True)

    for p in plane:
        rows = pl.ds(pl.multiple_of(lax.rem(p, 8) * 8, 8), 8)
        remote(small.at[rows], sslots1.at[a], sem.at[8], sem.at[9], *plane_id(p)).start()
    sslots1[a] = small[pl.ds(pl.multiple_of(f * 8, 8), 8), :]

    def output(rows, residual):
        branch = nn(act[rows, :], wr[...]) + vec(br)
        return (residual.astype(F32) + vec(ls) * branch).astype(BF)

    def output_inside(rows, three, count):
        out[three, 16:240, :] = output(rows, inside(x, three, count)).reshape(count, 224, 128)

    output_inside(pl.ds(0, 448), mid, 2)
    output_inside(pl.ds(448, 672), three1, 3)

    drain(slots1.at[pl.ds(0, 31)], 7)
    total = slots1[0].astype(F32)
    for q in range(1, 32):
        total = total + slots1[q].astype(F32)
    slotsz[z] = total.astype(BF)
    for q in stack:
        remote(
            slotsz.at[z], slotsz.at[z], sem.at[10], sem.at[11], f, hi * 16 + q * 2 + core
        ).start()

    put_outside(out, output(pl.ds(1120, 160), outside(x)))
    got = output(pl.ds(1280, 768), x[three2, :, :].reshape(768, 128))
    out[three2, :, :] = got.reshape(3, 256, 128)
    store = pltpu.make_async_copy(out, out_hbm, out_sem.at[0])
    store.start()

    drain(sslots1.at[pl.ds(0, 15)], 9)
    few = sslots1[0]
    for p in range(1, 16):
        few = few + sslots1[p]
    few_ref[...] = few
    for p in line:
        remote(few_ref, sslots2.at[s], sem.at[12], sem.at[13], f, hi * 16 + p).start()
    sslots2[s] = few

    drain(slotsz.at[pl.ds(0, 7)], 11)
    total = slotsz[0].astype(F32)
    for q in range(1, 8):
        total = total + slotsz[q].astype(F32)
    fin[a] = (total * factor).astype(BF)
    for p in plane:
        remote(fin.at[a], fin.at[a], sem.at[14], sem.at[15], *plane_id(p)).start()

    drain(sslots2.at[pl.ds(0, 15)], 13)
    few = sslots2[0]
    for p in range(1, 16):
        few = few + sslots2[p]
    sfin[...] = few * factor
    for g in others:
        remote(sfin, sgath.at[f], sem.at[16], sem.at[17], g, t).start()
    own_small = pltpu.make_async_copy(sfin, sgath.at[f], out_sem.at[2])
    own_small.start()
    drain(fin.at[pl.ds(0, 15)], 15)
    mine = gath.at[pl.ds(pl.multiple_of(core * 16, 16), 16)]
    remote(fin, mine, sem.at[20], sem.at[21], f, twin).start()
    own = pltpu.make_async_copy(fin, mine, out_sem.at[1])
    own.start()
    drain(sgath.at[pl.ds(0, 7)], 17)
    drain(gath.at[pl.ds(0, 16)], 21)

    store.wait()
    own.wait()
    own_small.wait()
    for slot, tile, cond in routes:

        @pl.when(cond)
        def _(slot=slot, tile=tile):
            side_copy(slot, tile).wait_send()

    @pl.when(has_up)
    def _():
        up_copy().wait_send()

    @pl.when(has_down)
    def _():
        down_copy().wait_send()

    @pl.when(edge)
    def _():
        drain(near_band.at[pl.ds(0, 7)], 0)
        drain(far_band, 18)
        drain(hbuf.at[pl.ds(0, 15)], 4)

    drain(pieces.at[pl.ds(0, 7)], 2)
    drain(slots1.at[pl.ds(0, 31)], 6)
    drain(sslots1.at[pl.ds(0, 15)], 8)
    drain(slotsz.at[pl.ds(0, 7)], 10)
    drain(sslots2.at[pl.ds(0, 15)], 12)
    drain(fin.at[pl.ds(0, 15)], 14)
    drain(fin, 20)
    drain(sgath.at[pl.ds(0, 7)], 16)


def run_main(factor, neighbours, *operands):
    dma = pltpu.SemaphoreType.DMA
    shape = lambda *dims: jax.ShapeDtypeStruct(dims, BF)
    return pl.pallas_call(
        functools.partial(main_kernel, factor),
        out_shape=(
            shape(8, 256, 128),
            shape(32, 32, 128),
            jax.ShapeDtypeStruct((8, 8, 128), F32),
        ),
        in_specs=[ANY] * 12,
        out_specs=(ANY, ANY, ANY),
        scratch_shapes=[pltpu.SMEM(neighbours.shape, jnp.int32)]
        + [pltpu.VMEM(item.shape, item.dtype) for item in operands]
        + [
            pltpu.VMEM((8, 256, 128), BF),
            pltpu.VMEM((3, 256, 128), BF),
            pltpu.VMEM((3, 256, 128), BF),
            pltpu.VMEM((16, 3, 16, 128), BF),
            pltpu.VMEM((6, 3, 16, 128), BF),
            pltpu.VMEM((3, 16, 128), BF),
            pltpu.VMEM((8, 3, 16, 128), BF),
            pltpu.VMEM((3, 16, 128), BF),
            pltpu.VMEM((8, 3, 16, 128), BF),
            pltpu.VMEM((8, 3, 16, 128), BF),
            pltpu.VMEM((8, 3, 16, 128), BF),
            pltpu.VMEM((7, 3, 16, 128), BF),
            pltpu.VMEM((14, 272, 128), F32),
            pltpu.VMEM((8, 256, 128), F32),
            pltpu.VMEM((49, 8, 128), F32),
            pltpu.VMEM((2048, 512), BF),
            pltpu.VMEM((1600, 128), BF),
            pltpu.VMEM((1600, 512), F32),
            pltpu.VMEM((144, 512), F32),
            pltpu.VMEM((128, 512), F32),
            pltpu.VMEM((4, 8, 128), F32),
            pltpu.VMEM((49, 8, 128), F32),
            pltpu.VMEM((32, 32, 128), BF),
            pltpu.VMEM((32, 32, 128), BF),
            pltpu.VMEM((8, 32, 128), BF),
            pltpu.VMEM((16, 32, 128), BF),
            pltpu.VMEM((64, 128), F32),
            pltpu.VMEM((16, 8, 128), F32),
            pltpu.VMEM((16, 8, 128), F32),
            pltpu.VMEM((8, 128), F32),
            pltpu.VMEM((8, 128), F32),
            dma((12,)), dma((3,)), dma((2,)), dma((2,)), dma((6,)), dma((6,)), dma((22,)),
        ],
        compiler_params=pltpu.CompilerParams(
            collective_id=0, has_side_effects=True, vmem_limit_bytes=56 * 1024 * 1024
        ),
        name="main",
    )(neighbours, *operands)


def unpack_kernel(
    raw, gath, sgath,
    out, kernel_grad, cb_grad, gain_grad, nb_grad, we_grad, be_grad, wr_grad, br_grad, ls_grad,
    stage, rows_in, few_in, sem,
):
    fetches = [
        pltpu.make_async_copy(src, dst, sem.at[i])
        for i, (src, dst) in enumerate(((gath, rows_in), (sgath, few_in)))
    ]
    parts = [pl.ds(i * 2, 2) for i in range(4)]
    loads = [
        pltpu.make_async_copy(raw.at[part], stage.at[part], sem.at[2 + i])
        for i, part in enumerate(parts)
    ]
    stores = [
        pltpu.make_async_copy(stage.at[part], out.at[part], sem.at[6 + i])
        for i, part in enumerate(parts)
    ]
    for fetch in fetches + loads:
        fetch.start()
    for fetch in fetches:
        fetch.wait()
    rows = rows_in.reshape(1024, 128)
    few = few_in[...].reshape(64, 128)
    for q in range(4):
        we_grad[:, q * 128 : q * 128 + 128] = rows[q * 128 : q * 128 + 128, :].astype(F32)
        be_grad[q * 128 : q * 128 + 128] = few[54 + q]
    wr_grad[...] = rows[512:1024, :].astype(F32)
    for i in range(7):
        kernel_grad[i] = few[i * 7 : i * 7 + 7]
    for i, ref in enumerate((cb_grad, gain_grad, nb_grad, br_grad, ls_grad)):
        ref[...] = few[49 + i]
    for load, store in zip(loads, stores):
        load.wait()
        store.start()
    for store in stores:
        store.wait()


def unpack(raw, gath, sgath):
    one = lambda *shape: jax.ShapeDtypeStruct(shape, F32)
    return pl.pallas_call(
        unpack_kernel,
        out_shape=(
            jax.ShapeDtypeStruct(raw.shape, raw.dtype),
            one(7, 7, 128), one(128), one(128), one(128), one(128, 512), one(512),
            one(512, 128), one(128), one(128),
        ),
        in_specs=[ANY, ANY, ANY],
        out_specs=(ANY,) + (VMEM,) * 9,
        scratch_shapes=[
            pltpu.VMEM(raw.shape, raw.dtype),
            pltpu.VMEM(gath.shape, gath.dtype),
            pltpu.VMEM(sgath.shape, sgath.dtype),
            pltpu.SemaphoreType.DMA((10,)),
        ],
        compiler_params=pltpu.CompilerParams(vmem_limit_bytes=56 * 1024 * 1024),
        name="unpack",
    )(raw, gath, sgath)


def body(
    inputs, kernel, conv_bias, norm_gain, norm_bias, expand_weight, expand_bias,
    reduce_weight, reduce_bias, layer_scale, neighbours, cotangent,
):
    factor = 1.0 / math.sqrt(FACES * 256 * 256)
    raw, gath, sgath = run_main(
        factor, jnp.transpose(neighbours, (2, 1, 0)), inputs[0], cotangent[0], kernel, conv_bias, norm_gain, norm_bias,
        expand_weight, expand_bias, reduce_weight, reduce_bias, layer_scale,
    )
    out, *grads = unpack(raw, gath, sgath)
    return (out[None], *grads)


def solution(mesh):
    split = P("face", "tile", None, None)
    return jax.shard_map(
        body,
        mesh=mesh,
        in_specs=(split,) + (P(),) * 10 + (split,),
        out_specs=(split,) + (P(),) * 9,
        check_vma=False,
    )
```

```python
import functools
import math

import jax
import jax.numpy as jnp
from jax import lax
from jax.experimental import pallas as pl
from jax.experimental.pallas import tpu as pltpu
from jax.sharding import PartitionSpec as P

EPS = 1e-06
MESH = pl.DeviceIdType.MESH
BF = jnp.bfloat16
F32 = jnp.float32
ROOT = math.sqrt(2.0 / math.pi)
CUBE = 0.044715
FACES = 8
TILES = 32


def ring(step, size):
    return min(step, size - step)


FACE_STEPS = sorted(
    ((dy, dx) for dy in range(2) for dx in range(4) if dy or dx), key=lambda d: -2 * d[0] - ring(d[1], 4)
)
PLANE_STEPS = sorted(
    ((dy, dx) for dy in range(4) for dx in range(4) if dy or dx), key=lambda d: -ring(d[0], 4) - ring(d[1], 4)
)
STACK_STEPS = sorted(range(1, 8), key=lambda d: -ring(d, 8))
VMEM = pl.BlockSpec(memory_space=pltpu.VMEM)
SMEM = pl.BlockSpec(memory_space=pltpu.SMEM)
ANY = pl.BlockSpec(memory_space=pl.ANY)


def place():
    return lax.axis_index("face"), lax.axis_index("tile")


def remote(src, dst, send, recv, face, tile):
    return pltpu.make_async_remote_copy(
        src_ref=src, dst_ref=dst, send_sem=send, recv_sem=recv,
        device_id=(face, tile), device_id_type=MESH,
    )


def nt(left, right):
    return lax.dot_general(left, right, (((1,), (1,)), ((), ())), preferred_element_type=F32)


def nn(left, right):
    return lax.dot_general(left, right, (((1,), (0,)), ((), ())), preferred_element_type=F32)


def one_hot(rows, cols, index):
    r = lax.broadcasted_iota(jnp.int32, (rows, cols), 0)
    c = lax.broadcasted_iota(jnp.int32, (rows, cols), 1)
    return jnp.where(c == index(r), 1.0, 0.0).astype(BF)


def fold(v):
    rows, chans = v.shape
    return jnp.sum(v.reshape(rows // 8, 8, chans), 0)


def main_kernel(
    factor,
    nbr_hbm, x_hbm, cot_hbm, kern_hbm, cb_hbm, gain_hbm, nb_hbm, we_hbm, be_hbm, wr_hbm, br_hbm, ls_hbm,
    out_hbm, gath, sgath,
    nbr, x, cot, kern, cb, gain, nb, we, be, wr, br, ls, out,
    top, bot, hbuf, side, piece, pieces, chosen, near_band, far_band, near_out, far_out,
    pad, conv, taps, act, pulled, pulled_wide, acc_e, acc_r, sums, ksum,
    big, slots1, slotsz, fin, small, few_half, fews, fewz, sfin,
    load_sem, out_sem, row_send, row_recv, side_send, side_recv, sem,
):
    f, t = place()
    last = TILES - 1
    mirror = last - t
    is_first = t == 0
    is_last = t == last
    has_up = t > 0
    has_down = t < last
    ward = lax.rem(t + 16, TILES)
    image = last - ward
    ward_up = ward > 0
    ward_down = ward < last
    image_up = jnp.logical_and(image > 0, image - 1 != t)
    image_down = jnp.logical_and(image < last, image + 1 != t)
    origin = [lax.rem(v + TILES, TILES) for v in (t + 15, t + 16, t + 17, 16 - t, 15 - t, 14 - t)]
    own3 = jnp.logical_and(has_up, origin[3] == t)
    own5 = jnp.logical_and(has_down, origin[5] == t)
    true = t >= 0
    valid = [
        has_up, true, has_down, jnp.logical_and(has_up, origin[3] != t), true,
        jnp.logical_and(has_down, origin[5] != t),
    ]
    edge = jnp.logical_or(is_first, is_last)
    hi = t // 16
    s = t % 16
    z = s // 2
    core = s % 2
    a = hi * 8 + f
    me = core * 16 + a
    twin = t + 1 - 2 * core
    yh, across = f // 4, f % 4
    row = yh * 2 + hi

    def plane_at(dy, dx):
        to = lax.rem(row + dy, 4)
        return to % 2 * 8 + to // 2 * 4 + lax.rem(across + dx, 4)

    others = [lax.rem(yh + dy, 2) * 4 + lax.rem(across + dx, 4) for dy, dx in FACE_STEPS]
    plane = [plane_at(dy, dx) for dy, dx in PLANE_STEPS]
    near = [c * 16 + p for p in plane for c in (core, 1 - core)] + [(1 - core) * 16 + a]
    stack = [lax.rem(z + dz, 8) for dz in STACK_STEPS]
    line = [q * 2 + c for q in stack for c in (core, 1 - core)] + [z * 2 + 1 - core]

    def plane_id(p):
        return lax.rem(p, 8), p // 8 * 16 + s

    def near_id(q):
        return lax.rem(q, 8), q % 16 // 8 * 16 + z * 2 + q // 16

    def drain(ref, which):
        pltpu.make_async_copy(ref, ref, sem.at[which]).wait()

    loads = [
        pltpu.make_async_copy(src, dst, load_sem.at[i])
        for i, (src, dst) in enumerate(
            (
                (x_hbm, x), (kern_hbm, kern), (cb_hbm, cb), (cot_hbm, cot), (we_hbm, we), (wr_hbm, wr),
                (nbr_hbm, nbr), (gain_hbm, gain), (nb_hbm, nb), (be_hbm, be), (br_hbm, br), (ls_hbm, ls),
            )
        )
    ]
    for load in loads:
        load.start()

    barrier = pltpu.get_barrier_semaphore()

    def hello(face, tile):
        pl.semaphore_signal(barrier, inc=1, device_id=(face, tile), device_id_type=MESH)

    @pl.when(edge)
    def _():
        for g in range(FACES):
            hello(g, mirror)

    @pl.when(has_up)
    def _():
        hello(f, t - 1)

    @pl.when(has_down)
    def _():
        hello(f, t + 1)

    for tile, cond in zip(origin, valid):

        @pl.when(cond)
        def _(tile=tile):
            hello(f, tile)

    for p in line:
        hello(f, hi * 16 + p)
    for q in near:
        hello(*near_id(q))

    loads[0].wait()
    for d in range(3):
        west = x[:, d : d + 1, :].astype(F32).reshape(8, 128)
        east = x[:, 255 - d : 256 - d, :].astype(F32).reshape(8, 128)
        piece[d] = jnp.concatenate([west, east], 0).astype(BF)
    pad[3:11, 8:264, :] = x[...].astype(F32)
    for load in loads[1:3]:
        load.wait()
    for i in range(7):
        for j in range(7):
            taps[i * 7 + j] = jnp.broadcast_to(kern[i, j : j + 1, :], (8, 128))
    bias = jnp.broadcast_to(cb[...].reshape(1, 128), (8, 128))

    def convolve(col, acc, out_rows, in_rows, base=0):
        acc = dict(zip(out_rows, acc))
        for j in range(7):
            for row in in_rows:
                hit = [r for r in out_rows if 0 <= row - r < 7]
                if hit:
                    v = pad[base + row, pl.ds(col + 5 + j, 8), :]
                    for r in hit:
                        acc[r] = acc[r] + taps[(row - r) * 7 + j] * v
        return [acc[r] for r in out_rows]

    @pl.loop(0, 7)
    def _(i):
        for u in range(4):
            col = pl.multiple_of(16 + i * 32 + u * 8, 8)
            for r, v in enumerate(convolve(col, [bias] * 8, range(8), range(3, 11))):
                conv[r, pl.ds(col, 8), :] = v

    one = lambda cond: cond.astype(jnp.int32)
    targets = one(ward_up) + one(ward_down) + one(image_up) + one(image_down) + 2
    count = 46 + one(has_up) + one(has_down) + targets + 8 * one(edge)
    pl.semaphore_wait(barrier, count)

    def columns(c):
        return pl.ds(pl.multiple_of(c * 16, 16), 16)

    def piece_copy(k, g):
        return remote(piece, pieces.at[f], sem.at[2], sem.at[3], g, ward)

    def up_copy():
        return remote(x.at[pl.ds(0, 3)], bot, row_send.at[0], row_recv.at[0], f, t - 1)

    def down_copy():
        return remote(x.at[pl.ds(5, 3)], top, row_send.at[1], row_recv.at[1], f, t + 1)

    for rows, cond in ((0, is_first), (5, is_last)):

        @pl.when(cond)
        def _(rows=rows):
            three = pl.ds(rows, 3)
            for g in others:
                remote(x.at[three, columns(g), :], near_band.at[f], sem.at[0], sem.at[1], g, t).start()
            for g in others + [f]:
                remote(
                    x.at[three, columns(g + 8), :], far_band.at[f], sem.at[18], sem.at[19], g, mirror
                ).start()
            near_band[f] = x[three, columns(f), :]

    for k, g in enumerate(others):
        piece_copy(k, g).start()

    @pl.when(has_up)
    def _():
        up_copy().start()

    @pl.when(has_down)
    def _():
        down_copy().start()

    for load in loads[3:]:
        load.wait()

    def side_copy(slot, tile):
        return remote(chosen, side.at[slot], side_send.at[slot], side_recv.at[slot], f, tile)

    routes = (
        (0, ward + 1, ward_down), (1, ward, true), (2, ward - 1, ward_up),
        (3, image + 1, image_down), (4, image, true), (5, image - 1, image_up),
    )

    def pass_sides():
        drain(pieces.at[pl.ds(0, 7)], 3)
        from_west = pieces[nbr[0, 3, f]]
        from_east = pieces[nbr[0, 1, f]]
        chosen[...] = jnp.concatenate(
            [from_west.astype(F32)[:, 8:16], from_east.astype(F32)[:, 0:8]], 1
        ).astype(BF)
        for slot, tile, cond in routes:

            @pl.when(cond)
            def _(slot=slot, tile=tile):
                side_copy(slot, tile).start()

        @pl.when(own3)
        def _():
            side[3] = chosen[...]

        @pl.when(own5)
        def _():
            side[5] = chosen[...]

    def pass_bands():
        for near_side, far_side, cond in ((0, 2, is_last), (2, 0, is_first)):

            @pl.when(cond)
            def _(near_side=near_side, far_side=far_side):
                drain(near_band.at[pl.ds(0, 7)], 1)
                for g in others + [f]:
                    near_out[g] = near_band[nbr[0, near_side, g]]
                    remote(near_out.at[g], hbuf.at[f], sem.at[4], sem.at[5], g, mirror).start()
                drain(far_band, 19)
                for k, g in enumerate(others):
                    far_out[k] = far_band[nbr[0, far_side, g]]
                    remote(far_out.at[k], hbuf.at[f + 8], sem.at[4], sem.at[5], g, t).start()
                hbuf[f + 8] = far_band[nbr[0, far_side, f]]

    def polar(flag, rows):
        drain(hbuf.at[pl.ds(0, 15)], 5)
        turn = one_hot(256, 256, lambda r: 255 - r)
        for d in range(3):
            band = jnp.concatenate([hbuf[k, d] for k in range(16)], 0)
            turned = nn(turn, band)
            pad[rows[d], 8:264, :] = jnp.where(flag == 1, turned, band.astype(F32))

    def finish(out_rows, in_rows):
        @pl.loop(0, 7)
        def _(i):
            for u in range(4):
                col = pl.multiple_of(16 + i * 32 + u * 8, 8)
                acc = [conv[r, pl.ds(col, 8), :] for r in out_rows]
                for r, v in zip(out_rows, convolve(col, acc, out_rows, in_rows)):
                    conv[r, pl.ds(col, 8), :] = v

    def finish_top():
        @pl.when(has_up)
        def _():
            down_copy().wait_recv()
            pad[0:3, 8:264, :] = top[...].astype(F32)

        @pl.when(is_first)
        def _():
            polar(nbr[2, 0, f], (0, 1, 2))

        finish(range(0, 3), range(0, 3))

    def finish_bottom():
        @pl.when(has_down)
        def _():
            up_copy().wait_recv()
            pad[11:14, 8:264, :] = bot[...].astype(F32)

        @pl.when(is_last)
        def _():
            polar(nbr[2, 2, f], (11, 12, 13))

        finish(range(5, 8), range(11, 14))

    acc_e[...] = jnp.zeros_like(acc_e)
    acc_r[...] = jnp.zeros_like(acc_r)
    sums[...] = jnp.zeros_like(sums)
    mean_of = jnp.full((128, 128), 1.0 / 128, BF)
    vec = lambda ref: ref[...].reshape(1, -1)

    def pull_back(cotangent):
        branch_cot = (cotangent.astype(F32) * vec(ls)).astype(BF)
        sums[3] += fold(branch_cot.astype(F32))
        return branch_cot, nt(branch_cot, wr[...])

    def mlp(c, pulled, rows, between=None):
        count = c.shape[0]
        centred = c - nn(c.astype(BF), mean_of)
        variance = nn((centred * centred).astype(BF), mean_of)
        inverse = lax.rsqrt(variance + EPS)
        normed = centred * inverse
        scaled = (normed * vec(gain) + vec(nb)).astype(BF)
        hidden = nn(scaled, we[...]) + vec(be)
        branch_cot, active_cot = pulled
        square = hidden * hidden
        gate = 0.5 + 0.5 * jnp.tanh(hidden * (ROOT + (ROOT * CUBE) * square))
        active = hidden * gate
        active_low = active.astype(BF)
        slope = gate + active * (1.0 - gate) * (2.0 * ROOT + (6.0 * ROOT * CUBE) * square)
        hidden_cot = (active_cot * slope).astype(BF)
        act[rows, :] = active_low
        left = jnp.concatenate([scaled.T, jnp.ones((16, count), BF)], 0)
        acc_e[...] += nn(left, hidden_cot)
        acc_r[...] += nn(branch_cot.T, active_low)
        if between is not None:
            between()
        scaled_cot = nt(hidden_cot, we[...])
        normed_cot = scaled_cot * vec(gain)
        m1 = nn(normed_cot.astype(BF), mean_of)
        m2 = nn((normed_cot * normed).astype(BF), mean_of)
        conv_cot = inverse * (normed_cot - m1 - normed * m2)
        sums[0] += fold(conv_cot)
        sums[1] += fold(scaled_cot * normed)
        sums[2] += fold(scaled_cot)
        return conv_cot

    def kernel_grad(base, rows, cols):
        steps = len(cols) // 4

        @pl.loop(0, 7)
        def _(j):
            def step(k, acc):
                acc = list(acc)
                for u in range(4):
                    col = cols[u] if steps == 1 else pl.multiple_of(cols[0] + k * 32 + u * 8, 8)
                    cots = [conv[base + r, pl.ds(col, 8), :] for r in range(rows)]
                    for row in range(rows + 6):
                        v = pad[base + row, pl.ds(col + 5 + j, 8), :]
                        for i in range(7):
                            if 0 <= row - i < rows:
                                acc[i] = acc[i] + cots[row - i] * v
                return tuple(acc)

            zero = (jnp.zeros((8, 128), F32),) * 7
            acc = step(0, zero) if steps == 1 else lax.fori_loop(0, steps, step, zero)
            for i in range(7):
                ksum[i * 7 + j] += acc[i]

    inner = range(16, 240, 8)
    low_first = t < 16
    base1 = jnp.where(low_first, 5, 0)
    base2 = 5 - base1
    base5 = jnp.where(low_first, 3, 0)
    mid, three1, three2 = pl.ds(3, 2), pl.ds(base1, 3), pl.ds(base2, 3)
    five = pl.ds(base5, 5)

    def inside(ref, rows, count):
        return ref[rows, 16:240, :].reshape(count * 224, 128)

    def outside(ref):
        return jnp.concatenate([ref[five, 0:16, :], ref[five, 240:256, :]], 1).reshape(160, 128)

    def put_outside(ref, value):
        value = value.reshape(5, 32, 128)
        ref[five, 0:16, :] = value[:, 0:16]
        ref[five, 240:256, :] = value[:, 16:32]

    got = mlp(inside(conv, mid, 2), pull_back(inside(cot, mid, 2)), pl.ds(0, 448))
    conv[mid, 16:240, :] = got.reshape(2, 224, 128)
    ksum[...] = jnp.zeros_like(ksum)
    kernel_grad(3, 2, inner)
    later = (inside(cot, three1, 3), outside(cot), cot[three2, :, :].reshape(768, 128))
    pulled[...], pulled_wide[...] = pull_back(jnp.concatenate(later, 0))
    pass_sides()

    @pl.when(low_first)
    def _():
        finish_bottom()

    @pl.when(jnp.logical_not(low_first))
    def _():
        finish_top()

    pass_bands()
    got = mlp(inside(conv, three1, 3), (pulled[0:672, :], pulled_wide[0:672, :]), pl.ds(448, 672))
    conv[three1, 16:240, :] = got.reshape(3, 224, 128)
    kernel_grad(base1, 3, inner)

    for slot, cond in enumerate(valid):

        @pl.when(cond)
        def _(slot=slot):
            side_copy(slot, origin[slot]).wait_recv()

    @pl.when(is_first)
    def _():
        side[0] = jnp.zeros((3, 16, 128), BF)
        side[3] = jnp.zeros((3, 16, 128), BF)

    @pl.when(is_last)
    def _():
        side[2] = jnp.zeros((3, 16, 128), BF)
        side[5] = jnp.zeros((3, 16, 128), BF)

    turn = one_hot(24, 24, lambda r: r // 8 * 8 + 7 - r % 8)
    for d in range(3):
        slots = [side[i, d].astype(F32) for i in range(6)]
        for first, side_id, col in ((0, 3, 7 - d), (8, 1, 264 + d)):
            straight = jnp.concatenate([slots[i][first : first + 8] for i in (0, 1, 2)], 0)
            turned = jnp.concatenate([slots[i][first : first + 8] for i in (3, 4, 5)], 0)
            turned = nn(turn, turned.astype(BF))
            halo = jnp.where(nbr[2, side_id, f] == 1, turned, straight)
            pad[0:14, col : col + 1, :] = halo[5:19].reshape(14, 1, 128)

    ends = (0, 8, 240, 248)

    def convolve_ends(base, rows):
        for col in ends:
            got = convolve(col, [bias] * rows, range(rows), range(rows + 6), base)
            for r, v in enumerate(got):
                conv[base + r, pl.ds(col, 8), :] = v

    convolve_ends(base5, 5)

    @pl.when(edge)
    def _():
        put_outside(conv, mlp(outside(conv), (pulled[672:832, :], pulled_wide[672:832, :]), pl.ds(1120, 160)))
        kernel_grad(base5, 5, ends)

    @pl.when(low_first)
    def _():
        finish_top()

    @pl.when(jnp.logical_not(low_first))
    def _():
        finish_bottom()

    convolve_ends(base2, 3)

    def send_large():
        for q in range(4):
            cols = slice(q * 128, q * 128 + 128)
            big[q * 4 : q * 4 + 4] = acc_e[0:128, cols].astype(BF).reshape(4, 32, 128)
            big[16 + q * 4 : 20 + q * 4] = acc_r[:, cols].T.astype(BF).reshape(4, 32, 128)
        for q in near:
            remote(big.at[q], slots1.at[me], sem.at[6], sem.at[7], *near_id(q)).start()

    def last_rows():
        return conv[three2, :, :].reshape(768, 128)

    @pl.when(edge)
    def _():
        got = mlp(last_rows(), (pulled[832:1600, :], pulled_wide[832:1600, :]), pl.ds(1280, 768), send_large)
        conv[three2, :, :] = got.reshape(3, 256, 128)

    @pl.when(jnp.logical_not(edge))
    def _():
        got = mlp(
            jnp.concatenate([outside(conv), last_rows()], 0),
            (pulled[672:1600, :], pulled_wide[672:1600, :]), pl.ds(1120, 928), send_large,
        )
        put_outside(conv, got[0:160])
        conv[three2, :, :] = got[160:928].reshape(3, 256, 128)

    slots1[me] = big[me]

    scale = jnp.zeros((8, 128), F32)
    for q in range(4):
        cols = slice(q * 128, q * 128 + 128)
        scale = scale + fold(acc_r[:, cols].T * wr[cols, :].astype(F32))
    small[...] = jnp.zeros_like(small)
    totals = [jnp.sum(sums[i], 0, keepdims=True) for i in range(4)]
    totals.append((jnp.sum(scale, 0, keepdims=True) + vec(br) * totals[3]) / vec(ls))
    for i in range(5):
        small[49 + i : 50 + i, :] = totals[i]
    for q in range(4):
        small[54 + q : 55 + q, :] = acc_e[128:129, q * 128 : q * 128 + 128]

    kernel_grad(base2, 3, range(0, 256, 8))

    @pl.when(jnp.logical_not(edge))
    def _():
        kernel_grad(base5, 5, ends)

    for i in range(49):
        small[i : i + 1, :] = jnp.sum(ksum[i], 0, keepdims=True)

    def half_of(part):
        return small.at[pl.ds(pl.multiple_of(part * 32, 32), 32)]

    remote(half_of(1 - core), few_half, sem.at[8], sem.at[9], f, twin).start()

    def output(rows, residual):
        branch = nn(act[rows, :], wr[...]) + vec(br)
        return (residual.astype(F32) + vec(ls) * branch).astype(BF)

    def output_inside(rows, three, count):
        out[three, 16:240, :] = output(rows, inside(x, three, count)).reshape(count, 224, 128)

    output_inside(pl.ds(0, 448), mid, 2)

    drain(few_half, 9)
    fews[a] = (half_of(core)[...] + few_half[...]).astype(BF)
    for p in plane:
        remote(fews.at[a], fews.at[a], sem.at[22], sem.at[23], *plane_id(p)).start()

    output_inside(pl.ds(448, 672), three1, 3)

    drain(slots1.at[pl.ds(0, 31)], 7)
    total = slots1[0].astype(F32)
    for q in range(1, 32):
        total = total + slots1[q].astype(F32)
    slotsz[z] = total.astype(BF)
    for q in stack:
        remote(
            slotsz.at[z], slotsz.at[z], sem.at[10], sem.at[11], f, hi * 16 + q * 2 + core
        ).start()

    put_outside(out, output(pl.ds(1120, 160), outside(x)))
    got = output(pl.ds(1280, 768), x[three2, :, :].reshape(768, 128))
    out[three2, :, :] = got.reshape(3, 256, 128)
    store = pltpu.make_async_copy(out, out_hbm, out_sem.at[0])
    store.start()

    drain(fews.at[pl.ds(0, 15)], 23)
    few = fews[0].astype(F32)
    for p in range(1, 16):
        few = few + fews[p].astype(F32)
    fewz[z] = few.astype(BF)
    for q in stack:
        remote(
            fewz.at[z], fewz.at[z], sem.at[12], sem.at[13], f, hi * 16 + q * 2 + core
        ).start()

    drain(slotsz.at[pl.ds(0, 7)], 11)
    total = slotsz[0].astype(F32)
    for q in range(1, 8):
        total = total + slotsz[q].astype(F32)
    fin[a] = (total * factor).astype(BF)
    for p in plane:
        remote(fin.at[a], fin.at[a], sem.at[14], sem.at[15], *plane_id(p)).start()

    drain(fewz.at[pl.ds(0, 7)], 13)
    few = fewz[0].astype(F32)
    for q in range(1, 8):
        few = few + fewz[q].astype(F32)
    sfin[...] = few * factor
    mine_small = sgath.at[pl.ds(pl.multiple_of(core * 32, 32), 32)]
    remote(sfin, mine_small, sem.at[16], sem.at[17], f, twin).start()
    own_small = pltpu.make_async_copy(sfin, mine_small, out_sem.at[2])
    own_small.start()
    drain(fin.at[pl.ds(0, 15)], 15)
    mine = gath.at[pl.ds(pl.multiple_of(core * 16, 16), 16)]
    remote(fin, mine, sem.at[20], sem.at[21], f, twin).start()
    own = pltpu.make_async_copy(fin, mine, out_sem.at[1])
    own.start()
    drain(sgath.at[pl.ds(0, 32)], 17)
    drain(gath.at[pl.ds(0, 16)], 21)

    store.wait()
    own.wait()
    own_small.wait()
    for slot, tile, cond in routes:

        @pl.when(cond)
        def _(slot=slot, tile=tile):
            side_copy(slot, tile).wait_send()

    @pl.when(has_up)
    def _():
        up_copy().wait_send()

    @pl.when(has_down)
    def _():
        down_copy().wait_send()

    @pl.when(edge)
    def _():
        drain(near_band.at[pl.ds(0, 7)], 0)
        drain(far_band, 18)
        drain(hbuf.at[pl.ds(0, 15)], 4)

    drain(pieces.at[pl.ds(0, 7)], 2)
    drain(slots1.at[pl.ds(0, 31)], 6)
    drain(few_half, 8)
    drain(fews.at[pl.ds(0, 15)], 22)
    drain(slotsz.at[pl.ds(0, 7)], 10)
    drain(fewz.at[pl.ds(0, 7)], 12)
    drain(fin.at[pl.ds(0, 15)], 14)
    drain(fin, 20)
    drain(sfin, 16)


def run_main(factor, neighbours, *operands):
    dma = pltpu.SemaphoreType.DMA
    shape = lambda *dims: jax.ShapeDtypeStruct(dims, BF)
    return pl.pallas_call(
        functools.partial(main_kernel, factor),
        out_shape=(
            shape(8, 256, 128),
            shape(32, 32, 128),
            jax.ShapeDtypeStruct((64, 128), F32),
        ),
        in_specs=[ANY] * 12,
        out_specs=(ANY, ANY, ANY),
        scratch_shapes=[pltpu.SMEM(neighbours.shape, jnp.int32)]
        + [pltpu.VMEM(item.shape, item.dtype) for item in operands]
        + [
            pltpu.VMEM((8, 256, 128), BF),
            pltpu.VMEM((3, 256, 128), BF),
            pltpu.VMEM((3, 256, 128), BF),
            pltpu.VMEM((16, 3, 16, 128), BF),
            pltpu.VMEM((6, 3, 16, 128), BF),
            pltpu.VMEM((3, 16, 128), BF),
            pltpu.VMEM((8, 3, 16, 128), BF),
            pltpu.VMEM((3, 16, 128), BF),
            pltpu.VMEM((8, 3, 16, 128), BF),
            pltpu.VMEM((8, 3, 16, 128), BF),
            pltpu.VMEM((8, 3, 16, 128), BF),
            pltpu.VMEM((7, 3, 16, 128), BF),
            pltpu.VMEM((14, 272, 128), F32),
            pltpu.VMEM((8, 256, 128), F32),
            pltpu.VMEM((49, 8, 128), F32),
            pltpu.VMEM((2048, 512), BF),
            pltpu.VMEM((1600, 128), BF),
            pltpu.VMEM((1600, 512), F32),
            pltpu.VMEM((144, 512), F32),
            pltpu.VMEM((128, 512), F32),
            pltpu.VMEM((4, 8, 128), F32),
            pltpu.VMEM((49, 8, 128), F32),
            pltpu.VMEM((32, 32, 128), BF),
            pltpu.VMEM((32, 32, 128), BF),
            pltpu.VMEM((8, 32, 128), BF),
            pltpu.VMEM((16, 32, 128), BF),
            pltpu.VMEM((64, 128), F32),
            pltpu.VMEM((32, 128), F32),
            pltpu.VMEM((16, 32, 128), BF),
            pltpu.VMEM((8, 32, 128), BF),
            pltpu.VMEM((32, 128), F32),
            dma((12,)), dma((3,)), dma((2,)), dma((2,)), dma((6,)), dma((6,)), dma((24,)),
        ],
        compiler_params=pltpu.CompilerParams(
            collective_id=0, has_side_effects=True, vmem_limit_bytes=56 * 1024 * 1024
        ),
        name="main",
    )(neighbours, *operands)


def unpack_kernel(
    raw, gath, sgath,
    out, kernel_grad, cb_grad, gain_grad, nb_grad, we_grad, be_grad, wr_grad, br_grad, ls_grad,
    stage, rows_in, few_in, sem,
):
    fetches = [
        pltpu.make_async_copy(src, dst, sem.at[i])
        for i, (src, dst) in enumerate(((gath, rows_in), (sgath, few_in)))
    ]
    parts = [pl.ds(i * 2, 2) for i in range(4)]
    loads = [
        pltpu.make_async_copy(raw.at[part], stage.at[part], sem.at[2 + i])
        for i, part in enumerate(parts)
    ]
    stores = [
        pltpu.make_async_copy(stage.at[part], out.at[part], sem.at[6 + i])
        for i, part in enumerate(parts)
    ]
    for fetch in fetches + loads:
        fetch.start()
    for fetch in fetches:
        fetch.wait()
    rows = rows_in.reshape(1024, 128)
    few = few_in
    for q in range(4):
        we_grad[:, q * 128 : q * 128 + 128] = rows[q * 128 : q * 128 + 128, :].astype(F32)
        be_grad[q * 128 : q * 128 + 128] = few[54 + q]
    wr_grad[...] = rows[512:1024, :].astype(F32)
    for i in range(7):
        kernel_grad[i] = few[i * 7 : i * 7 + 7]
    for i, ref in enumerate((cb_grad, gain_grad, nb_grad, br_grad, ls_grad)):
        ref[...] = few[49 + i]
    for load, store in zip(loads, stores):
        load.wait()
        store.start()
    for store in stores:
        store.wait()


def unpack(raw, gath, sgath):
    one = lambda *shape: jax.ShapeDtypeStruct(shape, F32)
    return pl.pallas_call(
        unpack_kernel,
        out_shape=(
            jax.ShapeDtypeStruct(raw.shape, raw.dtype),
            one(7, 7, 128), one(128), one(128), one(128), one(128, 512), one(512),
            one(512, 128), one(128), one(128),
        ),
        in_specs=[ANY, ANY, ANY],
        out_specs=(ANY,) + (VMEM,) * 9,
        scratch_shapes=[
            pltpu.VMEM(raw.shape, raw.dtype),
            pltpu.VMEM(gath.shape, gath.dtype),
            pltpu.VMEM(sgath.shape, sgath.dtype),
            pltpu.SemaphoreType.DMA((10,)),
        ],
        compiler_params=pltpu.CompilerParams(vmem_limit_bytes=56 * 1024 * 1024),
        name="unpack",
    )(raw, gath, sgath)


def body(
    inputs, kernel, conv_bias, norm_gain, norm_bias, expand_weight, expand_bias,
    reduce_weight, reduce_bias, layer_scale, neighbours, cotangent,
):
    factor = 1.0 / math.sqrt(FACES * 256 * 256)
    raw, gath, sgath = run_main(
        factor, jnp.transpose(neighbours, (2, 1, 0)), inputs[0], cotangent[0], kernel, conv_bias, norm_gain, norm_bias,
        expand_weight, expand_bias, reduce_weight, reduce_bias, layer_scale,
    )
    out, *grads = unpack(raw, gath, sgath)
    return (out[None], *grads)


def solution(mesh):
    split = P("face", "tile", None, None)
    return jax.shard_map(
        body,
        mesh=mesh,
        in_specs=(split,) + (P(),) * 10 + (split,),
        out_specs=(split,) + (P(),) * 9,
        check_vma=False,
    )
```

```python
import functools
import math

import jax
import jax.numpy as jnp
from jax import lax
from jax.experimental import pallas as pl
from jax.experimental.pallas import tpu as pltpu
from jax.sharding import PartitionSpec as P

EPS = 1e-06
MESH = pl.DeviceIdType.MESH
BF = jnp.bfloat16
F32 = jnp.float32
ROOT = math.sqrt(2.0 / math.pi)
CUBE = 0.044715
FACES = 8
TILES = 32


def ring(step, size):
    return min(step, size - step)


FACE_STEPS = sorted(
    ((dy, dx) for dy in range(2) for dx in range(4) if dy or dx), key=lambda d: -2 * d[0] - ring(d[1], 4)
)
PLANE_STEPS = sorted(
    ((dy, dx) for dy in range(4) for dx in range(4) if dy or dx), key=lambda d: -ring(d[0], 4) - ring(d[1], 4)
)
STACK_STEPS = sorted(range(1, 8), key=lambda d: -ring(d, 8))
VMEM = pl.BlockSpec(memory_space=pltpu.VMEM)
SMEM = pl.BlockSpec(memory_space=pltpu.SMEM)
ANY = pl.BlockSpec(memory_space=pl.ANY)


def place():
    return lax.axis_index("face"), lax.axis_index("tile")


def remote(src, dst, send, recv, face, tile):
    return pltpu.make_async_remote_copy(
        src_ref=src, dst_ref=dst, send_sem=send, recv_sem=recv,
        device_id=(face, tile), device_id_type=MESH,
    )


def nt(left, right):
    return lax.dot_general(left, right, (((1,), (1,)), ((), ())), preferred_element_type=F32)


def nn(left, right):
    return lax.dot_general(left, right, (((1,), (0,)), ((), ())), preferred_element_type=F32)


def one_hot(rows, cols, index):
    r = lax.broadcasted_iota(jnp.int32, (rows, cols), 0)
    c = lax.broadcasted_iota(jnp.int32, (rows, cols), 1)
    return jnp.where(c == index(r), 1.0, 0.0).astype(BF)


def fold(v):
    rows, chans = v.shape
    return jnp.sum(v.reshape(rows // 8, 8, chans), 0)


def main_kernel(
    factor,
    nbr_hbm, x_hbm, cot_hbm, kern_hbm, cb_hbm, gain_hbm, nb_hbm, we_hbm, be_hbm, wr_hbm, br_hbm, ls_hbm,
    out_hbm, gath, sgath,
    nbr, x, cot, kern, cb, gain, nb, we, be, wr, br, ls, out,
    top, bot, hbuf, side, piece, pieces, chosen, near_band, far_band, near_out, far_out,
    pad, conv, taps, act, pulled, pulled_wide, acc_e, acc_r, sums, ksum,
    big, slots1, slotsz, fin, small, few_half, fews, fewz, sfin,
    load_sem, out_sem, row_send, row_recv, side_send, side_recv, sem,
):
    f, t = place()
    last = TILES - 1
    mirror = last - t
    is_first = t == 0
    is_last = t == last
    has_up = t > 0
    has_down = t < last
    ward = lax.rem(t + 16, TILES)
    image = last - ward
    ward_up = ward > 0
    ward_down = ward < last
    image_up = jnp.logical_and(image > 0, image - 1 != t)
    image_down = jnp.logical_and(image < last, image + 1 != t)
    origin = [lax.rem(v + TILES, TILES) for v in (t + 15, t + 16, t + 17, 16 - t, 15 - t, 14 - t)]
    own3 = jnp.logical_and(has_up, origin[3] == t)
    own5 = jnp.logical_and(has_down, origin[5] == t)
    true = t >= 0
    valid = [
        has_up, true, has_down, jnp.logical_and(has_up, origin[3] != t), true,
        jnp.logical_and(has_down, origin[5] != t),
    ]
    edge = jnp.logical_or(is_first, is_last)
    hi = t // 16
    s = t % 16
    z = s // 2
    core = s % 2
    a = hi * 8 + f
    me = core * 16 + a
    twin = t + 1 - 2 * core
    yh, across = f // 4, f % 4
    row = yh * 2 + hi

    def plane_at(dy, dx):
        to = lax.rem(row + dy, 4)
        return to % 2 * 8 + to // 2 * 4 + lax.rem(across + dx, 4)

    others = [lax.rem(yh + dy, 2) * 4 + lax.rem(across + dx, 4) for dy, dx in FACE_STEPS]
    plane = [plane_at(dy, dx) for dy, dx in PLANE_STEPS]
    near = [c * 16 + p for p in plane for c in (core, 1 - core)] + [(1 - core) * 16 + a]
    stack = [lax.rem(z + dz, 8) for dz in STACK_STEPS]
    line = [q * 2 + c for q in stack for c in (core, 1 - core)] + [z * 2 + 1 - core]

    def plane_id(p):
        return lax.rem(p, 8), p // 8 * 16 + s

    def near_id(q):
        return lax.rem(q, 8), q % 16 // 8 * 16 + z * 2 + q // 16

    def drain(ref, which):
        pltpu.make_async_copy(ref, ref, sem.at[which]).wait()

    loads = [
        pltpu.make_async_copy(src, dst, load_sem.at[i])
        for i, (src, dst) in enumerate(
            (
                (x_hbm, x), (kern_hbm, kern), (cb_hbm, cb), (cot_hbm, cot), (we_hbm, we), (wr_hbm, wr),
                (nbr_hbm, nbr), (gain_hbm, gain), (nb_hbm, nb), (be_hbm, be), (br_hbm, br), (ls_hbm, ls),
            )
        )
    ]
    for load in loads:
        load.start()

    barrier = pltpu.get_barrier_semaphore()

    def hello(face, tile):
        pl.semaphore_signal(barrier, inc=1, device_id=(face, tile), device_id_type=MESH)

    @pl.when(edge)
    def _():
        for g in range(FACES):
            hello(g, mirror)

    @pl.when(has_up)
    def _():
        hello(f, t - 1)

    @pl.when(has_down)
    def _():
        hello(f, t + 1)

    for tile, cond in zip(origin, valid):

        @pl.when(cond)
        def _(tile=tile):
            hello(f, tile)

    for p in line:
        hello(f, hi * 16 + p)
    for q in near:
        hello(*near_id(q))

    loads[0].wait()
    for d in range(3):
        west = x[:, d : d + 1, :].astype(F32).reshape(8, 128)
        east = x[:, 255 - d : 256 - d, :].astype(F32).reshape(8, 128)
        piece[d] = jnp.concatenate([west, east], 0).astype(BF)
    pad[3:11, 8:264, :] = x[...].astype(F32)
    for load in loads[1:3]:
        load.wait()
    for i in range(7):
        for j in range(7):
            taps[i * 7 + j] = jnp.broadcast_to(kern[i, j : j + 1, :], (8, 128))
    bias = jnp.broadcast_to(cb[...].reshape(1, 128), (8, 128))

    def convolve(col, acc, out_rows, in_rows, base=0):
        acc = dict(zip(out_rows, acc))
        for j in range(7):
            for row in in_rows:
                hit = [r for r in out_rows if 0 <= row - r < 7]
                if hit:
                    v = pad[base + row, pl.ds(col + 5 + j, 8), :]
                    for r in hit:
                        acc[r] = acc[r] + taps[(row - r) * 7 + j] * v
        return [acc[r] for r in out_rows]

    @pl.loop(0, 4)
    def _(i):
        for u in range(7):
            col = pl.multiple_of(16 + i * 56 + u * 8, 8)
            for r, v in enumerate(convolve(col, [bias] * 8, range(8), range(3, 11))):
                conv[r, pl.ds(col, 8), :] = v

    one = lambda cond: cond.astype(jnp.int32)
    targets = one(ward_up) + one(ward_down) + one(image_up) + one(image_down) + 2
    count = 46 + one(has_up) + one(has_down) + targets + 8 * one(edge)
    pl.semaphore_wait(barrier, count)

    def columns(c):
        return pl.ds(pl.multiple_of(c * 16, 16), 16)

    def piece_copy(k, g):
        return remote(piece, pieces.at[f], sem.at[2], sem.at[3], g, ward)

    def up_copy():
        return remote(x.at[pl.ds(0, 3)], bot, row_send.at[0], row_recv.at[0], f, t - 1)

    def down_copy():
        return remote(x.at[pl.ds(5, 3)], top, row_send.at[1], row_recv.at[1], f, t + 1)

    for rows, cond in ((0, is_first), (5, is_last)):

        @pl.when(cond)
        def _(rows=rows):
            three = pl.ds(rows, 3)
            for g in others:
                remote(x.at[three, columns(g), :], near_band.at[f], sem.at[0], sem.at[1], g, t).start()
            for g in others + [f]:
                remote(
                    x.at[three, columns(g + 8), :], far_band.at[f], sem.at[18], sem.at[19], g, mirror
                ).start()
            near_band[f] = x[three, columns(f), :]

    for k, g in enumerate(others):
        piece_copy(k, g).start()

    @pl.when(has_up)
    def _():
        up_copy().start()

    @pl.when(has_down)
    def _():
        down_copy().start()

    for load in loads[3:]:
        load.wait()

    def side_copy(slot, tile):
        return remote(chosen, side.at[slot], side_send.at[slot], side_recv.at[slot], f, tile)

    routes = (
        (0, ward + 1, ward_down), (1, ward, true), (2, ward - 1, ward_up),
        (3, image + 1, image_down), (4, image, true), (5, image - 1, image_up),
    )

    def pass_sides():
        drain(pieces.at[pl.ds(0, 7)], 3)
        from_west = pieces[nbr[0, 3, f]]
        from_east = pieces[nbr[0, 1, f]]
        chosen[...] = jnp.concatenate(
            [from_west.astype(F32)[:, 8:16], from_east.astype(F32)[:, 0:8]], 1
        ).astype(BF)
        for slot, tile, cond in routes:

            @pl.when(cond)
            def _(slot=slot, tile=tile):
                side_copy(slot, tile).start()

        @pl.when(own3)
        def _():
            side[3] = chosen[...]

        @pl.when(own5)
        def _():
            side[5] = chosen[...]

    def pass_bands():
        for near_side, far_side, cond in ((0, 2, is_last), (2, 0, is_first)):

            @pl.when(cond)
            def _(near_side=near_side, far_side=far_side):
                drain(near_band.at[pl.ds(0, 7)], 1)
                for g in others + [f]:
                    near_out[g] = near_band[nbr[0, near_side, g]]
                    remote(near_out.at[g], hbuf.at[f], sem.at[4], sem.at[5], g, mirror).start()
                drain(far_band, 19)
                for k, g in enumerate(others):
                    far_out[k] = far_band[nbr[0, far_side, g]]
                    remote(far_out.at[k], hbuf.at[f + 8], sem.at[4], sem.at[5], g, t).start()
                hbuf[f + 8] = far_band[nbr[0, far_side, f]]

    def polar(flag, rows):
        drain(hbuf.at[pl.ds(0, 15)], 5)
        turn = one_hot(256, 256, lambda r: 255 - r)
        for d in range(3):
            band = jnp.concatenate([hbuf[k, d] for k in range(16)], 0)
            turned = nn(turn, band)
            pad[rows[d], 8:264, :] = jnp.where(flag == 1, turned, band.astype(F32))

    def finish(out_rows, in_rows):
        @pl.loop(0, 4)
        def _(i):
            for u in range(7):
                col = pl.multiple_of(16 + i * 56 + u * 8, 8)
                acc = [conv[r, pl.ds(col, 8), :] for r in out_rows]
                for r, v in zip(out_rows, convolve(col, acc, out_rows, in_rows)):
                    conv[r, pl.ds(col, 8), :] = v

    def finish_top():
        @pl.when(has_up)
        def _():
            down_copy().wait_recv()
            pad[0:3, 8:264, :] = top[...].astype(F32)

        @pl.when(is_first)
        def _():
            polar(nbr[2, 0, f], (0, 1, 2))

        finish(range(0, 3), range(0, 3))

    def finish_bottom():
        @pl.when(has_down)
        def _():
            up_copy().wait_recv()
            pad[11:14, 8:264, :] = bot[...].astype(F32)

        @pl.when(is_last)
        def _():
            polar(nbr[2, 2, f], (11, 12, 13))

        finish(range(5, 8), range(11, 14))

    acc_e[...] = jnp.zeros_like(acc_e)
    acc_r[...] = jnp.zeros_like(acc_r)
    sums[...] = jnp.zeros_like(sums)
    mean_of = jnp.full((128, 128), 1.0 / 128, BF)
    vec = lambda ref: ref[...].reshape(1, -1)

    def pull_back(cotangent):
        branch_cot = (cotangent.astype(F32) * vec(ls)).astype(BF)
        sums[3] += fold(branch_cot.astype(F32))
        return branch_cot, nt(branch_cot, wr[...])

    def mlp(c, pulled, rows, between=None):
        count = c.shape[0]
        centred = c - nn(c.astype(BF), mean_of)
        variance = nn((centred * centred).astype(BF), mean_of)
        inverse = lax.rsqrt(variance + EPS)
        normed = centred * inverse
        scaled = (normed * vec(gain) + vec(nb)).astype(BF)
        hidden = nn(scaled, we[...]) + vec(be)
        branch_cot, active_cot = pulled
        square = hidden * hidden
        gate = 0.5 + 0.5 * jnp.tanh(hidden * (ROOT + (ROOT * CUBE) * square))
        active = hidden * gate
        active_low = active.astype(BF)
        slope = gate + active * (1.0 - gate) * (2.0 * ROOT + (6.0 * ROOT * CUBE) * square)
        hidden_cot = (active_cot * slope).astype(BF)
        act[rows, :] = active_low
        left = jnp.concatenate([scaled.T, jnp.ones((16, count), BF)], 0)
        acc_e[...] += nn(left, hidden_cot)
        acc_r[...] += nn(branch_cot.T, active_low)
        if between is not None:
            between()
        scaled_cot = nt(hidden_cot, we[...])
        normed_cot = scaled_cot * vec(gain)
        m1 = nn(normed_cot.astype(BF), mean_of)
        m2 = nn((normed_cot * normed).astype(BF), mean_of)
        conv_cot = inverse * (normed_cot - m1 - normed * m2)
        sums[0] += fold(conv_cot)
        sums[1] += fold(scaled_cot * normed)
        sums[2] += fold(scaled_cot)
        return conv_cot

    def kernel_grad(base, rows, cols):
        steps = 1 if len(cols) == 4 else 4
        width = len(cols) // steps

        @pl.loop(0, 7)
        def _(j):
            def step(k, acc):
                acc = list(acc)
                for u in range(width):
                    col = cols[u] if steps == 1 else pl.multiple_of(cols[0] + k * width * 8 + u * 8, 8)
                    cots = [conv[base + r, pl.ds(col, 8), :] for r in range(rows)]
                    for row in range(rows + 6):
                        v = pad[base + row, pl.ds(col + 5 + j, 8), :]
                        for i in range(7):
                            if 0 <= row - i < rows:
                                acc[i] = acc[i] + cots[row - i] * v
                return tuple(acc)

            zero = (jnp.zeros((8, 128), F32),) * 7
            acc = step(0, zero) if steps == 1 else lax.fori_loop(0, steps, step, zero)
            for i in range(7):
                ksum[i * 7 + j] += acc[i]

    inner = range(16, 240, 8)
    low_first = t < 16
    base1 = jnp.where(low_first, 5, 0)
    base2 = 5 - base1
    base5 = jnp.where(low_first, 3, 0)
    mid, three1, three2 = pl.ds(3, 2), pl.ds(base1, 3), pl.ds(base2, 3)
    five = pl.ds(base5, 5)

    def inside(ref, rows, count):
        return ref[rows, 16:240, :].reshape(count * 224, 128)

    def outside(ref):
        return jnp.concatenate([ref[five, 0:16, :], ref[five, 240:256, :]], 1).reshape(160, 128)

    def put_outside(ref, value):
        value = value.reshape(5, 32, 128)
        ref[five, 0:16, :] = value[:, 0:16]
        ref[five, 240:256, :] = value[:, 16:32]

    got = mlp(inside(conv, mid, 2), pull_back(inside(cot, mid, 2)), pl.ds(0, 448))
    conv[mid, 16:240, :] = got.reshape(2, 224, 128)
    ksum[...] = jnp.zeros_like(ksum)
    kernel_grad(3, 2, inner)
    later = (inside(cot, three1, 3), outside(cot), cot[three2, :, :].reshape(768, 128))
    pulled[...], pulled_wide[...] = pull_back(jnp.concatenate(later, 0))
    pass_sides()

    @pl.when(low_first)
    def _():
        finish_bottom()

    @pl.when(jnp.logical_not(low_first))
    def _():
        finish_top()

    pass_bands()
    got = mlp(inside(conv, three1, 3), (pulled[0:672, :], pulled_wide[0:672, :]), pl.ds(448, 672))
    conv[three1, 16:240, :] = got.reshape(3, 224, 128)
    kernel_grad(base1, 3, inner)

    for slot, cond in enumerate(valid):

        @pl.when(cond)
        def _(slot=slot):
            side_copy(slot, origin[slot]).wait_recv()

    @pl.when(is_first)
    def _():
        side[0] = jnp.zeros((3, 16, 128), BF)
        side[3] = jnp.zeros((3, 16, 128), BF)

    @pl.when(is_last)
    def _():
        side[2] = jnp.zeros((3, 16, 128), BF)
        side[5] = jnp.zeros((3, 16, 128), BF)

    turn = one_hot(24, 24, lambda r: r // 8 * 8 + 7 - r % 8)
    for d in range(3):
        slots = [side[i, d].astype(F32) for i in range(6)]
        for first, side_id, col in ((0, 3, 7 - d), (8, 1, 264 + d)):
            straight = jnp.concatenate([slots[i][first : first + 8] for i in (0, 1, 2)], 0)
            turned = jnp.concatenate([slots[i][first : first + 8] for i in (3, 4, 5)], 0)
            turned = nn(turn, turned.astype(BF))
            halo = jnp.where(nbr[2, side_id, f] == 1, turned, straight)
            pad[0:14, col : col + 1, :] = halo[5:19].reshape(14, 1, 128)

    ends = (0, 8, 240, 248)

    def convolve_ends(base, rows):
        for col in ends:
            got = convolve(col, [bias] * rows, range(rows), range(rows + 6), base)
            for r, v in enumerate(got):
                conv[base + r, pl.ds(col, 8), :] = v

    convolve_ends(base5, 5)

    @pl.when(edge)
    def _():
        put_outside(conv, mlp(outside(conv), (pulled[672:832, :], pulled_wide[672:832, :]), pl.ds(1120, 160)))
        kernel_grad(base5, 5, ends)

    @pl.when(low_first)
    def _():
        finish_top()

    @pl.when(jnp.logical_not(low_first))
    def _():
        finish_bottom()

    convolve_ends(base2, 3)

    def send_large():
        for q in range(4):
            cols = slice(q * 128, q * 128 + 128)
            big[q * 4 : q * 4 + 4] = acc_e[0:128, cols].astype(BF).reshape(4, 32, 128)
            big[16 + q * 4 : 20 + q * 4] = acc_r[:, cols].T.astype(BF).reshape(4, 32, 128)
        for q in near:
            remote(big.at[q], slots1.at[me], sem.at[6], sem.at[7], *near_id(q)).start()

    def last_rows():
        return conv[three2, :, :].reshape(768, 128)

    @pl.when(edge)
    def _():
        got = mlp(last_rows(), (pulled[832:1600, :], pulled_wide[832:1600, :]), pl.ds(1280, 768), send_large)
        conv[three2, :, :] = got.reshape(3, 256, 128)

    @pl.when(jnp.logical_not(edge))
    def _():
        got = mlp(
            jnp.concatenate([outside(conv), last_rows()], 0),
            (pulled[672:1600, :], pulled_wide[672:1600, :]), pl.ds(1120, 928), send_large,
        )
        put_outside(conv, got[0:160])
        conv[three2, :, :] = got[160:928].reshape(3, 256, 128)

    slots1[me] = big[me]

    scale = jnp.zeros((8, 128), F32)
    for q in range(4):
        cols = slice(q * 128, q * 128 + 128)
        scale = scale + fold(acc_r[:, cols].T * wr[cols, :].astype(F32))
    small[...] = jnp.zeros_like(small)
    totals = [jnp.sum(sums[i], 0, keepdims=True) for i in range(4)]
    totals.append((jnp.sum(scale, 0, keepdims=True) + vec(br) * totals[3]) / vec(ls))
    for i in range(5):
        small[49 + i : 50 + i, :] = totals[i]
    for q in range(4):
        small[54 + q : 55 + q, :] = acc_e[128:129, q * 128 : q * 128 + 128]

    kernel_grad(base2, 3, range(0, 256, 8))

    @pl.when(jnp.logical_not(edge))
    def _():
        kernel_grad(base5, 5, ends)

    for i in range(49):
        small[i : i + 1, :] = jnp.sum(ksum[i], 0, keepdims=True)

    def half_of(part):
        return small.at[pl.ds(pl.multiple_of(part * 32, 32), 32)]

    remote(half_of(1 - core), few_half, sem.at[8], sem.at[9], f, twin).start()

    def output(rows, residual):
        branch = nn(act[rows, :], wr[...]) + vec(br)
        return (residual.astype(F32) + vec(ls) * branch).astype(BF)

    def output_inside(rows, three, count):
        out[three, 16:240, :] = output(rows, inside(x, three, count)).reshape(count, 224, 128)

    output_inside(pl.ds(0, 448), mid, 2)

    drain(few_half, 9)
    fews[a] = (half_of(core)[...] + few_half[...]).astype(BF)
    for p in plane:
        remote(fews.at[a], fews.at[a], sem.at[22], sem.at[23], *plane_id(p)).start()

    output_inside(pl.ds(448, 672), three1, 3)

    drain(slots1.at[pl.ds(0, 31)], 7)
    total = slots1[0].astype(F32)
    for q in range(1, 32):
        total = total + slots1[q].astype(F32)
    slotsz[z] = total.astype(BF)
    for q in stack:
        remote(
            slotsz.at[z], slotsz.at[z], sem.at[10], sem.at[11], f, hi * 16 + q * 2 + core
        ).start()

    put_outside(out, output(pl.ds(1120, 160), outside(x)))
    got = output(pl.ds(1280, 768), x[three2, :, :].reshape(768, 128))
    out[three2, :, :] = got.reshape(3, 256, 128)
    store = pltpu.make_async_copy(out, out_hbm, out_sem.at[0])
    store.start()

    drain(fews.at[pl.ds(0, 15)], 23)
    few = fews[0].astype(F32)
    for p in range(1, 16):
        few = few + fews[p].astype(F32)
    fewz[z] = few.astype(BF)
    for q in stack:
        remote(
            fewz.at[z], fewz.at[z], sem.at[12], sem.at[13], f, hi * 16 + q * 2 + core
        ).start()

    drain(slotsz.at[pl.ds(0, 7)], 11)
    total = slotsz[0].astype(F32)
    for q in range(1, 8):
        total = total + slotsz[q].astype(F32)
    fin[a] = (total * factor).astype(BF)
    for p in plane:
        remote(fin.at[a], fin.at[a], sem.at[14], sem.at[15], *plane_id(p)).start()

    drain(fewz.at[pl.ds(0, 7)], 13)
    few = fewz[0].astype(F32)
    for q in range(1, 8):
        few = few + fewz[q].astype(F32)
    sfin[...] = few * factor
    mine_small = sgath.at[pl.ds(pl.multiple_of(core * 32, 32), 32)]
    remote(sfin, mine_small, sem.at[16], sem.at[17], f, twin).start()
    own_small = pltpu.make_async_copy(sfin, mine_small, out_sem.at[2])
    own_small.start()
    drain(fin.at[pl.ds(0, 15)], 15)
    mine = gath.at[pl.ds(pl.multiple_of(core * 16, 16), 16)]
    remote(fin, mine, sem.at[20], sem.at[21], f, twin).start()
    own = pltpu.make_async_copy(fin, mine, out_sem.at[1])
    own.start()
    drain(sgath.at[pl.ds(0, 32)], 17)
    drain(gath.at[pl.ds(0, 16)], 21)

    store.wait()
    own.wait()
    own_small.wait()
    for slot, tile, cond in routes:

        @pl.when(cond)
        def _(slot=slot, tile=tile):
            side_copy(slot, tile).wait_send()

    @pl.when(has_up)
    def _():
        up_copy().wait_send()

    @pl.when(has_down)
    def _():
        down_copy().wait_send()

    @pl.when(edge)
    def _():
        drain(near_band.at[pl.ds(0, 7)], 0)
        drain(far_band, 18)
        drain(hbuf.at[pl.ds(0, 15)], 4)

    drain(pieces.at[pl.ds(0, 7)], 2)
    drain(slots1.at[pl.ds(0, 31)], 6)
    drain(few_half, 8)
    drain(fews.at[pl.ds(0, 15)], 22)
    drain(slotsz.at[pl.ds(0, 7)], 10)
    drain(fewz.at[pl.ds(0, 7)], 12)
    drain(fin.at[pl.ds(0, 15)], 14)
    drain(fin, 20)
    drain(sfin, 16)


def run_main(factor, neighbours, *operands):
    dma = pltpu.SemaphoreType.DMA
    shape = lambda *dims: jax.ShapeDtypeStruct(dims, BF)
    return pl.pallas_call(
        functools.partial(main_kernel, factor),
        out_shape=(
            shape(8, 256, 128),
            shape(32, 32, 128),
            jax.ShapeDtypeStruct((64, 128), F32),
        ),
        in_specs=[ANY] * 12,
        out_specs=(ANY, ANY, ANY),
        scratch_shapes=[pltpu.SMEM(neighbours.shape, jnp.int32)]
        + [pltpu.VMEM(item.shape, item.dtype) for item in operands]
        + [
            pltpu.VMEM((8, 256, 128), BF),
            pltpu.VMEM((3, 256, 128), BF),
            pltpu.VMEM((3, 256, 128), BF),
            pltpu.VMEM((16, 3, 16, 128), BF),
            pltpu.VMEM((6, 3, 16, 128), BF),
            pltpu.VMEM((3, 16, 128), BF),
            pltpu.VMEM((8, 3, 16, 128), BF),
            pltpu.VMEM((3, 16, 128), BF),
            pltpu.VMEM((8, 3, 16, 128), BF),
            pltpu.VMEM((8, 3, 16, 128), BF),
            pltpu.VMEM((8, 3, 16, 128), BF),
            pltpu.VMEM((7, 3, 16, 128), BF),
            pltpu.VMEM((14, 272, 128), F32),
            pltpu.VMEM((8, 256, 128), F32),
            pltpu.VMEM((49, 8, 128), F32),
            pltpu.VMEM((2048, 512), BF),
            pltpu.VMEM((1600, 128), BF),
            pltpu.VMEM((1600, 512), F32),
            pltpu.VMEM((144, 512), F32),
            pltpu.VMEM((128, 512), F32),
            pltpu.VMEM((4, 8, 128), F32),
            pltpu.VMEM((49, 8, 128), F32),
            pltpu.VMEM((32, 32, 128), BF),
            pltpu.VMEM((32, 32, 128), BF),
            pltpu.VMEM((8, 32, 128), BF),
            pltpu.VMEM((16, 32, 128), BF),
            pltpu.VMEM((64, 128), F32),
            pltpu.VMEM((32, 128), F32),
            pltpu.VMEM((16, 32, 128), BF),
            pltpu.VMEM((8, 32, 128), BF),
            pltpu.VMEM((32, 128), F32),
            dma((12,)), dma((3,)), dma((2,)), dma((2,)), dma((6,)), dma((6,)), dma((24,)),
        ],
        compiler_params=pltpu.CompilerParams(
            collective_id=0, has_side_effects=True, vmem_limit_bytes=56 * 1024 * 1024
        ),
        name="main",
    )(neighbours, *operands)


def unpack_kernel(raw, gath, sgath, *refs):
    outs, stages, (rows_in, few_in, sem) = refs[:10], refs[10:20], refs[20:]
    stage, kernel_grad, cb_grad, gain_grad, nb_grad, we_grad, be_grad, wr_grad, br_grad, ls_grad = stages
    fetches = [
        pltpu.make_async_copy(src, dst, sem.at[i])
        for i, (src, dst) in enumerate(((gath, rows_in), (sgath, few_in)))
    ]
    parts = [pl.ds(i * 4, 4) for i in range(2)]
    loads = [
        pltpu.make_async_copy(raw.at[part], stage.at[part], sem.at[2 + i])
        for i, part in enumerate(parts)
    ]
    stores = [
        pltpu.make_async_copy(stage.at[part], outs[0].at[part], sem.at[4 + i])
        for i, part in enumerate(parts)
    ]
    stores += [
        pltpu.make_async_copy(src, dst, sem.at[6 + i])
        for i, (src, dst) in enumerate(zip(stages[1:], outs[1:]))
    ]
    for fetch in fetches + loads:
        fetch.start()
    rows = rows_in.reshape(1024, 128)
    few = few_in
    fetches[1].wait()
    for q in range(4):
        be_grad[q * 128 : q * 128 + 128] = few[54 + q]
    for i in range(7):
        kernel_grad[i] = few[i * 7 : i * 7 + 7]
    for i, ref in enumerate((cb_grad, gain_grad, nb_grad, br_grad, ls_grad)):
        ref[...] = few[49 + i]
    for i in (2, 3, 4, 5, 7, 9, 10):
        stores[i].start()
    fetches[0].wait()
    for q in range(4):
        we_grad[:, q * 128 : q * 128 + 128] = rows[q * 128 : q * 128 + 128, :].astype(F32)
    stores[6].start()
    wr_grad[...] = rows[512:1024, :].astype(F32)
    stores[8].start()
    for i in range(2):
        loads[i].wait()
        stores[i].start()
    for store in stores:
        store.wait()


def unpack(raw, gath, sgath):
    one = lambda *shape: jax.ShapeDtypeStruct(shape, F32)
    shapes = (
        jax.ShapeDtypeStruct(raw.shape, raw.dtype),
        one(7, 7, 128), one(128), one(128), one(128), one(128, 512), one(512),
        one(512, 128), one(128), one(128),
    )
    return pl.pallas_call(
        unpack_kernel,
        out_shape=shapes,
        in_specs=[ANY, ANY, ANY],
        out_specs=(ANY,) * 10,
        scratch_shapes=[pltpu.VMEM(item.shape, item.dtype) for item in shapes + (gath, sgath)]
        + [pltpu.SemaphoreType.DMA((15,))],
        compiler_params=pltpu.CompilerParams(vmem_limit_bytes=56 * 1024 * 1024),
        name="unpack",
    )(raw, gath, sgath)


def body(
    inputs, kernel, conv_bias, norm_gain, norm_bias, expand_weight, expand_bias,
    reduce_weight, reduce_bias, layer_scale, neighbours, cotangent,
):
    factor = 1.0 / math.sqrt(FACES * 256 * 256)
    raw, gath, sgath = run_main(
        factor, jnp.transpose(neighbours, (2, 1, 0)), inputs[0], cotangent[0], kernel, conv_bias, norm_gain, norm_bias,
        expand_weight, expand_bias, reduce_weight, reduce_bias, layer_scale,
    )
    out, *grads = unpack(raw, gath, sgath)
    return (out[None], *grads)


def solution(mesh):
    split = P("face", "tile", None, None)
    return jax.shard_map(
        body,
        mesh=mesh,
        in_specs=(split,) + (P(),) * 10 + (split,),
        out_specs=(split,) + (P(),) * 9,
        check_vma=False,
    )
```

```python
import functools
import math

import jax
import jax.numpy as jnp
from jax import lax
from jax.experimental import pallas as pl
from jax.experimental.pallas import tpu as pltpu
from jax.sharding import PartitionSpec as P

EPS = 1e-06
MESH = pl.DeviceIdType.MESH
BF = jnp.bfloat16
F32 = jnp.float32
ROOT = math.sqrt(2.0 / math.pi)
CUBE = 0.044715
FACES = 8
TILES = 32


def ring(step, size):
    return min(step, size - step)


FACE_STEPS = sorted(
    ((dy, dx) for dy in range(2) for dx in range(4) if dy or dx), key=lambda d: -2 * d[0] - ring(d[1], 4)
)
PLANE_STEPS = sorted(
    ((dy, dx) for dy in range(4) for dx in range(4) if dy or dx), key=lambda d: -ring(d[0], 4) - ring(d[1], 4)
)
STACK_STEPS = sorted(range(1, 8), key=lambda d: -ring(d, 8))
VMEM = pl.BlockSpec(memory_space=pltpu.VMEM)
SMEM = pl.BlockSpec(memory_space=pltpu.SMEM)
ANY = pl.BlockSpec(memory_space=pl.ANY)


def place():
    return lax.axis_index("face"), lax.axis_index("tile")


def remote(src, dst, send, recv, face, tile):
    return pltpu.make_async_remote_copy(
        src_ref=src, dst_ref=dst, send_sem=send, recv_sem=recv,
        device_id=(face, tile), device_id_type=MESH,
    )


def nt(left, right):
    return lax.dot_general(left, right, (((1,), (1,)), ((), ())), preferred_element_type=F32)


def nn(left, right):
    return lax.dot_general(left, right, (((1,), (0,)), ((), ())), preferred_element_type=F32)


def one_hot(rows, cols, index):
    r = lax.broadcasted_iota(jnp.int32, (rows, cols), 0)
    c = lax.broadcasted_iota(jnp.int32, (rows, cols), 1)
    return jnp.where(c == index(r), 1.0, 0.0).astype(BF)


def fold(v):
    rows, chans = v.shape
    return jnp.sum(v.reshape(rows // 8, 8, chans), 0)


def main_kernel(
    factor,
    nbr_hbm, x_hbm, cot_hbm, kern_hbm, cb_hbm, gain_hbm, nb_hbm, we_hbm, be_hbm, wr_hbm, br_hbm, ls_hbm,
    out_hbm, gath, sgath,
    nbr, x, cot, kern, cb, gain, nb, we, be, wr, br, ls, out,
    top, bot, hbuf, side, piece, pieces, chosen, near_band, far_band, near_out, far_out,
    pad, conv, taps, act, pulled, pulled_wide, acc_e, acc_r, sums, ksum,
    big, slots1, slotsz, fin, small, few_half, fews, fewz, sfin,
    load_sem, out_sem, row_send, row_recv, side_send, side_recv, sem,
):
    f, t = place()
    last = TILES - 1
    mirror = last - t
    is_first = t == 0
    is_last = t == last
    has_up = t > 0
    has_down = t < last
    ward = lax.rem(t + 16, TILES)
    image = last - ward
    ward_up = ward > 0
    ward_down = ward < last
    image_up = jnp.logical_and(image > 0, image - 1 != t)
    image_down = jnp.logical_and(image < last, image + 1 != t)
    origin = [lax.rem(v + TILES, TILES) for v in (t + 15, t + 16, t + 17, 16 - t, 15 - t, 14 - t)]
    own3 = jnp.logical_and(has_up, origin[3] == t)
    own5 = jnp.logical_and(has_down, origin[5] == t)
    true = t >= 0
    valid = [
        has_up, true, has_down, jnp.logical_and(has_up, origin[3] != t), true,
        jnp.logical_and(has_down, origin[5] != t),
    ]
    edge = jnp.logical_or(is_first, is_last)
    hi = t // 16
    s = t % 16
    z = s // 2
    core = s % 2
    a = hi * 8 + f
    me = core * 16 + a
    twin = t + 1 - 2 * core
    yh, across = f // 4, f % 4
    row = yh * 2 + hi

    def plane_at(dy, dx):
        to = lax.rem(row + dy, 4)
        return to % 2 * 8 + to // 2 * 4 + lax.rem(across + dx, 4)

    others = [lax.rem(yh + dy, 2) * 4 + lax.rem(across + dx, 4) for dy, dx in FACE_STEPS]
    plane = [plane_at(dy, dx) for dy, dx in PLANE_STEPS]
    near = [c * 16 + p for p in plane for c in (core, 1 - core)] + [(1 - core) * 16 + a]
    stack = [lax.rem(z + dz, 8) for dz in STACK_STEPS]
    line = [q * 2 + c for q in stack for c in (core, 1 - core)] + [z * 2 + 1 - core]

    def plane_id(p):
        return lax.rem(p, 8), p // 8 * 16 + s

    def near_id(q):
        return lax.rem(q, 8), q % 16 // 8 * 16 + z * 2 + q // 16

    def drain(ref, which):
        pltpu.make_async_copy(ref, ref, sem.at[which]).wait()

    loads = [
        pltpu.make_async_copy(src, dst, load_sem.at[i])
        for i, (src, dst) in enumerate(
            (
                (x_hbm, x), (kern_hbm, kern), (cb_hbm, cb), (cot_hbm, cot), (we_hbm, we), (wr_hbm, wr),
                (nbr_hbm, nbr), (gain_hbm, gain), (nb_hbm, nb), (be_hbm, be), (br_hbm, br), (ls_hbm, ls),
            )
        )
    ]
    for load in loads:
        load.start()

    barrier = pltpu.get_barrier_semaphore()

    def hello(face, tile):
        pl.semaphore_signal(barrier, inc=1, device_id=(face, tile), device_id_type=MESH)

    @pl.when(edge)
    def _():
        for g in range(FACES):
            hello(g, mirror)

    @pl.when(has_up)
    def _():
        hello(f, t - 1)

    @pl.when(has_down)
    def _():
        hello(f, t + 1)

    for tile, cond in zip(origin, valid):

        @pl.when(cond)
        def _(tile=tile):
            hello(f, tile)

    for p in line:
        hello(f, hi * 16 + p)
    for q in near:
        hello(*near_id(q))

    loads[0].wait()
    for d in range(3):
        west = x[:, d : d + 1, :].astype(F32).reshape(8, 128)
        east = x[:, 255 - d : 256 - d, :].astype(F32).reshape(8, 128)
        piece[d] = jnp.concatenate([west, east], 0).astype(BF)
    pad[3:11, 8:264, :] = x[...].astype(F32)
    for load in loads[1:3]:
        load.wait()
    for i in range(7):
        for j in range(7):
            taps[i * 7 + j] = jnp.broadcast_to(kern[i, j : j + 1, :], (8, 128))
    bias = jnp.broadcast_to(cb[...].reshape(1, 128), (8, 128))

    def convolve(col, acc, out_rows, in_rows, base=0):
        acc = dict(zip(out_rows, acc))
        for j in range(7):
            for row in in_rows:
                hit = [r for r in out_rows if 0 <= row - r < 7]
                if hit:
                    v = pad[base + row, pl.ds(col + 5 + j, 8), :]
                    for r in hit:
                        acc[r] = acc[r] + taps[(row - r) * 7 + j] * v
        return [acc[r] for r in out_rows]

    @pl.loop(0, 4)
    def _(i):
        for u in range(7):
            col = pl.multiple_of(16 + i * 56 + u * 8, 8)
            for r, v in enumerate(convolve(col, [bias] * 8, range(8), range(3, 11))):
                conv[r, pl.ds(col, 8), :] = v

    one = lambda cond: cond.astype(jnp.int32)
    targets = one(ward_up) + one(ward_down) + one(image_up) + one(image_down) + 2
    count = 46 + one(has_up) + one(has_down) + targets + 8 * one(edge)
    pl.semaphore_wait(barrier, count)

    def columns(c):
        return pl.ds(pl.multiple_of(c * 16, 16), 16)

    def piece_copy(k, g):
        return remote(piece, pieces.at[f], sem.at[2], sem.at[3], g, ward)

    def up_copy():
        return remote(x.at[pl.ds(0, 3)], bot, row_send.at[0], row_recv.at[0], f, t - 1)

    def down_copy():
        return remote(x.at[pl.ds(5, 3)], top, row_send.at[1], row_recv.at[1], f, t + 1)

    for rows, cond in ((0, is_first), (5, is_last)):

        @pl.when(cond)
        def _(rows=rows):
            three = pl.ds(rows, 3)
            for g in others:
                remote(x.at[three, columns(g), :], near_band.at[f], sem.at[0], sem.at[1], g, t).start()
            for g in others + [f]:
                remote(
                    x.at[three, columns(g + 8), :], far_band.at[f], sem.at[18], sem.at[19], g, mirror
                ).start()
            near_band[f] = x[three, columns(f), :]

    @pl.when(has_up)
    def _():
        up_copy().start()

    @pl.when(has_down)
    def _():
        down_copy().start()

    for k, g in enumerate(others):
        piece_copy(k, g).start()

    for load in loads[3:]:
        load.wait()

    def side_copy(slot, tile):
        return remote(chosen, side.at[slot], side_send.at[slot], side_recv.at[slot], f, tile)

    routes = (
        (0, ward + 1, ward_down), (1, ward, true), (2, ward - 1, ward_up),
        (3, image + 1, image_down), (4, image, true), (5, image - 1, image_up),
    )

    def pass_sides():
        drain(pieces.at[pl.ds(0, 7)], 3)
        from_west = pieces[nbr[0, 3, f]]
        from_east = pieces[nbr[0, 1, f]]
        chosen[...] = jnp.concatenate(
            [from_west.astype(F32)[:, 8:16], from_east.astype(F32)[:, 0:8]], 1
        ).astype(BF)
        for slot, tile, cond in routes:

            @pl.when(cond)
            def _(slot=slot, tile=tile):
                side_copy(slot, tile).start()

        @pl.when(own3)
        def _():
            side[3] = chosen[...]

        @pl.when(own5)
        def _():
            side[5] = chosen[...]

    def pass_bands():
        for near_side, far_side, cond in ((0, 2, is_last), (2, 0, is_first)):

            @pl.when(cond)
            def _(near_side=near_side, far_side=far_side):
                drain(near_band.at[pl.ds(0, 7)], 1)
                for g in others + [f]:
                    near_out[g] = near_band[nbr[0, near_side, g]]
                    remote(near_out.at[g], hbuf.at[f], sem.at[4], sem.at[5], g, mirror).start()
                drain(far_band, 19)
                for k, g in enumerate(others):
                    far_out[k] = far_band[nbr[0, far_side, g]]
                    remote(far_out.at[k], hbuf.at[f + 8], sem.at[4], sem.at[5], g, t).start()
                hbuf[f + 8] = far_band[nbr[0, far_side, f]]

    def polar(flag, rows):
        drain(hbuf.at[pl.ds(0, 15)], 5)
        turn = one_hot(256, 256, lambda r: 255 - r)
        for d in range(3):
            band = jnp.concatenate([hbuf[k, d] for k in range(16)], 0)
            turned = nn(turn, band)
            pad[rows[d], 8:264, :] = jnp.where(flag == 1, turned, band.astype(F32))

    def finish(out_rows, in_rows):
        @pl.loop(0, 4)
        def _(i):
            for u in range(7):
                col = pl.multiple_of(16 + i * 56 + u * 8, 8)
                acc = [conv[r, pl.ds(col, 8), :] for r in out_rows]
                for r, v in zip(out_rows, convolve(col, acc, out_rows, in_rows)):
                    conv[r, pl.ds(col, 8), :] = v

    def finish_top():
        @pl.when(has_up)
        def _():
            down_copy().wait_recv()
            pad[0:3, 8:264, :] = top[...].astype(F32)

        @pl.when(is_first)
        def _():
            polar(nbr[2, 0, f], (0, 1, 2))

        finish(range(0, 3), range(0, 3))

    def finish_bottom():
        @pl.when(has_down)
        def _():
            up_copy().wait_recv()
            pad[11:14, 8:264, :] = bot[...].astype(F32)

        @pl.when(is_last)
        def _():
            polar(nbr[2, 2, f], (11, 12, 13))

        finish(range(5, 8), range(11, 14))

    acc_e[...] = jnp.zeros_like(acc_e)
    acc_r[...] = jnp.zeros_like(acc_r)
    sums[...] = jnp.zeros_like(sums)
    mean_of = jnp.full((128, 128), 1.0 / 128, BF)
    vec = lambda ref: ref[...].reshape(1, -1)

    def pull_back(cotangent):
        branch_cot = (cotangent.astype(F32) * vec(ls)).astype(BF)
        sums[3] += fold(branch_cot.astype(F32))
        return branch_cot, nt(branch_cot, wr[...])

    def mlp(c, pulled, rows, between=None):
        count = c.shape[0]
        centred = c - nn(c.astype(BF), mean_of)
        variance = nn((centred * centred).astype(BF), mean_of)
        inverse = lax.rsqrt(variance + EPS)
        normed = centred * inverse
        scaled = (normed * vec(gain) + vec(nb)).astype(BF)
        hidden = nn(scaled, we[...]) + vec(be)
        branch_cot, active_cot = pulled
        square = hidden * hidden
        gate = 0.5 + 0.5 * jnp.tanh(hidden * (ROOT + (ROOT * CUBE) * square))
        active = hidden * gate
        active_low = active.astype(BF)
        slope = gate + active * (1.0 - gate) * (2.0 * ROOT + (6.0 * ROOT * CUBE) * square)
        hidden_cot = (active_cot * slope).astype(BF)
        act[rows, :] = active_low
        left = jnp.concatenate([scaled.T, jnp.ones((16, count), BF)], 0)
        acc_e[...] += nn(left, hidden_cot)
        acc_r[...] += nn(branch_cot.T, active_low)
        if between is not None:
            between()
        scaled_cot = nt(hidden_cot, we[...])
        normed_cot = scaled_cot * vec(gain)
        m1 = nn(normed_cot.astype(BF), mean_of)
        m2 = nn((normed_cot * normed).astype(BF), mean_of)
        conv_cot = inverse * (normed_cot - m1 - normed * m2)
        sums[0] += fold(conv_cot)
        sums[1] += fold(scaled_cot * normed)
        sums[2] += fold(scaled_cot)
        return conv_cot

    def kernel_grad(base, rows, cols):
        steps = 1 if len(cols) == 4 else 4
        width = len(cols) // steps

        @pl.loop(0, 7)
        def _(j):
            def step(k, acc):
                acc = list(acc)
                for u in range(width):
                    col = cols[u] if steps == 1 else pl.multiple_of(cols[0] + k * width * 8 + u * 8, 8)
                    cots = [conv[base + r, pl.ds(col, 8), :] for r in range(rows)]
                    for row in range(rows + 6):
                        v = pad[base + row, pl.ds(col + 5 + j, 8), :]
                        for i in range(7):
                            if 0 <= row - i < rows:
                                acc[i] = acc[i] + cots[row - i] * v
                return tuple(acc)

            zero = (jnp.zeros((8, 128), F32),) * 7
            acc = step(0, zero) if steps == 1 else lax.fori_loop(0, steps, step, zero)
            for i in range(7):
                ksum[i * 7 + j] += acc[i]

    inner = range(16, 240, 8)
    low_first = t < 16
    base1 = jnp.where(low_first, 5, 0)
    base2 = 5 - base1
    base5 = jnp.where(low_first, 3, 0)
    mid, three1, three2 = pl.ds(3, 2), pl.ds(base1, 3), pl.ds(base2, 3)
    five = pl.ds(base5, 5)

    def inside(ref, rows, count):
        return ref[rows, 16:240, :].reshape(count * 224, 128)

    def outside(ref):
        return jnp.concatenate([ref[five, 0:16, :], ref[five, 240:256, :]], 1).reshape(160, 128)

    def put_outside(ref, value):
        value = value.reshape(5, 32, 128)
        ref[five, 0:16, :] = value[:, 0:16]
        ref[five, 240:256, :] = value[:, 16:32]

    got = mlp(inside(conv, mid, 2), pull_back(inside(cot, mid, 2)), pl.ds(0, 448))
    conv[mid, 16:240, :] = got.reshape(2, 224, 128)
    ksum[...] = jnp.zeros_like(ksum)
    kernel_grad(3, 2, inner)
    later = (inside(cot, three1, 3), outside(cot), cot[three2, :, :].reshape(768, 128))
    pulled[...], pulled_wide[...] = pull_back(jnp.concatenate(later, 0))
    pass_sides()

    @pl.when(low_first)
    def _():
        finish_bottom()

    @pl.when(jnp.logical_not(low_first))
    def _():
        finish_top()

    pass_bands()
    got = mlp(inside(conv, three1, 3), (pulled[0:672, :], pulled_wide[0:672, :]), pl.ds(448, 672))
    conv[three1, 16:240, :] = got.reshape(3, 224, 128)
    kernel_grad(base1, 3, inner)

    for slot, cond in enumerate(valid):

        @pl.when(cond)
        def _(slot=slot):
            side_copy(slot, origin[slot]).wait_recv()

    @pl.when(is_first)
    def _():
        side[0] = jnp.zeros((3, 16, 128), BF)
        side[3] = jnp.zeros((3, 16, 128), BF)

    @pl.when(is_last)
    def _():
        side[2] = jnp.zeros((3, 16, 128), BF)
        side[5] = jnp.zeros((3, 16, 128), BF)

    turn = one_hot(24, 24, lambda r: r // 8 * 8 + 7 - r % 8)
    for d in range(3):
        slots = [side[i, d].astype(F32) for i in range(6)]
        for first, side_id, col in ((0, 3, 7 - d), (8, 1, 264 + d)):
            straight = jnp.concatenate([slots[i][first : first + 8] for i in (0, 1, 2)], 0)
            turned = jnp.concatenate([slots[i][first : first + 8] for i in (3, 4, 5)], 0)
            turned = nn(turn, turned.astype(BF))
            halo = jnp.where(nbr[2, side_id, f] == 1, turned, straight)
            pad[0:14, col : col + 1, :] = halo[5:19].reshape(14, 1, 128)

    ends = (0, 8, 240, 248)

    def convolve_ends(base, rows):
        for col in ends:
            got = convolve(col, [bias] * rows, range(rows), range(rows + 6), base)
            for r, v in enumerate(got):
                conv[base + r, pl.ds(col, 8), :] = v

    convolve_ends(base5, 5)

    @pl.when(edge)
    def _():
        put_outside(conv, mlp(outside(conv), (pulled[672:832, :], pulled_wide[672:832, :]), pl.ds(1120, 160)))

    @pl.when(low_first)
    def _():
        finish_top()

    @pl.when(jnp.logical_not(low_first))
    def _():
        finish_bottom()

    convolve_ends(base2, 3)

    def send_large():
        for q in range(4):
            cols = slice(q * 128, q * 128 + 128)
            big[q * 4 : q * 4 + 4] = acc_e[0:128, cols].astype(BF).reshape(4, 32, 128)
            big[16 + q * 4 : 20 + q * 4] = acc_r[:, cols].T.astype(BF).reshape(4, 32, 128)
        for q in near:
            remote(big.at[q], slots1.at[me], sem.at[6], sem.at[7], *near_id(q)).start()

    def last_rows():
        return conv[three2, :, :].reshape(768, 128)

    @pl.when(edge)
    def _():
        got = mlp(last_rows(), (pulled[832:1600, :], pulled_wide[832:1600, :]), pl.ds(1280, 768), send_large)
        conv[three2, :, :] = got.reshape(3, 256, 128)

    @pl.when(jnp.logical_not(edge))
    def _():
        got = mlp(
            jnp.concatenate([outside(conv), last_rows()], 0),
            (pulled[672:1600, :], pulled_wide[672:1600, :]), pl.ds(1120, 928), send_large,
        )
        put_outside(conv, got[0:160])
        conv[three2, :, :] = got[160:928].reshape(3, 256, 128)

    slots1[me] = big[me]

    scale = jnp.zeros((8, 128), F32)
    for q in range(4):
        cols = slice(q * 128, q * 128 + 128)
        scale = scale + fold(acc_r[:, cols].T * wr[cols, :].astype(F32))
    small[...] = jnp.zeros_like(small)
    totals = [jnp.sum(sums[i], 0, keepdims=True) for i in range(4)]
    totals.append((jnp.sum(scale, 0, keepdims=True) + vec(br) * totals[3]) / vec(ls))
    for i in range(5):
        small[49 + i : 50 + i, :] = totals[i]
    for q in range(4):
        small[54 + q : 55 + q, :] = acc_e[128:129, q * 128 : q * 128 + 128]

    kernel_grad(base2, 3, range(0, 256, 8))
    kernel_grad(base5, 5, ends)

    for i in range(49):
        small[i : i + 1, :] = jnp.sum(ksum[i], 0, keepdims=True)

    def half_of(part):
        return small.at[pl.ds(pl.multiple_of(part * 32, 32), 32)]

    remote(half_of(1 - core), few_half, sem.at[8], sem.at[9], f, twin).start()

    def output(rows, residual):
        branch = nn(act[rows, :], wr[...]) + vec(br)
        return (residual.astype(F32) + vec(ls) * branch).astype(BF)

    def output_inside(rows, three, count):
        out[three, 16:240, :] = output(rows, inside(x, three, count)).reshape(count, 224, 128)

    output_inside(pl.ds(0, 448), mid, 2)

    drain(few_half, 9)
    fews[a] = (half_of(core)[...] + few_half[...]).astype(BF)
    for p in plane:
        remote(fews.at[a], fews.at[a], sem.at[22], sem.at[23], *plane_id(p)).start()

    output_inside(pl.ds(448, 672), three1, 3)

    drain(slots1.at[pl.ds(0, 31)], 7)
    total = slots1[0].astype(F32)
    for q in range(1, 32):
        total = total + slots1[q].astype(F32)
    slotsz[z] = total.astype(BF)
    for q in stack:
        remote(
            slotsz.at[z], slotsz.at[z], sem.at[10], sem.at[11], f, hi * 16 + q * 2 + core
        ).start()

    put_outside(out, output(pl.ds(1120, 160), outside(x)))
    got = output(pl.ds(1280, 768), x[three2, :, :].reshape(768, 128))
    out[three2, :, :] = got.reshape(3, 256, 128)
    store = pltpu.make_async_copy(out, out_hbm, out_sem.at[0])
    store.start()

    drain(fews.at[pl.ds(0, 15)], 23)
    few = fews[0].astype(F32)
    for p in range(1, 16):
        few = few + fews[p].astype(F32)
    fewz[z] = few.astype(BF)
    for q in stack:
        remote(
            fewz.at[z], fewz.at[z], sem.at[12], sem.at[13], f, hi * 16 + q * 2 + core
        ).start()

    drain(slotsz.at[pl.ds(0, 7)], 11)
    total = slotsz[0].astype(F32)
    for q in range(1, 8):
        total = total + slotsz[q].astype(F32)
    fin[...] = (total * factor).astype(BF)
    for q in near:
        remote(fin, gath.at[me], sem.at[14], sem.at[15], *near_id(q)).start()
    own = pltpu.make_async_copy(fin, gath.at[me], out_sem.at[1])
    own.start()

    drain(fewz.at[pl.ds(0, 7)], 13)
    few = fewz[0].astype(F32)
    for q in range(1, 8):
        few = few + fewz[q].astype(F32)
    sfin[...] = few * factor
    mine_small = sgath.at[pl.ds(pl.multiple_of(core * 32, 32), 32)]
    remote(sfin, mine_small, sem.at[16], sem.at[17], f, twin).start()
    own_small = pltpu.make_async_copy(sfin, mine_small, out_sem.at[2])
    own_small.start()
    drain(gath.at[pl.ds(0, 31)], 15)
    drain(sgath.at[pl.ds(0, 32)], 17)

    store.wait()
    own.wait()
    own_small.wait()
    for slot, tile, cond in routes:

        @pl.when(cond)
        def _(slot=slot, tile=tile):
            side_copy(slot, tile).wait_send()

    @pl.when(has_up)
    def _():
        up_copy().wait_send()

    @pl.when(has_down)
    def _():
        down_copy().wait_send()

    @pl.when(edge)
    def _():
        drain(near_band.at[pl.ds(0, 7)], 0)
        drain(far_band, 18)
        drain(hbuf.at[pl.ds(0, 15)], 4)

    drain(pieces.at[pl.ds(0, 7)], 2)
    drain(slots1.at[pl.ds(0, 31)], 6)
    drain(few_half, 8)
    drain(fews.at[pl.ds(0, 15)], 22)
    drain(slotsz.at[pl.ds(0, 7)], 10)
    drain(fewz.at[pl.ds(0, 7)], 12)
    drain(gath.at[pl.ds(0, 31)], 14)
    drain(sfin, 16)


def run_main(factor, neighbours, *operands):
    dma = pltpu.SemaphoreType.DMA
    shape = lambda *dims: jax.ShapeDtypeStruct(dims, BF)
    return pl.pallas_call(
        functools.partial(main_kernel, factor),
        out_shape=(
            shape(8, 256, 128),
            shape(32, 32, 128),
            jax.ShapeDtypeStruct((64, 128), F32),
        ),
        in_specs=[ANY] * 12,
        out_specs=(ANY, ANY, ANY),
        scratch_shapes=[pltpu.SMEM(neighbours.shape, jnp.int32)]
        + [pltpu.VMEM(item.shape, item.dtype) for item in operands]
        + [
            pltpu.VMEM((8, 256, 128), BF),
            pltpu.VMEM((3, 256, 128), BF),
            pltpu.VMEM((3, 256, 128), BF),
            pltpu.VMEM((16, 3, 16, 128), BF),
            pltpu.VMEM((6, 3, 16, 128), BF),
            pltpu.VMEM((3, 16, 128), BF),
            pltpu.VMEM((8, 3, 16, 128), BF),
            pltpu.VMEM((3, 16, 128), BF),
            pltpu.VMEM((8, 3, 16, 128), BF),
            pltpu.VMEM((8, 3, 16, 128), BF),
            pltpu.VMEM((8, 3, 16, 128), BF),
            pltpu.VMEM((7, 3, 16, 128), BF),
            pltpu.VMEM((14, 272, 128), F32),
            pltpu.VMEM((8, 256, 128), F32),
            pltpu.VMEM((49, 8, 128), F32),
            pltpu.VMEM((2048, 512), BF),
            pltpu.VMEM((1600, 128), BF),
            pltpu.VMEM((1600, 512), F32),
            pltpu.VMEM((144, 512), F32),
            pltpu.VMEM((128, 512), F32),
            pltpu.VMEM((4, 8, 128), F32),
            pltpu.VMEM((49, 8, 128), F32),
            pltpu.VMEM((32, 32, 128), BF),
            pltpu.VMEM((32, 32, 128), BF),
            pltpu.VMEM((8, 32, 128), BF),
            pltpu.VMEM((32, 128), BF),
            pltpu.VMEM((64, 128), F32),
            pltpu.VMEM((32, 128), F32),
            pltpu.VMEM((16, 32, 128), BF),
            pltpu.VMEM((8, 32, 128), BF),
            pltpu.VMEM((32, 128), F32),
            dma((12,)), dma((3,)), dma((2,)), dma((2,)), dma((6,)), dma((6,)), dma((24,)),
        ],
        compiler_params=pltpu.CompilerParams(
            collective_id=0, has_side_effects=True, vmem_limit_bytes=56 * 1024 * 1024
        ),
        name="main",
    )(neighbours, *operands)


def unpack_kernel(raw, gath, sgath, *refs):
    outs, stages, (rows_in, few_in, sem) = refs[:10], refs[10:20], refs[20:]
    stage, kernel_grad, cb_grad, gain_grad, nb_grad, we_grad, be_grad, wr_grad, br_grad, ls_grad = stages
    fetches = [
        pltpu.make_async_copy(src, dst, sem.at[i])
        for i, (src, dst) in enumerate(((gath, rows_in), (sgath, few_in)))
    ]
    parts = [pl.ds(i * 4, 4) for i in range(2)]
    loads = [
        pltpu.make_async_copy(raw.at[part], stage.at[part], sem.at[2 + i])
        for i, part in enumerate(parts)
    ]
    stores = [
        pltpu.make_async_copy(stage.at[part], outs[0].at[part], sem.at[4 + i])
        for i, part in enumerate(parts)
    ]
    stores += [
        pltpu.make_async_copy(src, dst, sem.at[6 + i])
        for i, (src, dst) in enumerate(zip(stages[1:], outs[1:]))
    ]
    for fetch in fetches + loads:
        fetch.start()
    rows = rows_in.reshape(1024, 128)
    few = few_in
    fetches[1].wait()
    for q in range(4):
        be_grad[q * 128 : q * 128 + 128] = few[54 + q]
    for i in range(7):
        kernel_grad[i] = few[i * 7 : i * 7 + 7]
    for i, ref in enumerate((cb_grad, gain_grad, nb_grad, br_grad, ls_grad)):
        ref[...] = few[49 + i]
    for i in (2, 3, 4, 5, 7, 9, 10):
        stores[i].start()
    fetches[0].wait()
    for q in range(4):
        we_grad[:, q * 128 : q * 128 + 128] = rows[q * 128 : q * 128 + 128, :].astype(F32)
    stores[6].start()
    wr_grad[...] = rows[512:1024, :].astype(F32)
    stores[8].start()
    for i in range(2):
        loads[i].wait()
        stores[i].start()
    for store in stores:
        store.wait()


def unpack(raw, gath, sgath):
    one = lambda *shape: jax.ShapeDtypeStruct(shape, F32)
    shapes = (
        jax.ShapeDtypeStruct(raw.shape, raw.dtype),
        one(7, 7, 128), one(128), one(128), one(128), one(128, 512), one(512),
        one(512, 128), one(128), one(128),
    )
    return pl.pallas_call(
        unpack_kernel,
        out_shape=shapes,
        in_specs=[ANY, ANY, ANY],
        out_specs=(ANY,) * 10,
        scratch_shapes=[pltpu.VMEM(item.shape, item.dtype) for item in shapes + (gath, sgath)]
        + [pltpu.SemaphoreType.DMA((15,))],
        compiler_params=pltpu.CompilerParams(vmem_limit_bytes=56 * 1024 * 1024),
        name="unpack",
    )(raw, gath, sgath)


def body(
    inputs, kernel, conv_bias, norm_gain, norm_bias, expand_weight, expand_bias,
    reduce_weight, reduce_bias, layer_scale, neighbours, cotangent,
):
    factor = 1.0 / math.sqrt(FACES * 256 * 256)
    raw, gath, sgath = run_main(
        factor, jnp.transpose(neighbours, (2, 1, 0)), inputs[0], cotangent[0], kernel, conv_bias, norm_gain, norm_bias,
        expand_weight, expand_bias, reduce_weight, reduce_bias, layer_scale,
    )
    out, *grads = unpack(raw, gath, sgath)
    return (out[None], *grads)


def solution(mesh):
    split = P("face", "tile", None, None)
    return jax.shard_map(
        body,
        mesh=mesh,
        in_specs=(split,) + (P(),) * 10 + (split,),
        out_specs=(split,) + (P(),) * 9,
        check_vma=False,
    )
```
